32 devices in a mesh: species: 4 (over y, core), tile: 8 (over z, x).
Axes of the slice: x: 2, y: 2, z: 4, core: 2. Of those that a mesh axis runs over, the one named last changes fastest.
Arguments:
- tracers: float32 [64, 16, 64, 128], P('species', None, 'tile'), may hold values from 0.1 to 4
- fluxes: float32 [4, 3, 16, 64, 128], P(None, None, 'species', 'tile'), may hold values from -0.15 to 0.15
- weight_in: bfloat16 [512, 64], replicated, may hold values from -0.75 to 0.75
- weight_out: bfloat16 [64, 512], replicated, may hold values from -0.25 to 0.25
Outputs:
- tracers_out: float32 [64, 16, 64, 128], P('species', None, 'tile')
The draws below stay inside these ranges and needn't reach their ends.
All inputs are finite; a program needn't handle non-finite values.
Results may differ from the reference program's by a relative error of at most 0.0035.
Values may be sent and summed in bfloat16 or wider, within the bound.
No kernel may reach another device: no remote copies, remote signals or barrier semaphores. Data moves between devices by JAX's collectives and lax.ppermute only.
A program may use at most 64 MiB of HBM per device.

```python
import math
from functools import partial
import jax
import jax.numpy as jnp
from jax import lax

SPECIES = 64
HID = 512
NZ = 16
NY = 128
STEPS = 4
NX = 64


def level_of(own_key, dims, split, least, largest):
    factor_of, own = 1.0, jax.random.fold_in(own_key, 6)
    for dim, parts in split:
        steps = jnp.exp(jax.random.uniform(jax.random.fold_in(own, dim), (parts,), jnp.float32, least / len(split), largest / len(split)))
        factor_of = factor_of * jnp.repeat(steps, dims[dim] // parts).reshape([-1 if axis == dim else 1 for axis in range(len(dims))])
    return factor_of


def bell_draw(stream_key, dims, deviation, limit, dtype=jnp.bfloat16):
    result = jax.random.normal(stream_key, dims, jnp.float32) * deviation
    return jnp.minimum(jnp.maximum(result, -limit), limit).astype(dtype)


def setup_inputs(seed: int = 0) -> dict:
    seeds = jax.random.split(jax.random.key(seed), 5)
    tracers = jnp.clip(jnp.exp(math.log(4.0) - 3.6888794 * jax.random.uniform(seeds[0], (SPECIES, NZ, NX, NY), jnp.float32) ** level_of(seeds[0], (SPECIES, NZ, NX, NY), ((0, 4), (2, 8)), -0.2, 0.2)), 0.1, 4.0)
    fluxes = jnp.clip(jax.random.uniform(seeds[1], (STEPS, 3, NZ, NX, NY), jnp.float32, -0.15, 0.15) * level_of(seeds[1], (STEPS, 3, NZ, NX, NY), ((2, 4), (3, 8)), -0.4, 0.0), -0.15, 0.15)
    weight_in = bell_draw(seeds[2], (HID, SPECIES), SPECIES ** -0.5, 0.75)
    weight_out = bell_draw(seeds[3], (SPECIES, HID), HID ** -0.5, 0.25)
    return dict(tracers=tracers, fluxes=fluxes, weight_in=weight_in, weight_out=weight_out)


def positive(value):
    return jnp.maximum(value, 0.0)


def negative(value):
    return jnp.minimum(value, 0.0)


def advance(padded_state, padded_x, flux_y, padded_z):
    inner = padded_state[:, 1:-1, 1:-1]
    along_x = padded_state[:, 1:-1]
    face_x = padded_x[:, 1:]
    faces_x = positive(face_x) * along_x[:, :, :-1] + negative(face_x) * along_x[:, :, 1:]
    along_z = padded_state[:, :, 1:-1]
    face_z = padded_z[1:]
    faces_z = positive(face_z) * along_z[:, :-1] + negative(face_z) * along_z[:, 1:]
    faces_y = positive(flux_y) * jnp.roll(inner, 1, 3) + negative(flux_y) * inner
    return inner + faces_x[:, :, :-1] - faces_x[:, :, 1:] + faces_y - jnp.roll(faces_y, -1, 3) + faces_z[:, :-1] - faces_z[:, 1:]


def reaction(weight_in, weight_out, level):
    flattened = level.reshape(level.shape[0], -1).astype(jnp.bfloat16)
    hidden = jax.nn.silu(jnp.dot(weight_in, flattened, preferred_element_type=jnp.float32)).astype(jnp.bfloat16)
    tendency = (0.5 * jnp.dot(weight_out, hidden, preferred_element_type=jnp.float32)).astype(jnp.bfloat16)
    return tendency.reshape(level.shape)


def reference(tracers, fluxes, weight_in, weight_out):
    shape_grid = fluxes.shape[2:]
    column = lax.broadcasted_iota(jnp.int32, shape_grid, 1)
    level_at = lax.broadcasted_iota(jnp.int32, shape_grid, 0)
    state = tracers
    for interval in range(STEPS):
        flux_x = jnp.where(column == 0, 0.0, fluxes[interval, 0])
        flux_y = fluxes[interval, 1]
        flux_z = jnp.where(level_at == 0, 0.0, fluxes[interval, 2])
        padded_x = jnp.pad(flux_x, ((0, 0), (1, 1), (0, 0)))
        padded_z = jnp.pad(flux_z, ((1, 1), (0, 0), (0, 0)))

        def single(species_row):
            padded_state = jnp.pad(species_row[None], ((0, 0), (1, 1), (1, 1), (0, 0)))
            return advance(padded_state, padded_x, flux_y, padded_z)[0]

        state = lax.map(single, state)
        tendency = lax.map(partial(reaction, weight_in, weight_out), jnp.moveaxis(state, 1, 0))
        state = state + jnp.moveaxis(tendency, 0, 1).astype(jnp.float32)
    return state
```

```python
import functools

import jax
import jax.numpy as jnp
from jax import lax
from jax.experimental import pallas as pl
from jax.experimental.pallas import tpu as pltpu
from jax.sharding import PartitionSpec as P

STEPS = 4
AXES = ("species", "tile")
PACK = 16
VMEM = pl.BlockSpec(memory_space=pltpu.VMEM)
SMEM = pl.BlockSpec(memory_space=pltpu.SMEM)
LIMIT = 24 * 1024 * 1024


def positive(value):
    return jnp.maximum(value, 0.0)


def negative(value):
    return jnp.minimum(value, 0.0)


def extended(cells, sides, width):
    for axis, dim in sides:
        count = lax.axis_size(axis)
        ends = count - 1
        head = lax.slice_in_dim(cells, 0, width, axis=dim)
        tail = lax.slice_in_dim(cells, cells.shape[dim] - width, cells.shape[dim], axis=dim)
        cells = jnp.concatenate(
            [
                lax.ppermute(tail, axis, [(i, (i + 1) % count) for i in range(ends)]),
                cells,
                lax.ppermute(head, axis, [((i + 1) % count, i) for i in range(ends)]),
            ],
            axis=dim,
        )
    return cells


def advance(padded_state, padded_x, flux_y, padded_z):
    inner = padded_state[:, 1:-1, 1:-1]
    along_x = padded_state[:, 1:-1]
    face_x = padded_x[:, 1:]
    faces_x = positive(face_x) * along_x[:, :, :-1] + negative(face_x) * along_x[:, :, 1:]
    along_z = padded_state[:, :, 1:-1]
    face_z = padded_z[1:]
    faces_z = positive(face_z) * along_z[:, :-1] + negative(face_z) * along_z[:, 1:]
    faces_y = positive(flux_y) * jnp.roll(inner, 1, 3) + negative(flux_y) * inner
    return (
        inner
        + faces_x[:, :, :-1]
        - faces_x[:, :, 1:]
        + faces_y
        - jnp.roll(faces_y, -1, 3)
        + faces_z[:, :-1]
        - faces_z[:, 1:]
    )


def by_levels(tracers, fluxes, weight_in, weight_out):
    spec_loc, depth_all, width_x, width_y = tracers.shape
    tile_at = lax.axis_index("tile")
    state = lax.all_to_all(tracers, "species", split_axis=1, concat_axis=0, tiled=True)
    spec_all, lev_loc = (state.shape[0], state.shape[1])
    grid_shape = (lev_loc, width_x, width_y)
    column = tile_at * width_x + lax.broadcasted_iota(jnp.int32, grid_shape, 1)
    level_at = lax.axis_index("species") * lev_loc + lax.broadcasted_iota(jnp.int32, grid_shape, 0)
    for interval in range(STEPS):
        own_flux = fluxes[interval]
        flux_x = jnp.where(column == 0, 0.0, own_flux[0])
        flux_y = own_flux[1]
        flux_z = jnp.where(level_at == 0, 0.0, own_flux[2])
        stacked = jnp.concatenate([state, flux_x[None], flux_z[None]], 0)
        padded = extended(stacked, (("species", 1), ("tile", 2)), 1)
        padded_state = padded[:spec_all]
        padded_x = padded[spec_all, 1:-1]
        padded_z = padded[spec_all + 1, :, 1:-1]
        state = advance(padded_state, padded_x, flux_y, padded_z)
        flattened = state.astype(jnp.bfloat16).reshape(spec_all, lev_loc, width_x * width_y)
        hidden = jax.nn.silu(
            jnp.einsum("hs,szc->hzc", weight_in, flattened, preferred_element_type=jnp.float32)
        ).astype(jnp.bfloat16)
        tendency = (
            0.5 * jnp.einsum("sh,hzc->szc", weight_out, hidden, preferred_element_type=jnp.float32)
        ).astype(jnp.bfloat16)
        state = state + tendency.reshape(state.shape).astype(jnp.float32)
    return lax.all_to_all(state, "species", split_axis=0, concat_axis=1, tiled=True)


def pack_kernel(count, depth, width, tile_ref, tracers_ref, fluxes_ref, out_ref):
    tile = tile_ref[0]
    odd = lax.rem(tile, 2)
    spec = tracers_ref.shape[0] // (depth * width)
    rows = fluxes_ref.shape[0] // width
    lev = depth // count
    parts = rows // PACK
    at = lax.broadcasted_iota(jnp.int32, (rows, 1), 0)
    is_x = lax.rem(lax.div(at, lev), 3) == 0
    for place in range(count):
        target = jnp.where(odd == 1, count - 1 - place, place)
        for side in range(2):
            x = 2 * place + side
            base = side * (depth + 2 * parts)
            for k in range(depth):
                cells = tracers_ref[pl.ds(k * width + x, spec, stride=depth * width), :]
                out_ref[target, base + k] = cells.astype(jnp.bfloat16)
            flux = fluxes_ref[pl.ds(x, rows, stride=width), :]
            if x == 0:
                flux = jnp.where(jnp.logical_and(is_x, tile == 0), 0.0, flux)
            flux = flux.astype(jnp.bfloat16)
            for part in range(parts):
                out_ref[target, depth + side * parts + part] = flux[part * PACK : (part + 1) * PACK]


def flux_rows(ref, first, parts, count, lev):
    blocks = []
    for source in range(count):
        tiles = [ref[source, first + part].astype(jnp.float32) for part in range(parts)]
        blocks.append(jnp.concatenate(tiles, 0))
    return [
        [
            jnp.concatenate(
                [b[(t * 3 + d) * lev : (t * 3 + d + 1) * lev] for b in blocks], 0
            )
            for d in range(3)
        ]
        for t in range(STEPS)
    ]


def unpack_kernel(depth, parts, got_ref, left_ref, right_ref, flux_left_ref, flux_right_ref):
    count = got_ref.shape[0]
    lev = depth // count
    spec = got_ref.shape[2]
    for side, (state_ref, flux_ref) in enumerate(
        ((left_ref, flux_left_ref), (right_ref, flux_right_ref))
    ):
        base = side * (depth + 2 * parts)
        for source in range(count):
            for k in range(depth):
                state_ref[k, source * spec : (source + 1) * spec] = got_ref[
                    source, base + k
                ].astype(jnp.float32)
        flux = flux_rows(got_ref, depth + side * parts, parts, count, lev)
        for t in range(STEPS):
            for d in range(3):
                flux_ref[t, d] = flux[t][d]


def step_kernel(
    t, is_left, first, parts, own_ref, side_ref, halo_ref, flux_ref, upper_ref, w_in_ref, w_out_ref, *rest
):
    depth, spec_all, width_y = own_ref.shape
    count, spec = halo_ref.shape[0], halo_ref.shape[2]
    lev = depth // count
    rest = list(rest)
    coef = rest.pop()
    send_ref = rest.pop(0)
    new_ref = rest.pop(0) if t < STEPS - 1 else None
    if first and not is_left:
        edge_ref = rest.pop(0)
        edge = flux_rows(halo_ref, depth, parts, count, lev)
        for i in range(STEPS):
            edge_ref[i] = edge[i][0]
        fx_hi = edge[t][0]
    elif is_left:
        fx_hi = upper_ref[t, 0]
    else:
        fx_hi = upper_ref[t]
    fx = flux_ref[t, 0]
    fy = flux_ref[t, 1]
    fy_hi = pltpu.roll(fy, width_y - 1, 1)
    fz = flux_ref[t, 2]
    fz = jnp.where(lax.broadcasted_iota(jnp.int32, fz.shape, 0) == 0, 0.0, fz)
    fz_hi = jnp.concatenate([fz[1:], jnp.zeros_like(fz[:1])], 0)
    coef[0] = (
        1.0
        + (negative(fx) - positive(fx_hi))
        + (negative(fy) - positive(fy_hi))
        + (negative(fz) - positive(fz_hi))
    )
    coef[1] = positive(fx) if is_left else -negative(fx_hi)
    coef[2] = -negative(fx_hi) if is_left else positive(fx)
    coef[3] = positive(fy)
    coef[4] = -negative(fy_hi)
    coef[5] = positive(fz)
    coef[6] = -negative(fz_hi)
    w_in = w_in_ref[...]
    w_out = w_out_ref[...]
    group = 2
    for k0 in range(0, depth, group):
        moved = []
        for k in range(k0, k0 + group):
            own = own_ref[k]
            halo = jnp.concatenate([halo_ref[s, k].astype(jnp.float32) for s in range(count)], 0)
            out = coef[0, pl.ds(k, 1)] * own
            out += coef[1, pl.ds(k, 1)] * halo
            out += coef[2, pl.ds(k, 1)] * side_ref[k]
            out += coef[3, pl.ds(k, 1)] * pltpu.roll(own, 1, 1)
            out += coef[4, pl.ds(k, 1)] * pltpu.roll(own, width_y - 1, 1)
            if k > 0:
                out += coef[5, pl.ds(k, 1)] * own_ref[k - 1]
            if k < depth - 1:
                out += coef[6, pl.ds(k, 1)] * own_ref[k + 1]
            moved.append(out)
        cells = jnp.concatenate([m.astype(jnp.bfloat16) for m in moved], 1)
        half = jnp.dot(w_in, cells, preferred_element_type=jnp.float32)
        hidden = (half + half * jnp.tanh(half)).astype(jnp.bfloat16)
        change = jnp.dot(w_out, hidden, preferred_element_type=jnp.float32)
        for i in range(group):
            new = moved[i] + change[:, i * width_y : (i + 1) * width_y]
            if new_ref is not None:
                new_ref[k0 + i] = new
            for s in range(count):
                send_ref[s, k0 + i] = new[s * spec : (s + 1) * spec].astype(jnp.bfloat16)


def finish_kernel(depth, width, tile_ref, got_ref, out_ref):
    odd = lax.rem(tile_ref[0], 2)
    count, spec = got_ref.shape[0], got_ref.shape[3]
    for place in range(count):
        source = jnp.where(odd == 1, count - 1 - place, place)
        for side in range(2):
            for k in range(depth):
                out_ref[pl.ds(k * width + 2 * place + side, spec, stride=depth * width), :] = got_ref[
                    source, side, k
                ].astype(jnp.float32)


def call(kernel, out_shape, in_specs, args, scratch=(), flops=0, trans=0):
    many = isinstance(out_shape, (list, tuple))
    moved = sum(a.size * a.dtype.itemsize for a in args)
    moved += sum(o.size * o.dtype.itemsize for o in (out_shape if many else [out_shape]))
    return pl.pallas_call(
        kernel,
        out_shape=out_shape,
        in_specs=in_specs,
        out_specs=[VMEM] * len(out_shape) if many else VMEM,
        scratch_shapes=scratch,
        compiler_params=pltpu.CompilerParams(vmem_limit_bytes=LIMIT),
        cost_estimate=pl.CostEstimate(flops=flops, bytes_accessed=moved, transcendentals=trans),
    )(*args)


def by_columns(tracers, fluxes, weight_in, weight_out):
    spec, depth, width, width_y = tracers.shape
    count, tiles = lax.axis_size("species"), lax.axis_size("tile")
    spec_all, hid, lev = spec * count, weight_in.shape[0], depth // count
    parts = STEPS * 3 * lev // PACK
    f32, bf16 = jnp.float32, jnp.bfloat16
    shape = jax.ShapeDtypeStruct

    chain = []
    for t in range(tiles):
        for place in range(count):
            s = place if t % 2 == 0 else count - 1 - place
            chain.append(s * tiles + t)
    to_left = [(chain[i + 1], chain[i]) for i in range(len(chain) - 1)]
    to_right = [(chain[i], chain[i + 1]) for i in range(len(chain) - 1)]

    tile = lax.axis_index("tile").astype(jnp.int32).reshape(1)
    w_in = weight_in * jnp.asarray(0.5, bf16)
    w_out = weight_out * jnp.asarray(0.5, bf16)

    pieces = 2 * depth + 2 * parts
    packed = call(
        functools.partial(pack_kernel, count, depth, width),
        shape((count, pieces, spec, width_y), bf16),
        [SMEM, VMEM, VMEM],
        (tile, tracers.reshape(-1, width_y), fluxes.reshape(-1, width_y)),
    )
    got = lax.all_to_all(packed, "species", split_axis=0, concat_axis=0, tiled=True)
    from_right = lax.ppermute(got[:, : depth + parts], AXES, to_left)
    from_left = lax.ppermute(got[:, depth + 2 * parts :], AXES, to_right)
    row = shape((depth, spec_all, width_y), f32)
    flux = shape((STEPS, 3, depth, width_y), f32)
    left, right, flux_left, flux_right = call(
        functools.partial(unpack_kernel, depth, parts), [row, row, flux, flux], [VMEM], (got,)
    )
    sent = shape((count, depth, spec, width_y), bf16)
    edge = flux_right
    flops = 4 * depth * width_y * spec_all * hid
    trans = depth * width_y * hid

    def step(t, is_left, own, side, halo):
        nonlocal edge
        first = t == 0
        outs = [sent] + ([row] if t < STEPS - 1 else [])
        if first and not is_left:
            outs.append(shape((STEPS, depth, width_y), f32))
        args = (
            own,
            side,
            halo,
            flux_left if is_left else flux_right,
            flux_right if is_left else edge,
            w_in,
            w_out,
        )
        outs = call(
            functools.partial(step_kernel, t, is_left, first, parts),
            outs,
            [VMEM] * len(args),
            args,
            scratch=[pltpu.VMEM((7, depth, width_y), f32)],
            flops=flops,
            trans=trans,
        )
        if first and not is_left:
            edge = outs[-1]
        return outs[0], (outs[1] if t < STEPS - 1 else None)

    for t in range(STEPS):
        last = t == STEPS - 1
        old_left, old_right = left, right
        if t % 2 == 0:
            send_right, right = step(t, False, old_right, old_left, from_right)
            left_in = from_left
            if not last:
                from_left = lax.ppermute(send_right, AXES, to_right)
            send_left, left = step(t, True, old_left, old_right, left_in)
            if not last:
                from_right = lax.ppermute(send_left, AXES, to_left)
        else:
            send_left, left = step(t, True, old_left, old_right, from_left)
            right_in = from_right
            if not last:
                from_right = lax.ppermute(send_left, AXES, to_left)
            send_right, right = step(t, False, old_right, old_left, right_in)
            if not last:
                from_left = lax.ppermute(send_right, AXES, to_right)
    done = lax.all_to_all(
        jnp.stack([send_left, send_right], 1), "species", split_axis=0, concat_axis=0, tiled=True
    )
    out = call(
        functools.partial(finish_kernel, depth, width),
        shape((spec * depth * width, width_y), f32),
        [SMEM, VMEM],
        (tile, done),
    )
    return out.reshape(tracers.shape)


def per_device(tracers, fluxes, weight_in, weight_out):
    spec, depth, width, width_y = tracers.shape
    count = lax.axis_size("species")
    fits = (
        width == 2 * count
        and depth % (2 * count) == 0
        and spec == PACK
        and width_y % 128 == 0
        and width % 8 == 0
        and (STEPS * 3 * depth // count) % PACK == 0
    )
    chosen = by_columns if fits else by_levels
    return chosen(tracers, fluxes, weight_in, weight_out)


def solution(mesh):
    placed = (P("species", None, "tile", None), P(None, None, "species", "tile", None), P(), P())
    return jax.shard_map(
        per_device,
        mesh=mesh,
        in_specs=placed,
        out_specs=P("species", None, "tile", None),
        check_vma=False,
    )
```

```python
import functools

import jax
import jax.numpy as jnp
from jax import lax
from jax.experimental import pallas as pl
from jax.experimental.pallas import tpu as pltpu
from jax.sharding import PartitionSpec as P

STEPS = 4
AXES = ("species", "tile")
PACK = 16
GROUP = 4
VMEM = pl.BlockSpec(memory_space=pltpu.VMEM)
SMEM = pl.BlockSpec(memory_space=pltpu.SMEM)
LIMIT = 24 * 1024 * 1024


def positive(value):
    return jnp.maximum(value, 0.0)


def negative(value):
    return jnp.minimum(value, 0.0)


def extended(cells, sides, width):
    for axis, dim in sides:
        count = lax.axis_size(axis)
        ends = count - 1
        head = lax.slice_in_dim(cells, 0, width, axis=dim)
        tail = lax.slice_in_dim(cells, cells.shape[dim] - width, cells.shape[dim], axis=dim)
        cells = jnp.concatenate(
            [
                lax.ppermute(tail, axis, [(i, (i + 1) % count) for i in range(ends)]),
                cells,
                lax.ppermute(head, axis, [((i + 1) % count, i) for i in range(ends)]),
            ],
            axis=dim,
        )
    return cells


def advance(padded_state, padded_x, flux_y, padded_z):
    inner = padded_state[:, 1:-1, 1:-1]
    along_x = padded_state[:, 1:-1]
    face_x = padded_x[:, 1:]
    faces_x = positive(face_x) * along_x[:, :, :-1] + negative(face_x) * along_x[:, :, 1:]
    along_z = padded_state[:, :, 1:-1]
    face_z = padded_z[1:]
    faces_z = positive(face_z) * along_z[:, :-1] + negative(face_z) * along_z[:, 1:]
    faces_y = positive(flux_y) * jnp.roll(inner, 1, 3) + negative(flux_y) * inner
    return (
        inner
        + faces_x[:, :, :-1]
        - faces_x[:, :, 1:]
        + faces_y
        - jnp.roll(faces_y, -1, 3)
        + faces_z[:, :-1]
        - faces_z[:, 1:]
    )


def by_levels(tracers, fluxes, weight_in, weight_out):
    spec_loc, depth_all, width_x, width_y = tracers.shape
    tile_at = lax.axis_index("tile")
    state = lax.all_to_all(tracers, "species", split_axis=1, concat_axis=0, tiled=True)
    spec_all, lev_loc = (state.shape[0], state.shape[1])
    grid_shape = (lev_loc, width_x, width_y)
    column = tile_at * width_x + lax.broadcasted_iota(jnp.int32, grid_shape, 1)
    level_at = lax.axis_index("species") * lev_loc + lax.broadcasted_iota(jnp.int32, grid_shape, 0)
    for interval in range(STEPS):
        own_flux = fluxes[interval]
        flux_x = jnp.where(column == 0, 0.0, own_flux[0])
        flux_y = own_flux[1]
        flux_z = jnp.where(level_at == 0, 0.0, own_flux[2])
        stacked = jnp.concatenate([state, flux_x[None], flux_z[None]], 0)
        padded = extended(stacked, (("species", 1), ("tile", 2)), 1)
        padded_state = padded[:spec_all]
        padded_x = padded[spec_all, 1:-1]
        padded_z = padded[spec_all + 1, :, 1:-1]
        state = advance(padded_state, padded_x, flux_y, padded_z)
        flattened = state.astype(jnp.bfloat16).reshape(spec_all, lev_loc, width_x * width_y)
        hidden = jax.nn.silu(
            jnp.einsum("hs,szc->hzc", weight_in, flattened, preferred_element_type=jnp.float32)
        ).astype(jnp.bfloat16)
        tendency = (
            0.5 * jnp.einsum("sh,hzc->szc", weight_out, hidden, preferred_element_type=jnp.float32)
        ).astype(jnp.bfloat16)
        state = state + tendency.reshape(state.shape).astype(jnp.float32)
    return lax.all_to_all(state, "species", split_axis=0, concat_axis=1, tiled=True)


def place_of(species, tile, count):
    return jnp.where(lax.rem(tile, 2) == 1, count - 1 - species, species)


def pack_kernel(count, depth, width, at_ref, tracers_ref, fluxes_ref, *out_refs):
    tile, species = at_ref[0], at_ref[1]
    spec = tracers_ref.shape[0] // (depth * width)
    lev = depth // count
    for d, out_ref in enumerate(out_refs):
        place = place_of(species ^ d, tile, count)
        low = 2 * place
        b_at = low + lax.rem(place, 2)
        a_at = low + 1 - lax.rem(place, 2)
        for base, x in ((0, b_at), (depth + 1, a_at)):
            for k in range(depth):
                cells = tracers_ref[pl.ds(k * width + x, spec, stride=depth * width), :]
                out_ref[base + k] = cells.astype(jnp.bfloat16)

        def tile_of(direction, x):
            return jnp.concatenate(
                [
                    fluxes_ref[pl.ds((t * 3 + direction) * lev * width + x, lev, stride=width), :]
                    for t in range(STEPS)
                ],
                0,
            )

        outer = jnp.logical_and(tile == 0, place == 0)
        tiles = [jnp.where(outer, 0.0, tile_of(0, low)), tile_of(0, low + 1)]
        tiles += [tile_of(1, b_at), tile_of(1, a_at), tile_of(2, b_at), tile_of(2, a_at)]
        out_ref[depth] = tiles[0].astype(jnp.bfloat16)
        for i, part in enumerate(tiles[1:]):
            out_ref[2 * depth + 1 + i] = part.astype(jnp.bfloat16)


def unpack_kernel(depth, at_ref, *refs):
    count = len(refs) - 5
    got, (b_ref, a_ref, msg_b_ref, msg_a_ref, flux_ref) = refs[:count], refs[count:]
    lev = depth // count
    spec = got[0].shape[1]
    for d in range(count):
        source = at_ref[1] ^ d
        rows = pl.ds(pl.multiple_of(source * spec, spec), spec)
        for base, state_ref, msg_ref in ((0, b_ref, msg_b_ref), (depth + 1, a_ref, msg_a_ref)):
            first = 0 if base == 0 else 1
            for k in range(depth):
                cells = got[d][base + k]
                state_ref[k, rows] = cells.astype(jnp.float32)
                msg_ref[source, k] = cells
            msg_ref[source, depth] = got[d][depth]
        for i in range(6):
            part = got[d][depth if i == 0 else 2 * depth + i].astype(jnp.float32)
            for t in range(STEPS):
                flux_ref[t, i, source] = part[t * lev : (t + 1) * lev]


def step_kernel(t, is_a, group, at_ref, own_ref, other_ref, halo_ref, flux_ref, edge_ref, w_in_ref, w_out_ref, *rest):
    rest = list(rest)
    first, last = t == 0, t == STEPS - 1
    depth, spec_all, width_y = own_ref.shape
    count, spec = halo_ref.shape[0], halo_ref.shape[2]
    lev = depth // count
    coef, cells_ref = rest[-2:]
    if last and is_a:
        send_ref = rest[0]
    elif last:
        sent_a_ref, outs, send_ref = rest[0], rest[1 : 1 + count], rest[1 + count]
    else:
        send_ref, new_ref = rest[:2]

    def whole(index):
        return jnp.concatenate([flux_ref[t, index, s] for s in range(count)], 0)

    if first:
        parts = [halo_ref[s, depth].astype(jnp.float32) for s in range(count)]
        for i in range(STEPS):
            rest[2][i] = jnp.concatenate([p[i * lev : (i + 1) * lev] for p in parts], 0)
        beyond = rest[2][t]
    else:
        beyond = edge_ref[t]
    is_first = lax.rem(at_ref[2], 2) == (1 if is_a else 0)
    fx_first, fx_second = whole(0), whole(1)
    fx = jnp.where(is_first, fx_first, fx_second)
    fx_hi = jnp.where(is_first, fx_second, beyond)
    fy = whole(3 if is_a else 2)
    fy_hi = pltpu.roll(fy, width_y - 1, 1)
    fz = whole(5 if is_a else 4)
    fz = jnp.where(lax.broadcasted_iota(jnp.int32, fz.shape, 0) == 0, 0.0, fz)
    fz_hi = jnp.concatenate([fz[1:], jnp.zeros_like(fz[:1])], 0)
    low, high = positive(fx), -negative(fx_hi)
    coef[0] = (
        1.0
        + (negative(fx) - positive(fx_hi))
        + (negative(fy) - positive(fy_hi))
        + (negative(fz) - positive(fz_hi))
    )
    coef[1] = jnp.where(is_first, low, high)
    coef[2] = jnp.where(is_first, high, low)
    coef[3] = positive(fy)
    coef[4] = -negative(fy_hi)
    coef[5] = positive(fz)
    coef[6] = -negative(fz_hi)
    w_in = w_in_ref[...]
    w_out = w_out_ref[...]

    def transport(k0):
        moved = []
        for k in range(k0, k0 + group):
            own = own_ref[k]
            halo = jnp.concatenate([halo_ref[s, k].astype(jnp.float32) for s in range(count)], 0)
            out = coef[0, pl.ds(k, 1)] * own
            out += coef[1, pl.ds(k, 1)] * halo
            out += coef[2, pl.ds(k, 1)] * other_ref[k]
            out += coef[3, pl.ds(k, 1)] * pltpu.roll(own, 1, 1)
            out += coef[4, pl.ds(k, 1)] * pltpu.roll(own, width_y - 1, 1)
            if k > 0:
                out += coef[5, pl.ds(k, 1)] * own_ref[k - 1]
            if k < depth - 1:
                out += coef[6, pl.ds(k, 1)] * own_ref[k + 1]
            cells_ref[k] = out
            moved.append(out.astype(jnp.bfloat16))
        cells = jnp.concatenate(moved, 1)
        return jnp.dot(w_in, cells, preferred_element_type=jnp.float32)

    def activate(half):
        return (half + half * jnp.tanh(half)).astype(jnp.bfloat16)

    def finish(k0, hidden):
        change = jnp.dot(w_out, hidden, preferred_element_type=jnp.float32)
        for i in range(group):
            new = cells_ref[k0 + i] + change[:, i * width_y : (i + 1) * width_y]
            if not last:
                new_ref[k0 + i] = new
            for s in range(count):
                send_ref[s, k0 + i] = new[s * spec : (s + 1) * spec].astype(jnp.bfloat16)

    half = transport(0)
    for k0 in range(0, depth, group):
        ahead = transport(k0 + group) if k0 + group < depth else None
        finish(k0, activate(half))
        half = ahead
    if last and not is_a:
        for d in range(count):
            outs[d][0] = send_ref[at_ref[1] ^ d]
            outs[d][1] = sent_a_ref[at_ref[1] ^ d]


def finish_kernel(depth, width, at_ref, *refs):
    out_ref = refs[-1]
    count, spec = len(refs) - 1, refs[0].shape[2]
    for d in range(count):
        place = place_of(at_ref[1] ^ d, at_ref[0], count)
        b_at = 2 * place + lax.rem(place, 2)
        a_at = 2 * place + 1 - lax.rem(place, 2)
        for side, x in enumerate((b_at, a_at)):
            for k in range(depth):
                out_ref[pl.ds(k * width + x, spec, stride=depth * width), :] = refs[d][side, k].astype(
                    jnp.float32
                )


def call(kernel, out_shape, args, scratch=(), limit=LIMIT, flops=0, trans=0):
    many = isinstance(out_shape, (list, tuple))
    moved = sum(a.size * a.dtype.itemsize for a in args)
    moved += sum(o.size * o.dtype.itemsize for o in (out_shape if many else [out_shape]))
    return pl.pallas_call(
        kernel,
        out_shape=out_shape,
        in_specs=[SMEM if a.dtype == jnp.int32 else VMEM for a in args],
        out_specs=[VMEM] * len(out_shape) if many else VMEM,
        scratch_shapes=scratch,
        compiler_params=pltpu.CompilerParams(vmem_limit_bytes=limit),
        cost_estimate=pl.CostEstimate(flops=flops, bytes_accessed=moved, transcendentals=trans),
    )(*args)


def by_columns(tracers, fluxes, weight_in, weight_out):
    spec, depth, width, width_y = tracers.shape
    count, tiles = lax.axis_size("species"), lax.axis_size("tile")
    spec_all, hid = spec * count, weight_in.shape[0]
    f32, bf16 = jnp.float32, jnp.bfloat16
    shape = jax.ShapeDtypeStruct

    chain = []
    for t in range(tiles):
        for place in range(count):
            s = place if t % 2 == 0 else count - 1 - place
            chain.append(s * tiles + t)
    swap_a, swap_b = [], []
    for i in range(len(chain) - 1):
        (swap_a if i % 2 == 0 else swap_b).extend(
            [(chain[i], chain[i + 1]), (chain[i + 1], chain[i])]
        )

    tile = lax.axis_index("tile").astype(jnp.int32)
    species = lax.axis_index("species").astype(jnp.int32)
    at = jnp.stack([tile, species, place_of(species, tile, count)])
    w_in = weight_in * jnp.asarray(0.5, bf16)
    w_out = weight_out * jnp.asarray(0.5, bf16)

    def exchange(pieces):
        got = list(pieces)
        for d in [*range(2, count), 1]:
            got[d] = lax.ppermute(pieces[d], "species", [(s, s ^ d) for s in range(count)])
        return got

    piece = shape((2 * depth + 6, spec, width_y), bf16)
    packed = call(
        functools.partial(pack_kernel, count, depth, width),
        [piece] * count,
        (at, tracers.reshape(-1, width_y), fluxes.reshape(-1, width_y)),
    )
    got = exchange(packed)
    row = shape((depth, spec_all, width_y), f32)
    message = shape((count, depth + 1, spec, width_y), bf16)
    sent = shape((count, depth, spec, width_y), bf16)
    edges = shape((STEPS, depth, width_y), f32)
    b, a, send_b, send_a, flux = call(
        functools.partial(unpack_kernel, depth),
        [row, row, message, message, shape((STEPS, 6, count, depth // count, width_y), f32)],
        (at, *got),
    )
    halo_b = lax.ppermute(send_b, AXES, swap_b)
    halo_a = lax.ppermute(send_a, AXES, swap_a)

    def step(t, is_a, own, other, halo, edge, more=()):
        last = t == STEPS - 1
        outs = [sent, row, edges][: 3 if t == 0 else 2]
        scratch = []
        if last:
            outs = [sent] if is_a else [shape((2, depth, spec, width_y), bf16)] * count
            scratch = [] if is_a else [pltpu.VMEM(sent.shape, bf16)]
        return call(
            functools.partial(step_kernel, t, is_a, GROUP),
            outs,
            (at, own, other, halo, flux, edge, w_in, w_out, *more),
            scratch=[*scratch, pltpu.VMEM((7, depth, width_y), f32), pltpu.VMEM(row.shape, f32)],
            flops=4 * depth * width_y * spec_all * hid,
            trans=depth * width_y * hid,
        )

    edge_a = edge_b = flux
    for t in range(STEPS):
        first, last = t == 0, t == STEPS - 1
        made_a = step(t, True, a, b, halo_a, edge_a)
        if last:
            pieces = step(t, False, b, a, halo_b, edge_b, made_a)
            break
        halo_a = lax.ppermute(made_a[0], AXES, swap_a)
        made_b = step(t, False, b, a, halo_b, edge_b)
        halo_b = lax.ppermute(made_b[0], AXES, swap_b)
        if first:
            edge_a, edge_b = made_a[2], made_b[2]
        a, b = made_a[1], made_b[1]
    out = call(
        functools.partial(finish_kernel, depth, width),
        shape((spec * depth * width, width_y), f32),
        (at, *exchange(pieces)),
    )
    return out.reshape(tracers.shape)


def per_device(tracers, fluxes, weight_in, weight_out):
    spec, depth, width, width_y = tracers.shape
    count = lax.axis_size("species")
    fits = (
        width == 2 * count
        and count % 2 == 0
        and count & (count - 1) == 0
        and depth % count == 0
        and depth % GROUP == 0
        and spec == PACK
        and width_y % 128 == 0
        and width % 8 == 0
        and STEPS * (depth // count) == PACK
    )
    chosen = by_columns if fits else by_levels
    return chosen(tracers, fluxes, weight_in, weight_out)


def solution(mesh):
    placed = (P("species", None, "tile", None), P(None, None, "species", "tile", None), P(), P())
    return jax.shard_map(
        per_device,
        mesh=mesh,
        in_specs=placed,
        out_specs=P("species", None, "tile", None),
        check_vma=False,
    )
```

```python
import functools

import jax
import jax.numpy as jnp
from jax import lax
from jax.experimental import pallas as pl
from jax.experimental.pallas import tpu as pltpu
from jax.sharding import PartitionSpec as P

STEPS = 4
AXES = ("species", "tile")
PACK = 16
GROUP = 4
PARTS = 4
VMEM = pl.BlockSpec(memory_space=pltpu.VMEM)
SMEM = pl.BlockSpec(memory_space=pltpu.SMEM)
LIMIT = 24 * 1024 * 1024
FULL = 56 * 1024 * 1024


def positive(value):
    return jnp.maximum(value, 0.0)


def negative(value):
    return jnp.minimum(value, 0.0)


def extended(cells, sides, width):
    for axis, dim in sides:
        count = lax.axis_size(axis)
        ends = count - 1
        head = lax.slice_in_dim(cells, 0, width, axis=dim)
        tail = lax.slice_in_dim(cells, cells.shape[dim] - width, cells.shape[dim], axis=dim)
        cells = jnp.concatenate(
            [
                lax.ppermute(tail, axis, [(i, (i + 1) % count) for i in range(ends)]),
                cells,
                lax.ppermute(head, axis, [((i + 1) % count, i) for i in range(ends)]),
            ],
            axis=dim,
        )
    return cells


def advance(padded_state, padded_x, flux_y, padded_z):
    inner = padded_state[:, 1:-1, 1:-1]
    along_x = padded_state[:, 1:-1]
    face_x = padded_x[:, 1:]
    faces_x = positive(face_x) * along_x[:, :, :-1] + negative(face_x) * along_x[:, :, 1:]
    along_z = padded_state[:, :, 1:-1]
    face_z = padded_z[1:]
    faces_z = positive(face_z) * along_z[:, :-1] + negative(face_z) * along_z[:, 1:]
    faces_y = positive(flux_y) * jnp.roll(inner, 1, 3) + negative(flux_y) * inner
    return (
        inner
        + faces_x[:, :, :-1]
        - faces_x[:, :, 1:]
        + faces_y
        - jnp.roll(faces_y, -1, 3)
        + faces_z[:, :-1]
        - faces_z[:, 1:]
    )


def by_levels(tracers, fluxes, weight_in, weight_out):
    spec_loc, depth_all, width_x, width_y = tracers.shape
    tile_at = lax.axis_index("tile")
    state = lax.all_to_all(tracers, "species", split_axis=1, concat_axis=0, tiled=True)
    spec_all, lev_loc = (state.shape[0], state.shape[1])
    grid_shape = (lev_loc, width_x, width_y)
    column = tile_at * width_x + lax.broadcasted_iota(jnp.int32, grid_shape, 1)
    level_at = lax.axis_index("species") * lev_loc + lax.broadcasted_iota(jnp.int32, grid_shape, 0)
    for interval in range(STEPS):
        own_flux = fluxes[interval]
        flux_x = jnp.where(column == 0, 0.0, own_flux[0])
        flux_y = own_flux[1]
        flux_z = jnp.where(level_at == 0, 0.0, own_flux[2])
        stacked = jnp.concatenate([state, flux_x[None], flux_z[None]], 0)
        padded = extended(stacked, (("species", 1), ("tile", 2)), 1)
        padded_state = padded[:spec_all]
        padded_x = padded[spec_all, 1:-1]
        padded_z = padded[spec_all + 1, :, 1:-1]
        state = advance(padded_state, padded_x, flux_y, padded_z)
        flattened = state.astype(jnp.bfloat16).reshape(spec_all, lev_loc, width_x * width_y)
        hidden = jax.nn.silu(
            jnp.einsum("hs,szc->hzc", weight_in, flattened, preferred_element_type=jnp.float32)
        ).astype(jnp.bfloat16)
        tendency = (
            0.5 * jnp.einsum("sh,hzc->szc", weight_out, hidden, preferred_element_type=jnp.float32)
        ).astype(jnp.bfloat16)
        state = state + tendency.reshape(state.shape).astype(jnp.float32)
    return lax.all_to_all(state, "species", split_axis=0, concat_axis=1, tiled=True)


def place_of(species, tile, count):
    return jnp.where(lax.rem(tile, 2) == 1, count - 1 - species, species)


def columns_of(place):
    return (2 * place, 2 * place + 1) if place % 2 == 0 else (2 * place + 1, 2 * place)


def for_each_place(at_ref, count, act):
    for own in range(count):
        pl.when(at_ref[2] == own)(functools.partial(act, own))


def pack_kernel(count, at_ref, tracers_ref, fluxes_ref, *refs):
    out_refs, (held, flux_ref, sems) = refs[:count], refs[count:]
    parts, spec, rows, width_y = held.shape
    width = 2 * count
    lev = rows // width
    depth = parts * lev
    lev_own = fluxes_ref.shape[0] // (STEPS * 3 * width)
    copies = [pltpu.make_async_copy(fluxes_ref, flux_ref, sems.at[parts])]
    for part in range(parts):
        source = tracers_ref.at[:, pl.ds(part * rows, rows), :]
        copies.append(pltpu.make_async_copy(source, held.at[part], sems.at[part]))
    for copy in copies:
        copy.start()
    outer = at_ref[0] == 0

    def fluxes(own):
        for d in range(count):
            place = own ^ d
            b_at, a_at = columns_of(place)

            def tile_of(direction, x):
                return jnp.concatenate(
                    [
                        flux_ref[
                            pl.ds((t * 3 + direction) * lev_own * width + x, lev_own, stride=width), :
                        ]
                        for t in range(STEPS)
                    ],
                    0,
                )

            first = tile_of(0, 2 * place)
            if place == 0:
                first = jnp.where(outer, 0.0, first)
            out_refs[d][depth] = first.astype(jnp.bfloat16)
            others = ((0, 2 * place + 1), (1, b_at), (1, a_at), (2, b_at), (2, a_at))
            for i, (direction, x) in enumerate(others):
                out_refs[d][2 * depth + 1 + i] = tile_of(direction, x).astype(jnp.bfloat16)

    def tracers(part, own):
        flat = held.at[part].reshape(spec * rows, width_y)
        for d in range(count):
            b_at, a_at = columns_of(own ^ d)
            for base, x in ((0, b_at), (depth + 1, a_at)):
                for k in range(lev):
                    cells = flat[pl.ds(k * width + x, spec, stride=rows), :]
                    out_refs[d][base + part * lev + k] = cells.astype(jnp.bfloat16)

    copies[0].wait()
    for_each_place(at_ref, count, fluxes)
    for part in range(parts):
        copies[1 + part].wait()
        for_each_place(at_ref, count, functools.partial(tracers, part))


def unpack_kernel(depth, at_ref, *refs):
    count = len(refs) - 5
    got, (b_ref, a_ref, msg_b_ref, msg_a_ref, flux_ref) = refs[:count], refs[count:]
    lev = depth // count
    spec = got[0].shape[1]
    for d in range(count):
        source = at_ref[1] ^ d
        rows = pl.ds(pl.multiple_of(source * spec, spec), spec)
        for base, state_ref, msg_ref in ((0, b_ref, msg_b_ref), (depth + 1, a_ref, msg_a_ref)):
            first = 0 if base == 0 else 1
            for k in range(depth):
                cells = got[d][base + k]
                state_ref[k, rows] = cells.astype(jnp.float32)
                msg_ref[source, k] = cells
            msg_ref[source, depth] = got[d][depth]
        for i in range(6):
            part = got[d][depth if i == 0 else 2 * depth + i].astype(jnp.float32)
            for t in range(STEPS):
                flux_ref[t, i, source] = part[t * lev : (t + 1) * lev]


def step_kernel(t, is_a, group, tiles, at_ref, own_ref, other_ref, halo_ref, flux_ref, edge_ref, w_in_ref, w_out_ref, *rest):
    rest = list(rest)
    first, last = t == 0, t == STEPS - 1
    depth, spec_all, width_y = own_ref.shape
    count, spec = halo_ref.shape[0], halo_ref.shape[2]
    lev = depth // count
    coef, cells_ref = rest[-2:]
    if last and is_a:
        send_ref = rest[0]
    elif last:
        sent_a_ref, outs, send_ref = rest[0], rest[1 : 1 + count], rest[1 + count]
    else:
        send_ref, new_ref = rest[:2]

    def whole(index):
        return jnp.concatenate([flux_ref[t, index, s] for s in range(count)], 0)

    if first:
        parts = [halo_ref[s, depth].astype(jnp.float32) for s in range(count)]
        for i in range(STEPS):
            rest[2][i] = jnp.concatenate([p[i * lev : (i + 1) * lev] for p in parts], 0)
        if not is_a:
            is_end = jnp.logical_and(at_ref[0] == tiles - 1, at_ref[2] == count - 1)
            for i in range(STEPS):
                rest[2][i] = jnp.where(is_end, 0.0, rest[2][i])
        beyond = rest[2][t]
    else:
        beyond = edge_ref[t]
    is_first = lax.rem(at_ref[2], 2) == (1 if is_a else 0)
    fx_first, fx_second = whole(0), whole(1)
    fx = jnp.where(is_first, fx_first, fx_second)
    fx_hi = jnp.where(is_first, fx_second, beyond)
    fy = whole(3 if is_a else 2)
    fy_hi = pltpu.roll(fy, width_y - 1, 1)
    fz = whole(5 if is_a else 4)
    fz = jnp.where(lax.broadcasted_iota(jnp.int32, fz.shape, 0) == 0, 0.0, fz)
    fz_hi = jnp.concatenate([fz[1:], jnp.zeros_like(fz[:1])], 0)
    low, high = positive(fx), -negative(fx_hi)
    coef[0] = (
        1.0
        + (negative(fx) - positive(fx_hi))
        + (negative(fy) - positive(fy_hi))
        + (negative(fz) - positive(fz_hi))
    )
    coef[1] = jnp.where(is_first, low, high)
    coef[2] = jnp.where(is_first, high, low)
    coef[3] = positive(fy)
    coef[4] = -negative(fy_hi)
    coef[5] = positive(fz)
    coef[6] = -negative(fz_hi)
    w_in = w_in_ref[...]
    w_out = w_out_ref[...]

    def transport(k0):
        moved = []
        for k in range(k0, k0 + group):
            own = own_ref[k]
            halo = jnp.concatenate([halo_ref[s, k].astype(jnp.float32) for s in range(count)], 0)
            out = coef[0, pl.ds(k, 1)] * own
            out += coef[1, pl.ds(k, 1)] * halo
            out += coef[2, pl.ds(k, 1)] * other_ref[k]
            out += coef[3, pl.ds(k, 1)] * pltpu.roll(own, 1, 1)
            out += coef[4, pl.ds(k, 1)] * pltpu.roll(own, width_y - 1, 1)
            if k > 0:
                out += coef[5, pl.ds(k, 1)] * own_ref[k - 1]
            if k < depth - 1:
                out += coef[6, pl.ds(k, 1)] * own_ref[k + 1]
            cells_ref[k] = out
            moved.append(out.astype(jnp.bfloat16))
        cells = jnp.concatenate(moved, 1)
        return jnp.dot(w_in, cells, preferred_element_type=jnp.float32)

    def activate(half):
        half = half.astype(jnp.bfloat16)
        return half + half * jnp.tanh(half)

    def finish(k0, hidden):
        change = jnp.dot(w_out, hidden, preferred_element_type=jnp.float32)
        for i in range(group):
            new = cells_ref[k0 + i] + change[:, i * width_y : (i + 1) * width_y]
            if not last:
                new_ref[k0 + i] = new
            for s in range(count):
                send_ref[s, k0 + i] = new[s * spec : (s + 1) * spec].astype(jnp.bfloat16)

    half = transport(0)
    for k0 in range(0, depth, group):
        ahead = transport(k0 + group) if k0 + group < depth else None
        finish(k0, activate(half))
        half = ahead
    if last and not is_a:
        for d in range(count):
            outs[d][0] = send_ref[at_ref[1] ^ d]
            outs[d][1] = sent_a_ref[at_ref[1] ^ d]


def finish_kernel(at_ref, *refs):
    out_ref, held, sems = refs[-3:]
    count, depth, spec = len(refs) - 3, refs[0].shape[1], refs[0].shape[2]
    parts, _, rows, width_y = held.shape
    width = 2 * count
    lev = rows // width

    def store(part, own):
        flat = held.at[part].reshape(spec * rows, width_y)
        for d in range(count):
            for side, x in enumerate(columns_of(own ^ d)):
                for k in range(lev):
                    cells = refs[d][side, part * lev + k].astype(jnp.float32)
                    flat[pl.ds(k * width + x, spec, stride=rows), :] = cells

    copies = []
    for part in range(parts):
        for_each_place(at_ref, count, functools.partial(store, part))
        target = out_ref.at[:, pl.ds(part * rows, rows), :]
        copies.append(pltpu.make_async_copy(held.at[part], target, sems.at[part]))
        copies[-1].start()
    for copy in copies:
        copy.wait()


def call(kernel, out_shape, args, scratch=(), limit=LIMIT, far=(), far_out=False, flops=0, trans=0):
    many = isinstance(out_shape, (list, tuple))
    moved = sum(a.size * a.dtype.itemsize for a in args)
    moved += sum(o.size * o.dtype.itemsize for o in (out_shape if many else [out_shape]))
    anywhere = pl.BlockSpec(memory_space=pl.ANY)
    return pl.pallas_call(
        kernel,
        out_shape=out_shape,
        in_specs=[
            anywhere if i in far else SMEM if a.dtype == jnp.int32 else VMEM
            for i, a in enumerate(args)
        ],
        out_specs=[VMEM] * len(out_shape) if many else anywhere if far_out else VMEM,
        scratch_shapes=scratch,
        compiler_params=pltpu.CompilerParams(vmem_limit_bytes=limit),
        cost_estimate=pl.CostEstimate(flops=flops, bytes_accessed=moved, transcendentals=trans),
    )(*args)


def by_columns(tracers, fluxes, weight_in, weight_out):
    spec, depth, width, width_y = tracers.shape
    count, tiles = lax.axis_size("species"), lax.axis_size("tile")
    spec_all, hid = spec * count, weight_in.shape[0]
    f32, bf16 = jnp.float32, jnp.bfloat16
    shape = jax.ShapeDtypeStruct

    chain = []
    for t in range(tiles):
        for place in range(count):
            s = place if t % 2 == 0 else count - 1 - place
            chain.append(s * tiles + t)
    swap_a, swap_b = [], [(chain[0], chain[0]), (chain[-1], chain[-1])]
    for i in range(len(chain) - 1):
        (swap_a if i % 2 == 0 else swap_b).extend(
            [(chain[i], chain[i + 1]), (chain[i + 1], chain[i])]
        )

    tile = lax.axis_index("tile").astype(jnp.int32)
    species = lax.axis_index("species").astype(jnp.int32)
    at = jnp.stack([tile, species, place_of(species, tile, count)])
    w_in = weight_in * jnp.asarray(0.5, bf16)
    w_out = weight_out * jnp.asarray(0.5, bf16)

    def exchange(pieces):
        got = list(pieces)
        for d in [*range(2, count), 1]:
            got[d] = lax.ppermute(pieces[d], "species", [(s, s ^ d) for s in range(count)])
        return got

    piece = shape((2 * depth + 6, spec, width_y), bf16)
    held = pltpu.VMEM((PARTS, spec, depth * width // PARTS, width_y), f32)
    flux_rows = fluxes.reshape(-1, width_y)
    packed = call(
        functools.partial(pack_kernel, count),
        [piece] * count,
        (at, tracers.reshape(spec, depth * width, width_y), flux_rows),
        scratch=[
            held,
            pltpu.VMEM(flux_rows.shape, f32),
            pltpu.SemaphoreType.DMA((PARTS + 1,)),
        ],
        limit=FULL,
        far=(1, 2),
    )
    got = exchange(packed)
    row = shape((depth, spec_all, width_y), f32)
    message = shape((count, depth + 1, spec, width_y), bf16)
    sent = shape((count, depth, spec, width_y), bf16)
    edges = shape((STEPS, depth, width_y), f32)
    b, a, send_b, send_a, flux = call(
        functools.partial(unpack_kernel, depth),
        [row, row, message, message, shape((STEPS, 6, count, depth // count, width_y), f32)],
        (at, *got),
    )
    halo_b = lax.ppermute(send_b, AXES, swap_b)
    halo_a = lax.ppermute(send_a, AXES, swap_a)

    def step(t, is_a, own, other, halo, edge, more=()):
        last = t == STEPS - 1
        outs = [sent, row, edges][: 3 if t == 0 else 2]
        scratch = []
        if last:
            outs = [sent] if is_a else [shape((2, depth, spec, width_y), bf16)] * count
            scratch = [] if is_a else [pltpu.VMEM(sent.shape, bf16)]
        return call(
            functools.partial(step_kernel, t, is_a, GROUP, tiles),
            outs,
            (at, own, other, halo, flux, edge, w_in, w_out, *more),
            scratch=[*scratch, pltpu.VMEM((7, depth, width_y), f32), pltpu.VMEM(row.shape, f32)],
            flops=4 * depth * width_y * spec_all * hid,
            trans=depth * width_y * hid,
        )

    edge_a = edge_b = flux
    for t in range(STEPS):
        first, last = t == 0, t == STEPS - 1
        made_a = step(t, True, a, b, halo_a, edge_a)
        if last:
            pieces = step(t, False, b, a, halo_b, edge_b, made_a)
            break
        halo_a = lax.ppermute(made_a[0], AXES, swap_a)
        made_b = step(t, False, b, a, halo_b, edge_b)
        halo_b = lax.ppermute(made_b[0], AXES, swap_b)
        if first:
            edge_a, edge_b = made_a[2], made_b[2]
        a, b = made_a[1], made_b[1]
    out = call(
        finish_kernel,
        shape((spec, depth * width, width_y), f32),
        (at, *exchange(pieces)),
        scratch=[held, pltpu.SemaphoreType.DMA((PARTS,))],
        far_out=True,
    )
    return out.reshape(tracers.shape)


def per_device(tracers, fluxes, weight_in, weight_out):
    spec, depth, width, width_y = tracers.shape
    count = lax.axis_size("species")
    fits = (
        width == 2 * count
        and count % 2 == 0
        and count & (count - 1) == 0
        and depth % count == 0
        and depth % GROUP == 0
        and depth % PARTS == 0
        and spec == PACK
        and width_y % 128 == 0
        and width % 8 == 0
        and STEPS * (depth // count) == PACK
    )
    chosen = by_columns if fits else by_levels
    return chosen(tracers, fluxes, weight_in, weight_out)


def solution(mesh):
    placed = (P("species", None, "tile", None), P(None, None, "species", "tile", None), P(), P())
    return jax.shard_map(
        per_device,
        mesh=mesh,
        in_specs=placed,
        out_specs=P("species", None, "tile", None),
        check_vma=False,
    )
```

```python
import functools

import jax
import jax.numpy as jnp
from jax import lax
from jax.experimental import pallas as pl
from jax.experimental.pallas import tpu as pltpu
from jax.sharding import PartitionSpec as P

STEPS = 4
AXES = ("species", "tile")
PACK = 16
GROUP = 4
PARTS = 4
VMEM = pl.BlockSpec(memory_space=pltpu.VMEM)
LIMIT = 24 * 1024 * 1024
FULL = 56 * 1024 * 1024


def positive(value):
    return jnp.maximum(value, 0.0)


def negative(value):
    return jnp.minimum(value, 0.0)


def extended(cells, sides, width):
    for axis, dim in sides:
        count = lax.axis_size(axis)
        ends = count - 1
        head = lax.slice_in_dim(cells, 0, width, axis=dim)
        tail = lax.slice_in_dim(cells, cells.shape[dim] - width, cells.shape[dim], axis=dim)
        cells = jnp.concatenate(
            [
                lax.ppermute(tail, axis, [(i, (i + 1) % count) for i in range(ends)]),
                cells,
                lax.ppermute(head, axis, [((i + 1) % count, i) for i in range(ends)]),
            ],
            axis=dim,
        )
    return cells


def advance(padded_state, padded_x, flux_y, padded_z):
    inner = padded_state[:, 1:-1, 1:-1]
    along_x = padded_state[:, 1:-1]
    face_x = padded_x[:, 1:]
    faces_x = positive(face_x) * along_x[:, :, :-1] + negative(face_x) * along_x[:, :, 1:]
    along_z = padded_state[:, :, 1:-1]
    face_z = padded_z[1:]
    faces_z = positive(face_z) * along_z[:, :-1] + negative(face_z) * along_z[:, 1:]
    faces_y = positive(flux_y) * jnp.roll(inner, 1, 3) + negative(flux_y) * inner
    return (
        inner
        + faces_x[:, :, :-1]
        - faces_x[:, :, 1:]
        + faces_y
        - jnp.roll(faces_y, -1, 3)
        + faces_z[:, :-1]
        - faces_z[:, 1:]
    )


def by_levels(tracers, fluxes, weight_in, weight_out):
    spec_loc, depth_all, width_x, width_y = tracers.shape
    tile_at = lax.axis_index("tile")
    state = lax.all_to_all(tracers, "species", split_axis=1, concat_axis=0, tiled=True)
    spec_all, lev_loc = (state.shape[0], state.shape[1])
    grid_shape = (lev_loc, width_x, width_y)
    column = tile_at * width_x + lax.broadcasted_iota(jnp.int32, grid_shape, 1)
    level_at = lax.axis_index("species") * lev_loc + lax.broadcasted_iota(jnp.int32, grid_shape, 0)
    for interval in range(STEPS):
        own_flux = fluxes[interval]
        flux_x = jnp.where(column == 0, 0.0, own_flux[0])
        flux_y = own_flux[1]
        flux_z = jnp.where(level_at == 0, 0.0, own_flux[2])
        stacked = jnp.concatenate([state, flux_x[None], flux_z[None]], 0)
        padded = extended(stacked, (("species", 1), ("tile", 2)), 1)
        padded_state = padded[:spec_all]
        padded_x = padded[spec_all, 1:-1]
        padded_z = padded[spec_all + 1, :, 1:-1]
        state = advance(padded_state, padded_x, flux_y, padded_z)
        flattened = state.astype(jnp.bfloat16).reshape(spec_all, lev_loc, width_x * width_y)
        hidden = jax.nn.silu(
            jnp.einsum("hs,szc->hzc", weight_in, flattened, preferred_element_type=jnp.float32)
        ).astype(jnp.bfloat16)
        tendency = (
            0.5 * jnp.einsum("sh,hzc->szc", weight_out, hidden, preferred_element_type=jnp.float32)
        ).astype(jnp.bfloat16)
        state = state + tendency.reshape(state.shape).astype(jnp.float32)
    return lax.all_to_all(state, "species", split_axis=0, concat_axis=1, tiled=True)


def place_and_species(count):
    species = lax.axis_index("species")
    return jnp.where(lax.rem(lax.axis_index("tile"), 2) == 1, count - 1 - species, species), species


def columns_of(place):
    odd = lax.rem(place, 2)
    return 2 * place + odd, 2 * place + 1 - odd


def pack_kernel(count, tracers_ref, fluxes_ref, *refs):
    out_refs, (held, flux_ref, sems) = refs[:count], refs[count:]
    parts, spec, rows, width_y = held.shape
    width = 2 * count
    lev = rows // width
    depth = parts * lev
    lev_own = fluxes_ref.shape[0] // (STEPS * 3 * width)
    own, _ = place_and_species(count)
    outer = lax.axis_index("tile") == 0
    copies = []
    for part in range(parts):
        source = tracers_ref.at[:, pl.ds(part * rows, rows), :]
        copies.append(pltpu.make_async_copy(source, held.at[part], sems.at[part]))
    copies.append(pltpu.make_async_copy(fluxes_ref, flux_ref, sems.at[parts]))
    for copy in copies:
        copy.start()

    columns = [columns_of(own ^ d) for d in range(count)]
    for part in range(parts):
        copies[part].wait()
        flat = held.at[part].reshape(spec * rows, width_y)

        def level(k, carry):
            for d in range(count):
                for base, x in zip((0, depth + 1), columns[d]):
                    cells = flat[pl.ds(k * width + x, spec, stride=rows), :]
                    out_refs[d][base + part * lev + k] = cells.astype(jnp.bfloat16)
            return carry

        lax.fori_loop(0, lev, level, 0)

    copies[parts].wait()
    for d in range(count):
        b_at, a_at = columns[d]
        low = jnp.minimum(b_at, a_at)

        def tile_of(direction, x):
            return jnp.concatenate(
                [
                    flux_ref[pl.ds((t * 3 + direction) * lev_own * width + x, lev_own, stride=width), :]
                    for t in range(STEPS)
                ],
                0,
            )

        first = jnp.where(jnp.logical_and(outer, low == 0), 0.0, tile_of(0, low))
        out_refs[d][depth] = first.astype(jnp.bfloat16)
        others = ((0, low + 1), (1, b_at), (1, a_at), (2, b_at), (2, a_at))
        for i, (direction, x) in enumerate(others):
            out_refs[d][2 * depth + 1 + i] = tile_of(direction, x).astype(jnp.bfloat16)


def unpack_kernel(depth, *refs):
    count = len(refs) - 7
    got, refs = refs[:count], refs[count:]
    b_ref, a_ref, msg_b_ref, msg_a_ref, flux_ref, kept, sem = refs
    copy = pltpu.make_async_copy(got[0], kept, sem)
    copy.start()
    got = [kept, *got[1:]]
    lev = depth // count
    spec = got[0].shape[1]
    _, species = place_and_species(count)

    def level(d, k, carry):
        rows = pl.ds(pl.multiple_of((species ^ d) * spec, spec), spec)
        for base, state_ref, msg_ref in ((0, b_ref, msg_b_ref), (depth + 1, a_ref, msg_a_ref)):
            cells = got[d][base + k]
            state_ref[k, rows] = cells.astype(jnp.float32)
            msg_ref[species ^ d, k] = cells
        return carry

    for d in [*range(1, count), 0]:
        if d == 0:
            copy.wait()
        lax.fori_loop(0, depth, functools.partial(level, d), 0, unroll=4)
        source = species ^ d
        for msg_ref in (msg_b_ref, msg_a_ref):
            msg_ref[source, depth] = got[d][depth]
        for i in range(6):
            part = got[d][depth if i == 0 else 2 * depth + i].astype(jnp.float32)
            for t in range(STEPS):
                flux_ref[t, i, source] = part[t * lev : (t + 1) * lev]


def step_kernel(t, is_a, group, own_ref, other_ref, halo_ref, flux_ref, edge_ref, w_in_ref, w_out_ref, *rest):
    rest = list(rest)
    first, last = t == 0, t == STEPS - 1
    depth, spec_all, width_y = own_ref.shape
    count, spec = halo_ref.shape[0], halo_ref.shape[2]
    lev = depth // count
    place, species = place_and_species(count)
    coef, moved_ref, cells_ref = rest[-3:]
    if last and is_a:
        send_ref = rest[0]
    elif last:
        sent_a_ref, outs, send_ref = rest[0], rest[1 : 1 + count], rest[1 + count]
    else:
        send_ref, new_ref = rest[:2]

    def whole(index):
        return jnp.concatenate([flux_ref[t, index, s] for s in range(count)], 0)

    if first:
        parts = [halo_ref[s, depth].astype(jnp.float32) for s in range(count)]
        for i in range(STEPS):
            rest[2][i] = jnp.concatenate([p[i * lev : (i + 1) * lev] for p in parts], 0)
        beyond = rest[2][t]
    else:
        beyond = edge_ref[t]
    is_first = lax.rem(place, 2) == (1 if is_a else 0)
    fx_first, fx_second = whole(0), whole(1)
    fx = jnp.where(is_first, fx_first, fx_second)
    fx_hi = jnp.where(is_first, fx_second, beyond)
    fy = whole(3 if is_a else 2)
    fy_hi = pltpu.roll(fy, width_y - 1, 1)
    fz = whole(5 if is_a else 4)
    fz = jnp.where(lax.broadcasted_iota(jnp.int32, fz.shape, 0) == 0, 0.0, fz)
    fz_hi = jnp.concatenate([fz[1:], jnp.zeros_like(fz[:1])], 0)
    low, high = positive(fx), -negative(fx_hi)
    coef[0] = (
        1.0
        + (negative(fx) - positive(fx_hi))
        + (negative(fy) - positive(fy_hi))
        + (negative(fz) - positive(fz_hi))
    )
    coef[1] = jnp.where(is_first, low, high)
    coef[2] = jnp.where(is_first, high, low)
    coef[3] = positive(fy)
    coef[4] = -negative(fy_hi)
    coef[5] = positive(fz)
    coef[6] = -negative(fz_hi)
    w_in = w_in_ref[...]
    w_out = w_out_ref[...]

    def level(k, slot, column):
        own = own_ref[k]
        halo = jnp.concatenate([halo_ref[s, k].astype(jnp.float32) for s in range(count)], 0)
        out = coef[0, pl.ds(k, 1)] * own
        out += coef[1, pl.ds(k, 1)] * halo
        out += coef[2, pl.ds(k, 1)] * other_ref[k]
        out += coef[3, pl.ds(k, 1)] * pltpu.roll(own, 1, 1)
        out += coef[4, pl.ds(k, 1)] * pltpu.roll(own, width_y - 1, 1)
        out += coef[5, pl.ds(k, 1)] * own_ref[jnp.maximum(k - 1, 0)]
        out += coef[6, pl.ds(k, 1)] * own_ref[jnp.minimum(k + 1, depth - 1)]
        moved_ref[k] = out
        cells_ref[slot, :, column * width_y : (column + 1) * width_y] = out.astype(jnp.bfloat16)

    groups = depth // group

    def body(g, carry):
        slot = lax.rem(g, 2)
        half = jnp.dot(w_in, cells_ref[slot], preferred_element_type=jnp.float32)
        ahead = jnp.minimum(g + 1, groups - 1)
        for i in range(group):
            level(ahead * group + i, 1 - slot, i)
        hidden = (half + half * jnp.tanh(half)).astype(jnp.bfloat16)
        change = jnp.dot(w_out, hidden, preferred_element_type=jnp.float32)
        for i in range(group):
            k = g * group + i
            new = moved_ref[k] + change[:, i * width_y : (i + 1) * width_y]
            if not last:
                new_ref[k] = new
            for s in range(count):
                send_ref[s, k] = new[s * spec : (s + 1) * spec].astype(jnp.bfloat16)
        return carry

    for i in range(group):
        level(i, 0, i)
    lax.fori_loop(0, groups, body, 0)
    if last and not is_a:
        for d in range(count):
            outs[d][0] = send_ref[species ^ d]
            outs[d][1] = sent_a_ref[species ^ d]


def finish_kernel(*refs):
    out_ref, held, sems = refs[-3:]
    count, spec = len(refs) - 3, refs[0].shape[2]
    parts, _, rows, width_y = held.shape
    width = 2 * count
    lev = rows // width
    own, _ = place_and_species(count)
    columns = [columns_of(own ^ d) for d in range(count)]
    copies = []
    for part in range(parts):
        flat = held.at[part].reshape(spec * rows, width_y)

        def level(k, carry):
            for d in range(count):
                for side, x in enumerate(columns[d]):
                    cells = refs[d][side, part * lev + k].astype(jnp.float32)
                    flat[pl.ds(k * width + x, spec, stride=rows), :] = cells
            return carry

        lax.fori_loop(0, lev, level, 0)
        target = out_ref.at[:, pl.ds(part * rows, rows), :]
        copies.append(pltpu.make_async_copy(held.at[part], target, sems.at[part]))
        copies[-1].start()
    for copy in copies:
        copy.wait()


def call(kernel, out_shape, args, scratch=(), limit=LIMIT, far=(), far_out=False, flops=0, trans=0):
    many = isinstance(out_shape, (list, tuple))
    moved = sum(a.size * a.dtype.itemsize for a in args)
    moved += sum(o.size * o.dtype.itemsize for o in (out_shape if many else [out_shape]))
    anywhere = pl.BlockSpec(memory_space=pl.ANY)
    return pl.pallas_call(
        kernel,
        out_shape=out_shape,
        in_specs=[
            anywhere if i in far else VMEM
            for i in range(len(args))
        ],
        out_specs=[VMEM] * len(out_shape) if many else anywhere if far_out else VMEM,
        scratch_shapes=scratch,
        compiler_params=pltpu.CompilerParams(vmem_limit_bytes=limit),
        cost_estimate=pl.CostEstimate(flops=flops, bytes_accessed=moved, transcendentals=trans),
    )(*args)


def by_columns(tracers, fluxes, weight_in, weight_out):
    spec, depth, width, width_y = tracers.shape
    count, tiles = lax.axis_size("species"), lax.axis_size("tile")
    spec_all, hid = spec * count, weight_in.shape[0]
    f32, bf16 = jnp.float32, jnp.bfloat16
    shape = jax.ShapeDtypeStruct

    chain = []
    for t in range(tiles):
        for place in range(count):
            s = place if t % 2 == 0 else count - 1 - place
            chain.append(s * tiles + t)
    swap_a, swap_b = [], []
    for i in range(len(chain) - 1):
        (swap_a if i % 2 == 0 else swap_b).extend(
            [(chain[i], chain[i + 1]), (chain[i + 1], chain[i])]
        )

    w_in = weight_in * jnp.asarray(0.5, bf16)
    w_out = weight_out * jnp.asarray(0.5, bf16)

    def exchange(pieces):
        got = list(pieces)
        for d in [*range(2, count), 1]:
            got[d] = lax.ppermute(pieces[d], "species", [(s, s ^ d) for s in range(count)])
        return got

    piece = shape((2 * depth + 6, spec, width_y), bf16)
    held = pltpu.VMEM((PARTS, spec, depth * width // PARTS, width_y), f32)
    flux_rows = fluxes.reshape(-1, width_y)
    packed = call(
        functools.partial(pack_kernel, count),
        [piece] * count,
        (tracers.reshape(spec, depth * width, width_y), flux_rows),
        scratch=[
            held,
            pltpu.VMEM(flux_rows.shape, f32),
            pltpu.SemaphoreType.DMA((PARTS + 1,)),
        ],
        limit=FULL,
        far=(0, 1),
    )
    got = exchange(packed)
    row = shape((depth, spec_all, width_y), f32)
    message = shape((count, depth + 1, spec, width_y), bf16)
    sent = shape((count, depth, spec, width_y), bf16)
    edges = shape((STEPS, depth, width_y), f32)
    b, a, send_b, send_a, flux = call(
        functools.partial(unpack_kernel, depth),
        [row, row, message, message, shape((STEPS, 6, count, depth // count, width_y), f32)],
        got,
        scratch=[pltpu.VMEM(piece.shape, bf16), pltpu.SemaphoreType.DMA],
        far=(0,),
    )
    halo_b = lax.ppermute(send_b, AXES, swap_b)
    halo_a = lax.ppermute(send_a, AXES, swap_a)

    common = [
        pltpu.VMEM((7, depth, width_y), f32),
        pltpu.VMEM(row.shape, f32),
        pltpu.VMEM((2, spec_all, GROUP * width_y), bf16),
    ]

    def step(t, is_a, own, other, halo, edge, more=()):
        last = t == STEPS - 1
        outs = [sent, row, edges][: 3 if t == 0 else 2]
        scratch = []
        if last:
            outs = [sent] if is_a else [shape((2, depth, spec, width_y), bf16)] * count
            scratch = [] if is_a else [pltpu.VMEM(sent.shape, bf16)]
        return call(
            functools.partial(step_kernel, t, is_a, GROUP),
            outs,
            (own, other, halo, flux, edge, w_in, w_out, *more),
            scratch=[*scratch, *common],
            flops=4 * depth * width_y * spec_all * hid,
            trans=depth * width_y * hid,
        )

    edge_a = edge_b = flux
    for t in range(STEPS):
        first, last = t == 0, t == STEPS - 1
        made_a = step(t, True, a, b, halo_a, edge_a)
        if last:
            pieces = step(t, False, b, a, halo_b, edge_b, made_a)
            break
        halo_a = lax.ppermute(made_a[0], AXES, swap_a)
        made_b = step(t, False, b, a, halo_b, edge_b)
        halo_b = lax.ppermute(made_b[0], AXES, swap_b)
        if first:
            edge_a, edge_b = made_a[2], made_b[2]
        a, b = made_a[1], made_b[1]
    out = call(
        finish_kernel,
        shape((spec, depth * width, width_y), f32),
        exchange(pieces),
        scratch=[held, pltpu.SemaphoreType.DMA((PARTS,))],
        far_out=True,
    )
    return out.reshape(tracers.shape)


def per_device(tracers, fluxes, weight_in, weight_out):
    spec, depth, width, width_y = tracers.shape
    count = lax.axis_size("species")
    fits = (
        width == 2 * count
        and count % 2 == 0
        and count & (count - 1) == 0
        and depth % count == 0
        and depth % GROUP == 0
        and depth % PARTS == 0
        and spec == PACK
        and width_y % 128 == 0
        and width % 8 == 0
        and STEPS * (depth // count) == PACK
    )
    chosen = by_columns if fits else by_levels
    return chosen(tracers, fluxes, weight_in, weight_out)


def solution(mesh):
    placed = (P("species", None, "tile", None), P(None, None, "species", "tile", None), P(), P())
    return jax.shard_map(
        per_device,
        mesh=mesh,
        in_specs=placed,
        out_specs=P("species", None, "tile", None),
        check_vma=False,
    )
```

```python
import functools

import jax
import jax.numpy as jnp
from jax import lax
from jax.experimental import pallas as pl
from jax.experimental.pallas import tpu as pltpu
from jax.sharding import PartitionSpec as P

STEPS = 4
AXES = ("species", "tile")
PACK = 16
GROUP = 4
PARTS = 4
VMEM = pl.BlockSpec(memory_space=pltpu.VMEM)
LIMIT = 24 * 1024 * 1024
FULL = 56 * 1024 * 1024


def positive(value):
    return jnp.maximum(value, 0.0)


def negative(value):
    return jnp.minimum(value, 0.0)


def extended(cells, sides, width):
    for axis, dim in sides:
        count = lax.axis_size(axis)
        ends = count - 1
        head = lax.slice_in_dim(cells, 0, width, axis=dim)
        tail = lax.slice_in_dim(cells, cells.shape[dim] - width, cells.shape[dim], axis=dim)
        cells = jnp.concatenate(
            [
                lax.ppermute(tail, axis, [(i, (i + 1) % count) for i in range(ends)]),
                cells,
                lax.ppermute(head, axis, [((i + 1) % count, i) for i in range(ends)]),
            ],
            axis=dim,
        )
    return cells


def advance(padded_state, padded_x, flux_y, padded_z):
    inner = padded_state[:, 1:-1, 1:-1]
    along_x = padded_state[:, 1:-1]
    face_x = padded_x[:, 1:]
    faces_x = positive(face_x) * along_x[:, :, :-1] + negative(face_x) * along_x[:, :, 1:]
    along_z = padded_state[:, :, 1:-1]
    face_z = padded_z[1:]
    faces_z = positive(face_z) * along_z[:, :-1] + negative(face_z) * along_z[:, 1:]
    faces_y = positive(flux_y) * jnp.roll(inner, 1, 3) + negative(flux_y) * inner
    return (
        inner
        + faces_x[:, :, :-1]
        - faces_x[:, :, 1:]
        + faces_y
        - jnp.roll(faces_y, -1, 3)
        + faces_z[:, :-1]
        - faces_z[:, 1:]
    )


def by_levels(tracers, fluxes, weight_in, weight_out):
    spec_loc, depth_all, width_x, width_y = tracers.shape
    tile_at = lax.axis_index("tile")
    state = lax.all_to_all(tracers, "species", split_axis=1, concat_axis=0, tiled=True)
    spec_all, lev_loc = (state.shape[0], state.shape[1])
    grid_shape = (lev_loc, width_x, width_y)
    column = tile_at * width_x + lax.broadcasted_iota(jnp.int32, grid_shape, 1)
    level_at = lax.axis_index("species") * lev_loc + lax.broadcasted_iota(jnp.int32, grid_shape, 0)
    for interval in range(STEPS):
        own_flux = fluxes[interval]
        flux_x = jnp.where(column == 0, 0.0, own_flux[0])
        flux_y = own_flux[1]
        flux_z = jnp.where(level_at == 0, 0.0, own_flux[2])
        stacked = jnp.concatenate([state, flux_x[None], flux_z[None]], 0)
        padded = extended(stacked, (("species", 1), ("tile", 2)), 1)
        padded_state = padded[:spec_all]
        padded_x = padded[spec_all, 1:-1]
        padded_z = padded[spec_all + 1, :, 1:-1]
        state = advance(padded_state, padded_x, flux_y, padded_z)
        flattened = state.astype(jnp.bfloat16).reshape(spec_all, lev_loc, width_x * width_y)
        hidden = jax.nn.silu(
            jnp.einsum("hs,szc->hzc", weight_in, flattened, preferred_element_type=jnp.float32)
        ).astype(jnp.bfloat16)
        tendency = (
            0.5 * jnp.einsum("sh,hzc->szc", weight_out, hidden, preferred_element_type=jnp.float32)
        ).astype(jnp.bfloat16)
        state = state + tendency.reshape(state.shape).astype(jnp.float32)
    return lax.all_to_all(state, "species", split_axis=0, concat_axis=1, tiled=True)


def place_and_species(count):
    species = lax.axis_index("species")
    return jnp.where(lax.rem(lax.axis_index("tile"), 2) == 1, count - 1 - species, species), species


def columns_of(place):
    odd = lax.rem(place, 2)
    return 2 * place + odd, 2 * place + 1 - odd


def pack_kernel(count, tracers_ref, fluxes_ref, *refs):
    out_refs, (held, flux_ref, sems) = refs[:count], refs[count:]
    parts, spec, rows, width_y = held.shape
    width = 2 * count
    lev = rows // width
    depth = parts * lev
    lev_own = fluxes_ref.shape[0] // (STEPS * 3 * width)
    own, _ = place_and_species(count)
    outer = lax.axis_index("tile") == 0
    copies = []
    for part in range(parts):
        source = tracers_ref.at[:, pl.ds(part * rows, rows), :]
        copies.append(pltpu.make_async_copy(source, held.at[part], sems.at[part]))
    copies.append(pltpu.make_async_copy(fluxes_ref, flux_ref, sems.at[parts]))
    for copy in copies:
        copy.start()

    columns = [columns_of(own ^ d) for d in range(count)]
    for part in range(parts):
        copies[part].wait()
        flat = held.at[part].reshape(spec * rows, width_y)

        def level(k, carry):
            for d in range(count):
                for base, x in zip((depth + 4, 0), columns[d]):
                    cells = flat[pl.ds(k * width + x, spec, stride=rows), :]
                    out_refs[d][base + part * lev + k] = cells.astype(jnp.bfloat16)
            return carry

        lax.fori_loop(0, lev, level, 0)

    copies[parts].wait()
    for d in range(count):
        b_at, a_at = columns[d]
        low = jnp.minimum(b_at, a_at)

        def tile_of(direction, x):
            return jnp.concatenate(
                [
                    flux_ref[pl.ds((t * 3 + direction) * lev_own * width + x, lev_own, stride=width), :]
                    for t in range(STEPS)
                ],
                0,
            )

        first = jnp.where(jnp.logical_and(outer, low == 0), 0.0, tile_of(0, low))
        out_refs[d][depth] = first.astype(jnp.bfloat16)
        others = ((0, low + 1, 1), (1, b_at, 2), (2, b_at, 3), (1, a_at, depth + 4), (2, a_at, depth + 5))
        for direction, x, to in others:
            out_refs[d][depth + to] = tile_of(direction, x).astype(jnp.bfloat16)


def unpack_kernel(depth, *refs):
    count = len(refs) - 7
    got, refs = refs[:count], refs[count:]
    b_ref, a_ref, msg_b_ref, msg_a_ref, flux_ref, kept, sem = refs
    copy = pltpu.make_async_copy(got[0], kept, sem)
    copy.start()
    got = [kept, *got[1:]]
    lev = depth // count
    spec = got[0].shape[1]
    _, species = place_and_species(count)

    def level(d, k, carry):
        rows = pl.ds(pl.multiple_of((species ^ d) * spec, spec), spec)
        for base, state_ref, msg_ref in ((depth + 4, b_ref, msg_b_ref), (0, a_ref, msg_a_ref)):
            cells = got[d][base + k]
            state_ref[k, rows] = cells.astype(jnp.float32)
            msg_ref[species ^ d, k] = cells
        return carry

    for d in [*range(1, count), 0]:
        if d == 0:
            copy.wait()
        lax.fori_loop(0, depth, functools.partial(level, d), 0, unroll=4)
        source = species ^ d
        msg_a_ref[source, depth] = got[d][depth]
        for i in range(4):
            msg_b_ref[source, depth + i] = got[d][depth + i]
        for i in range(6):
            part = got[d][depth + i if i < 4 else 2 * depth + i].astype(jnp.float32)
            for t in range(STEPS):
                flux_ref[t, i, source] = part[t * lev : (t + 1) * lev]


def column_kernel(
    t, kind, group, sends, own_ref, inner_ref, outer_ref, flux_ref, from_a_ref, from_b_ref, w_in_ref, w_out_ref, *rest
):
    last = t == STEPS - 1
    coef, moved_ref, cells_ref = rest[-3:]
    count, spec, lev = from_a_ref.shape[0], from_a_ref.shape[2], flux_ref.shape[3]
    depth, spec_all, width_y = inner_ref.shape
    place, species = place_and_species(count)
    rest = list(rest)
    sent_b_ref = rest.pop(0) if last and kind == "A" else None
    outs = rest[:count] if last and kind == "A" else None
    send_ref = rest[count] if outs else rest.pop(0) if sends else None
    new_ref = None if last else rest.pop(0)

    def cells_of(ref, k):
        if ref.shape == inner_ref.shape:
            return ref[k]
        return jnp.concatenate([ref[s, k].astype(jnp.float32) for s in range(count)], 0)

    def mine(index):
        return jnp.concatenate([flux_ref[t, index, s] for s in range(count)], 0)

    def theirs(ref, index):
        parts = [ref[s, depth + index].astype(jnp.float32) for s in range(count)]
        return jnp.concatenate([p[t * lev : (t + 1) * lev] for p in parts], 0)

    even = lax.rem(place, 2) == 0
    if kind == "A":
        outer_high = even
        fx = jnp.where(even, mine(1), mine(0))
        fx_hi = jnp.where(even, theirs(from_a_ref, 0), mine(1))
        fy, fz = mine(4), mine(5)
    elif kind == "B":
        outer_high = jnp.logical_not(even)
        fx = jnp.where(even, mine(0), mine(1))
        fx_hi = jnp.where(even, mine(1), theirs(from_b_ref, 0))
        fy, fz = mine(2), mine(3)
    else:
        outer_high = jnp.logical_not(even)
        fx = jnp.where(even, theirs(from_b_ref, 1), theirs(from_b_ref, 0))
        fx_hi = jnp.where(even, mine(0), theirs(from_b_ref, 1))
        fy, fz = theirs(from_b_ref, 2), theirs(from_b_ref, 3)
    fy_hi = pltpu.roll(fy, width_y - 1, 1)
    fz = jnp.where(lax.broadcasted_iota(jnp.int32, fz.shape, 0) == 0, 0.0, fz)
    fz_hi = jnp.concatenate([fz[1:], jnp.zeros_like(fz[:1])], 0)
    low, high = positive(fx), -negative(fx_hi)
    coef[0] = (
        1.0
        + (negative(fx) - positive(fx_hi))
        + (negative(fy) - positive(fy_hi))
        + (negative(fz) - positive(fz_hi))
    )
    coef[1] = jnp.where(outer_high, high, low)
    coef[2] = jnp.where(outer_high, low, high)
    coef[3] = positive(fy)
    coef[4] = -negative(fy_hi)
    coef[5] = positive(fz)
    coef[6] = -negative(fz_hi)
    w_in = w_in_ref[...]
    w_out = w_out_ref[...]

    def level(k, slot, column):
        own = cells_of(own_ref, k)
        out = coef[0, pl.ds(k, 1)] * own
        out += coef[1, pl.ds(k, 1)] * cells_of(outer_ref, k)
        out += coef[2, pl.ds(k, 1)] * inner_ref[k]
        out += coef[3, pl.ds(k, 1)] * pltpu.roll(own, 1, 1)
        out += coef[4, pl.ds(k, 1)] * pltpu.roll(own, width_y - 1, 1)
        out += coef[5, pl.ds(k, 1)] * cells_of(own_ref, jnp.maximum(k - 1, 0))
        out += coef[6, pl.ds(k, 1)] * cells_of(own_ref, jnp.minimum(k + 1, depth - 1))
        moved_ref[k] = out
        cells_ref[slot, :, column * width_y : (column + 1) * width_y] = out.astype(jnp.bfloat16)

    groups = depth // group

    def body(g, carry):
        slot = lax.rem(g, 2)
        half = jnp.dot(w_in, cells_ref[slot], preferred_element_type=jnp.float32)
        ahead = jnp.minimum(g + 1, groups - 1)
        for i in range(group):
            level(ahead * group + i, 1 - slot, i)
        hidden = (half + half * jnp.tanh(half)).astype(jnp.bfloat16)
        change = jnp.dot(w_out, hidden, preferred_element_type=jnp.float32)
        for i in range(group):
            k = g * group + i
            new = moved_ref[k] + change[:, i * width_y : (i + 1) * width_y]
            if new_ref is not None:
                new_ref[k] = new
            if send_ref is not None:
                for s in range(count):
                    send_ref[s, k] = new[s * spec : (s + 1) * spec].astype(jnp.bfloat16)
        return carry

    for i in range(group):
        level(i, 0, i)
    lax.fori_loop(0, groups, body, 0)
    if outs is not None:
        for d in range(count):
            outs[d][0] = sent_b_ref[species ^ d]
            outs[d][1] = send_ref[species ^ d]


def finish_kernel(*refs):
    out_ref, held, sems = refs[-3:]
    count, spec = len(refs) - 3, refs[0].shape[2]
    parts, _, rows, width_y = held.shape
    width = 2 * count
    lev = rows // width
    own, _ = place_and_species(count)
    columns = [columns_of(own ^ d) for d in range(count)]
    copies = []
    for part in range(parts):
        flat = held.at[part].reshape(spec * rows, width_y)

        def level(k, carry):
            for d in range(count):
                for side, x in enumerate(columns[d]):
                    cells = refs[d][side, part * lev + k].astype(jnp.float32)
                    flat[pl.ds(k * width + x, spec, stride=rows), :] = cells
            return carry

        lax.fori_loop(0, lev, level, 0)
        target = out_ref.at[:, pl.ds(part * rows, rows), :]
        copies.append(pltpu.make_async_copy(held.at[part], target, sems.at[part]))
        copies[-1].start()
    for copy in copies:
        copy.wait()


def call(kernel, out_shape, args, scratch=(), limit=LIMIT, far=(), far_out=False, flops=0, trans=0):
    many = isinstance(out_shape, (list, tuple))
    moved = sum(a.size * a.dtype.itemsize for a in args)
    moved += sum(o.size * o.dtype.itemsize for o in (out_shape if many else [out_shape]))
    anywhere = pl.BlockSpec(memory_space=pl.ANY)
    return pl.pallas_call(
        kernel,
        out_shape=out_shape,
        in_specs=[
            anywhere if i in far else VMEM
            for i in range(len(args))
        ],
        out_specs=[VMEM] * len(out_shape) if many else anywhere if far_out else VMEM,
        scratch_shapes=scratch,
        compiler_params=pltpu.CompilerParams(vmem_limit_bytes=limit),
        cost_estimate=pl.CostEstimate(flops=flops, bytes_accessed=moved, transcendentals=trans),
    )(*args)


def by_columns(tracers, fluxes, weight_in, weight_out):
    spec, depth, width, width_y = tracers.shape
    count, tiles = lax.axis_size("species"), lax.axis_size("tile")
    spec_all, hid = spec * count, weight_in.shape[0]
    f32, bf16 = jnp.float32, jnp.bfloat16
    shape = jax.ShapeDtypeStruct

    chain = []
    for t in range(tiles):
        for place in range(count):
            s = place if t % 2 == 0 else count - 1 - place
            chain.append(s * tiles + t)
    swap_a, swap_b = [], []
    for i in range(len(chain) - 1):
        (swap_a if i % 2 == 0 else swap_b).extend(
            [(chain[i], chain[i + 1]), (chain[i + 1], chain[i])]
        )

    w_in = weight_in * jnp.asarray(0.5, bf16)
    w_out = weight_out * jnp.asarray(0.5, bf16)

    def exchange(pieces):
        got = list(pieces)
        for d in [*range(2, count), 1]:
            got[d] = lax.ppermute(pieces[d], "species", [(s, s ^ d) for s in range(count)])
        return got

    piece = shape((2 * depth + 6, spec, width_y), bf16)
    held = pltpu.VMEM((PARTS, spec, depth * width // PARTS, width_y), f32)
    flux_rows = fluxes.reshape(-1, width_y)
    packed = call(
        functools.partial(pack_kernel, count),
        [piece] * count,
        (tracers.reshape(spec, depth * width, width_y), flux_rows),
        scratch=[
            held,
            pltpu.VMEM(flux_rows.shape, f32),
            pltpu.SemaphoreType.DMA((PARTS + 1,)),
        ],
        limit=FULL,
        far=(0, 1),
    )
    got = exchange(packed)
    row = shape((depth, spec_all, width_y), f32)
    sent = shape((count, depth, spec, width_y), bf16)
    b, a, send_b, send_a, flux = call(
        functools.partial(unpack_kernel, depth),
        [
            row,
            row,
            shape((count, depth + 4, spec, width_y), bf16),
            shape((count, depth + 1, spec, width_y), bf16),
            shape((STEPS, 6, count, depth // count, width_y), f32),
        ],
        got,
        scratch=[pltpu.VMEM(piece.shape, bf16), pltpu.SemaphoreType.DMA],
        far=(0,),
    )
    halo_a = from_a = lax.ppermute(send_a, AXES, swap_a)
    halo_b = from_b = lax.ppermute(send_b, AXES, swap_b)
    halo_c = lax.ppermute(send_a, AXES, swap_b)
    common = [
        pltpu.VMEM((7, depth, width_y), f32),
        pltpu.VMEM(row.shape, f32),
        pltpu.VMEM((2, spec_all, GROUP * width_y), bf16),
    ]

    def column(t, kind, own, inner, outer, sends=True, more=()):
        scratch = list(common)
        if t < STEPS - 1:
            outs = [sent, row] if sends else [row]
        elif kind == "A":
            outs = [shape((2, depth, spec, width_y), bf16)] * count
            scratch = [pltpu.VMEM(sent.shape, bf16), *common]
        else:
            outs = [sent]
        return call(
            functools.partial(column_kernel, t, kind, GROUP, sends),
            outs,
            (own, inner, outer, flux, from_a, from_b, w_in, w_out, *more),
            scratch=scratch,
            flops=4 * depth * width_y * spec_all * hid,
            trans=depth * width_y * hid,
        )

    for t in range(0, STEPS, 2):
        send_a, new_a = column(t, "A", a, b, halo_a)
        halo_a = lax.ppermute(send_a, AXES, swap_a)
        (new_b,) = column(t, "B", b, a, halo_b, sends=False)
        (ghost,) = column(t, "G", halo_b, b, halo_c, sends=False)
        a, b = new_a, new_b
        made_b = column(t + 1, "B", b, a, ghost)
        if t + 1 == STEPS - 1:
            pieces = column(t + 1, "A", a, b, halo_a, more=made_b)
            break
        halo_b = lax.ppermute(made_b[0], AXES, swap_b)
        send_a, new_a = column(t + 1, "A", a, b, halo_a)
        halo_a = lax.ppermute(send_a, AXES, swap_a)
        halo_c = lax.ppermute(send_a, AXES, swap_b)
        a, b = new_a, made_b[1]
    out = call(
        finish_kernel,
        shape((spec, depth * width, width_y), f32),
        exchange(pieces),
        scratch=[held, pltpu.SemaphoreType.DMA((PARTS,))],
        far_out=True,
    )
    return out.reshape(tracers.shape)


def per_device(tracers, fluxes, weight_in, weight_out):
    spec, depth, width, width_y = tracers.shape
    count = lax.axis_size("species")
    fits = (
        width == 2 * count
        and count % 2 == 0
        and STEPS % 2 == 0
        and count & (count - 1) == 0
        and depth % count == 0
        and depth % GROUP == 0
        and depth % PARTS == 0
        and spec == PACK
        and width_y % 128 == 0
        and width % 8 == 0
        and STEPS * (depth // count) == PACK
    )
    chosen = by_columns if fits else by_levels
    return chosen(tracers, fluxes, weight_in, weight_out)


def solution(mesh):
    placed = (P("species", None, "tile", None), P(None, None, "species", "tile", None), P(), P())
    return jax.shard_map(
        per_device,
        mesh=mesh,
        in_specs=placed,
        out_specs=P("species", None, "tile", None),
        check_vma=False,
    )
```

```python
import functools

import jax
import jax.numpy as jnp
from jax import lax
from jax.experimental import pallas as pl
from jax.experimental.pallas import tpu as pltpu
from jax.sharding import PartitionSpec as P

STEPS = 4
AXES = ("species", "tile")
PACK = 16
GROUP = 4
PARTS = 4
VMEM = pl.BlockSpec(memory_space=pltpu.VMEM)
LIMIT = 24 * 1024 * 1024
FULL = 56 * 1024 * 1024


def positive(value):
    return jnp.maximum(value, 0.0)


def negative(value):
    return jnp.minimum(value, 0.0)


def extended(cells, sides, width):
    for axis, dim in sides:
        count = lax.axis_size(axis)
        ends = count - 1
        head = lax.slice_in_dim(cells, 0, width, axis=dim)
        tail = lax.slice_in_dim(cells, cells.shape[dim] - width, cells.shape[dim], axis=dim)
        cells = jnp.concatenate(
            [
                lax.ppermute(tail, axis, [(i, (i + 1) % count) for i in range(ends)]),
                cells,
                lax.ppermute(head, axis, [((i + 1) % count, i) for i in range(ends)]),
            ],
            axis=dim,
        )
    return cells


def advance(padded_state, padded_x, flux_y, padded_z):
    inner = padded_state[:, 1:-1, 1:-1]
    along_x = padded_state[:, 1:-1]
    face_x = padded_x[:, 1:]
    faces_x = positive(face_x) * along_x[:, :, :-1] + negative(face_x) * along_x[:, :, 1:]
    along_z = padded_state[:, :, 1:-1]
    face_z = padded_z[1:]
    faces_z = positive(face_z) * along_z[:, :-1] + negative(face_z) * along_z[:, 1:]
    faces_y = positive(flux_y) * jnp.roll(inner, 1, 3) + negative(flux_y) * inner
    return (
        inner
        + faces_x[:, :, :-1]
        - faces_x[:, :, 1:]
        + faces_y
        - jnp.roll(faces_y, -1, 3)
        + faces_z[:, :-1]
        - faces_z[:, 1:]
    )


def by_levels(tracers, fluxes, weight_in, weight_out):
    spec_loc, depth_all, width_x, width_y = tracers.shape
    tile_at = lax.axis_index("tile")
    state = lax.all_to_all(tracers, "species", split_axis=1, concat_axis=0, tiled=True)
    spec_all, lev_loc = (state.shape[0], state.shape[1])
    grid_shape = (lev_loc, width_x, width_y)
    column = tile_at * width_x + lax.broadcasted_iota(jnp.int32, grid_shape, 1)
    level_at = lax.axis_index("species") * lev_loc + lax.broadcasted_iota(jnp.int32, grid_shape, 0)
    for interval in range(STEPS):
        own_flux = fluxes[interval]
        flux_x = jnp.where(column == 0, 0.0, own_flux[0])
        flux_y = own_flux[1]
        flux_z = jnp.where(level_at == 0, 0.0, own_flux[2])
        stacked = jnp.concatenate([state, flux_x[None], flux_z[None]], 0)
        padded = extended(stacked, (("species", 1), ("tile", 2)), 1)
        padded_state = padded[:spec_all]
        padded_x = padded[spec_all, 1:-1]
        padded_z = padded[spec_all + 1, :, 1:-1]
        state = advance(padded_state, padded_x, flux_y, padded_z)
        flattened = state.astype(jnp.bfloat16).reshape(spec_all, lev_loc, width_x * width_y)
        hidden = jax.nn.silu(
            jnp.einsum("hs,szc->hzc", weight_in, flattened, preferred_element_type=jnp.float32)
        ).astype(jnp.bfloat16)
        tendency = (
            0.5 * jnp.einsum("sh,hzc->szc", weight_out, hidden, preferred_element_type=jnp.float32)
        ).astype(jnp.bfloat16)
        state = state + tendency.reshape(state.shape).astype(jnp.float32)
    return lax.all_to_all(state, "species", split_axis=0, concat_axis=1, tiled=True)


def place_and_species(count):
    species = lax.axis_index("species")
    return jnp.where(lax.rem(lax.axis_index("tile"), 2) == 1, count - 1 - species, species), species


def columns_of(place):
    odd = lax.rem(place, 2)
    return 2 * place + odd, 2 * place + 1 - odd


def pack_kernel(count, tracers_ref, fluxes_ref, *refs):
    out_refs, (held, flux_ref, sems) = refs[:count], refs[count:]
    parts, spec, rows, width_y = held.shape
    width = 2 * count
    lev = rows // width
    depth = parts * lev
    lev_own = fluxes_ref.shape[0] // (STEPS * 3 * width)
    own, _ = place_and_species(count)
    outer = lax.axis_index("tile") == 0
    copies = []
    for part in range(parts):
        source = tracers_ref.at[:, pl.ds(part * rows, rows), :]
        copies.append(pltpu.make_async_copy(source, held.at[part], sems.at[part]))
    copies.append(pltpu.make_async_copy(fluxes_ref, flux_ref, sems.at[parts]))
    for copy in copies:
        copy.start()

    columns = [columns_of(own ^ d) for d in range(count)]
    for part in range(parts):
        copies[part].wait()
        flat = held.at[part].reshape(spec * rows, width_y)

        def level(k, carry):
            for d in range(count):
                for base, x in zip((depth + 4, 0), columns[d]):
                    cells = flat[pl.ds(k * width + x, spec, stride=rows), :]
                    out_refs[d][base + part * lev + k] = cells.astype(jnp.bfloat16)
            return carry

        lax.fori_loop(0, lev, level, 0)

    copies[parts].wait()
    for d in range(count):
        b_at, a_at = columns[d]
        low = jnp.minimum(b_at, a_at)

        def tile_of(direction, x):
            return jnp.concatenate(
                [
                    flux_ref[pl.ds((t * 3 + direction) * lev_own * width + x, lev_own, stride=width), :]
                    for t in range(STEPS)
                ],
                0,
            )

        first = jnp.where(jnp.logical_and(outer, low == 0), 0.0, tile_of(0, low))
        out_refs[d][depth] = first.astype(jnp.bfloat16)
        others = ((0, low + 1, 1), (1, b_at, 2), (2, b_at, 3), (1, a_at, depth + 4), (2, a_at, depth + 5))
        for direction, x, to in others:
            out_refs[d][depth + to] = tile_of(direction, x).astype(jnp.bfloat16)


def unpack_kernel(depth, *refs):
    count = len(refs) - 7
    got, refs = refs[:count], refs[count:]
    b_ref, a_ref, msg_b_ref, msg_a_ref, flux_ref, kept, sem = refs
    copy = pltpu.make_async_copy(got[0], kept, sem)
    copy.start()
    got = [kept, *got[1:]]
    lev = depth // count
    spec = got[0].shape[1]
    _, species = place_and_species(count)

    def level(d, k, carry):
        rows = pl.ds(pl.multiple_of((species ^ d) * spec, spec), spec)
        for base, state_ref, msg_ref in ((depth + 4, b_ref, msg_b_ref), (0, a_ref, msg_a_ref)):
            cells = got[d][base + k]
            state_ref[k, rows] = cells.astype(jnp.float32)
            msg_ref[species ^ d, k] = cells
        return carry

    for d in [*range(1, count), 0]:
        if d == 0:
            copy.wait()
        lax.fori_loop(0, depth, functools.partial(level, d), 0, unroll=4)
        source = species ^ d
        msg_a_ref[source, depth] = got[d][depth]
        for i in range(4):
            msg_b_ref[source, depth + i] = got[d][depth + i]
        for i in range(6):
            part = got[d][depth + i if i < 4 else 2 * depth + i].astype(jnp.float32)
            for t in range(STEPS):
                flux_ref[t, i, source] = part[t * lev : (t + 1) * lev]


def column_kernel(
    t, kind, group, sends, own_ref, inner_ref, outer_ref, flux_ref, from_ref, w_in_ref, w_out_ref, *rest
):
    last = t == STEPS - 1
    coef, moved_ref, cells_ref, half_ref = rest[-4:]
    count, spec, lev = from_ref.shape[0], from_ref.shape[2], flux_ref.shape[3]
    depth, spec_all, width_y = inner_ref.shape
    place, species = place_and_species(count)
    rest = list(rest)
    sent_b_ref = rest.pop(0) if last and kind == "A" else None
    outs = rest[:count] if last and kind == "A" else None
    send_ref = rest[count] if outs else rest.pop(0) if sends else None
    new_ref = None if last else rest.pop(0)

    def cells_of(ref, k):
        if ref.shape == inner_ref.shape:
            return ref[k]
        return jnp.concatenate([ref[s, k].astype(jnp.float32) for s in range(count)], 0)

    def mine(index):
        return jnp.concatenate([flux_ref[t, index, s] for s in range(count)], 0)

    def theirs(index):
        parts = [from_ref[s, depth + index].astype(jnp.float32) for s in range(count)]
        return jnp.concatenate([p[t * lev : (t + 1) * lev] for p in parts], 0)

    even = lax.rem(place, 2) == 0
    if kind == "A":
        outer_high = even
        fx = jnp.where(even, mine(1), mine(0))
        fx_hi = jnp.where(even, theirs(0), mine(1))
        fy, fz = mine(4), mine(5)
    elif kind == "B":
        outer_high = jnp.logical_not(even)
        fx = jnp.where(even, mine(0), mine(1))
        fx_hi = jnp.where(even, mine(1), theirs(0))
        fy, fz = mine(2), mine(3)
    else:
        outer_high = jnp.logical_not(even)
        fx = jnp.where(even, theirs(1), theirs(0))
        fx_hi = jnp.where(even, mine(0), theirs(1))
        fy, fz = theirs(2), theirs(3)
    fy_hi = pltpu.roll(fy, width_y - 1, 1)
    fz = jnp.where(lax.broadcasted_iota(jnp.int32, fz.shape, 0) == 0, 0.0, fz)
    fz_hi = jnp.concatenate([fz[1:], jnp.zeros_like(fz[:1])], 0)
    low, high = positive(fx), -negative(fx_hi)
    coef[0] = (
        1.0
        + (negative(fx) - positive(fx_hi))
        + (negative(fy) - positive(fy_hi))
        + (negative(fz) - positive(fz_hi))
    )
    coef[1] = jnp.where(outer_high, high, low)
    coef[2] = jnp.where(outer_high, low, high)
    coef[3] = positive(fy)
    coef[4] = -negative(fy_hi)
    coef[5] = positive(fz)
    coef[6] = -negative(fz_hi)

    def level(k, column):
        own = cells_of(own_ref, k)
        out = coef[0, pl.ds(k, 1)] * own
        out += coef[1, pl.ds(k, 1)] * cells_of(outer_ref, k)
        out += coef[2, pl.ds(k, 1)] * inner_ref[k]
        out += coef[3, pl.ds(k, 1)] * pltpu.roll(own, 1, 1)
        out += coef[4, pl.ds(k, 1)] * pltpu.roll(own, width_y - 1, 1)
        out += coef[5, pl.ds(k, 1)] * cells_of(own_ref, jnp.maximum(k - 1, 0))
        out += coef[6, pl.ds(k, 1)] * cells_of(own_ref, jnp.minimum(k + 1, depth - 1))
        moved_ref[k] = out
        cells_ref[:, column * width_y : (column + 1) * width_y] = out.astype(jnp.bfloat16)

    groups = depth // group
    hid = w_in_ref.shape[0]
    piece = hid // 2
    wide = 2 * width_y

    def first_matmul(slot, i, j):
        half_ref[slot, i * piece : (i + 1) * piece, j * wide : (j + 1) * wide] = jnp.dot(
            w_in_ref[i * piece : (i + 1) * piece, :],
            cells_ref[:, j * wide : (j + 1) * wide],
            preferred_element_type=jnp.float32,
        )

    def body(g, carry):
        slot = lax.rem(g, 2)
        ahead = jnp.minimum(g + 1, groups - 1)
        for i in range(group):
            level(ahead * group + i, i)
        for j in range(group * width_y // wide):
            change = 0.0
            for i in range(2):
                first_matmul(1 - slot, i, j)
                half = half_ref[slot, i * piece : (i + 1) * piece, j * wide : (j + 1) * wide]
                hidden = (half + half * jnp.tanh(half)).astype(jnp.bfloat16)
                change += jnp.dot(
                    w_out_ref[:, i * piece : (i + 1) * piece], hidden, preferred_element_type=jnp.float32
                )
            for i in range(2):
                k = g * group + 2 * j + i
                new = moved_ref[k] + change[:, i * width_y : (i + 1) * width_y]
                if new_ref is not None:
                    new_ref[k] = new
                if send_ref is not None:
                    for s in range(count):
                        send_ref[s, k] = new[s * spec : (s + 1) * spec].astype(jnp.bfloat16)
        return carry

    for i in range(group):
        level(i, i)
    for j in range(group * width_y // wide):
        for i in range(2):
            first_matmul(0, i, j)
    lax.fori_loop(0, groups, body, 0)
    if outs is not None:
        for d in range(count):
            outs[d][0] = sent_b_ref[species ^ d]
            outs[d][1] = send_ref[species ^ d]


def finish_kernel(*refs):
    out_ref, held, sems = refs[-3:]
    count, spec = len(refs) - 3, refs[0].shape[2]
    parts, _, rows, width_y = held.shape
    width = 2 * count
    lev = rows // width
    own, _ = place_and_species(count)
    columns = [columns_of(own ^ d) for d in range(count)]
    copies = []
    for part in range(parts):
        flat = held.at[part].reshape(spec * rows, width_y)

        def level(k, carry):
            for d in range(count):
                for side, x in enumerate(columns[d]):
                    cells = refs[d][side, part * lev + k].astype(jnp.float32)
                    flat[pl.ds(k * width + x, spec, stride=rows), :] = cells
            return carry

        lax.fori_loop(0, lev, level, 0)
        target = out_ref.at[:, pl.ds(part * rows, rows), :]
        copies.append(pltpu.make_async_copy(held.at[part], target, sems.at[part]))
        copies[-1].start()
    for copy in copies:
        copy.wait()


def call(kernel, out_shape, args, scratch=(), limit=LIMIT, far=(), far_out=False):
    many = isinstance(out_shape, (list, tuple))
    anywhere = pl.BlockSpec(memory_space=pl.ANY)
    return pl.pallas_call(
        kernel,
        out_shape=out_shape,
        in_specs=[
            anywhere if i in far else VMEM
            for i in range(len(args))
        ],
        out_specs=[VMEM] * len(out_shape) if many else anywhere if far_out else VMEM,
        scratch_shapes=scratch,
        compiler_params=pltpu.CompilerParams(vmem_limit_bytes=limit),
        cost_estimate=pl.CostEstimate(flops=1024, bytes_accessed=1024, transcendentals=0),
    )(*args)


def by_columns(tracers, fluxes, weight_in, weight_out):
    spec, depth, width, width_y = tracers.shape
    count, tiles = lax.axis_size("species"), lax.axis_size("tile")
    spec_all = spec * count
    f32, bf16 = jnp.float32, jnp.bfloat16
    shape = jax.ShapeDtypeStruct

    chain = []
    for t in range(tiles):
        for place in range(count):
            s = place if t % 2 == 0 else count - 1 - place
            chain.append(s * tiles + t)
    swap_a, swap_b = [], []
    for i in range(len(chain) - 1):
        (swap_a if i % 2 == 0 else swap_b).extend(
            [(chain[i], chain[i + 1]), (chain[i + 1], chain[i])]
        )

    w_in = weight_in * jnp.asarray(0.5, bf16)
    w_out = weight_out * jnp.asarray(0.5, bf16)

    def exchange(pieces):
        got = list(pieces)
        for d in [*range(2, count), 1]:
            got[d] = lax.ppermute(pieces[d], "species", [(s, s ^ d) for s in range(count)])
        return got

    piece = shape((2 * depth + 6, spec, width_y), bf16)
    held = pltpu.VMEM((PARTS, spec, depth * width // PARTS, width_y), f32)
    flux_rows = fluxes.reshape(-1, width_y)
    packed = call(
        functools.partial(pack_kernel, count),
        [piece] * count,
        (tracers.reshape(spec, depth * width, width_y), flux_rows),
        scratch=[
            held,
            pltpu.VMEM(flux_rows.shape, f32),
            pltpu.SemaphoreType.DMA((PARTS + 1,)),
        ],
        limit=FULL,
        far=(0, 1),
    )
    got = exchange(packed)
    row = shape((depth, spec_all, width_y), f32)
    sent = shape((count, depth, spec, width_y), bf16)
    b, a, send_b, send_a, flux = call(
        functools.partial(unpack_kernel, depth),
        [
            row,
            row,
            shape((count, depth + 4, spec, width_y), bf16),
            shape((count, depth + 1, spec, width_y), bf16),
            shape((STEPS, 6, count, depth // count, width_y), f32),
        ],
        got,
        scratch=[pltpu.VMEM(piece.shape, bf16), pltpu.SemaphoreType.DMA],
        far=(0,),
    )
    halo_a = from_a = lax.ppermute(send_a, AXES, swap_a)
    halo_b = from_b = lax.ppermute(send_b, AXES, swap_b)
    halo_c = lax.ppermute(send_a, AXES, swap_b)
    common = [
        pltpu.VMEM((7, depth, width_y), f32),
        pltpu.VMEM(row.shape, f32),
        pltpu.VMEM((spec_all, GROUP * width_y), bf16),
        pltpu.VMEM((2, weight_in.shape[0], GROUP * width_y), f32),
    ]

    def column(t, kind, own, inner, outer, sends=True, more=()):
        scratch = list(common)
        if t < STEPS - 1:
            outs = [sent, row] if sends else [row]
        elif kind == "A":
            outs = [shape((2, depth, spec, width_y), bf16)] * count
            scratch = [pltpu.VMEM(sent.shape, bf16), *common]
        else:
            outs = [sent]
        return call(
            functools.partial(column_kernel, t, kind, GROUP, sends),
            outs,
            (own, inner, outer, flux, from_a if kind == "A" else from_b, w_in, w_out, *more),
            scratch=scratch,
        )

    for t in range(0, STEPS, 2):
        send_a, new_a = column(t, "A", a, b, halo_a)
        halo_a = lax.ppermute(send_a, AXES, swap_a)
        (new_b,) = column(t, "B", b, a, halo_b, sends=False)
        (ghost,) = column(t, "G", halo_b, b, halo_c, sends=False)
        a, b = new_a, new_b
        made_b = column(t + 1, "B", b, a, ghost)
        if t + 1 == STEPS - 1:
            pieces = column(t + 1, "A", a, b, halo_a, more=made_b)
            break
        halo_b = lax.ppermute(made_b[0], AXES, swap_b)
        send_a, new_a = column(t + 1, "A", a, b, halo_a)
        halo_a = lax.ppermute(send_a, AXES, swap_a)
        halo_c = lax.ppermute(send_a, AXES, swap_b)
        a, b = new_a, made_b[1]
    out = call(
        finish_kernel,
        shape((spec, depth * width, width_y), f32),
        exchange(pieces),
        scratch=[held, pltpu.SemaphoreType.DMA((PARTS,))],
        far_out=True,
    )
    return out.reshape(tracers.shape)


def per_device(tracers, fluxes, weight_in, weight_out):
    spec, depth, width, width_y = tracers.shape
    count = lax.axis_size("species")
    fits = (
        width == 2 * count
        and count % 2 == 0
        and STEPS % 2 == 0
        and count & (count - 1) == 0
        and depth % count == 0
        and depth % GROUP == 0
        and depth % PARTS == 0
        and spec == PACK
        and width_y % 128 == 0
        and width % 8 == 0
        and STEPS * (depth // count) == PACK
    )
    chosen = by_columns if fits else by_levels
    return chosen(tracers, fluxes, weight_in, weight_out)


def solution(mesh):
    placed = (P("species", None, "tile", None), P(None, None, "species", "tile", None), P(), P())
    return jax.shard_map(
        per_device,
        mesh=mesh,
        in_specs=placed,
        out_specs=P("species", None, "tile", None),
        check_vma=False,
    )
```

```python
import functools

import jax
import jax.numpy as jnp
from jax import lax
from jax.experimental import pallas as pl
from jax.experimental.pallas import tpu as pltpu
from jax.sharding import PartitionSpec as P

STEPS = 4
AXES = ("species", "tile")
PACK = 16
GROUP = 4
PARTS = 4
VMEM = pl.BlockSpec(memory_space=pltpu.VMEM)
LIMIT = 24 * 1024 * 1024


def positive(value):
    return jnp.maximum(value, 0.0)


def negative(value):
    return jnp.minimum(value, 0.0)


def extended(cells, sides, width):
    for axis, dim in sides:
        count = lax.axis_size(axis)
        ends = count - 1
        head = lax.slice_in_dim(cells, 0, width, axis=dim)
        tail = lax.slice_in_dim(cells, cells.shape[dim] - width, cells.shape[dim], axis=dim)
        cells = jnp.concatenate(
            [
                lax.ppermute(tail, axis, [(i, (i + 1) % count) for i in range(ends)]),
                cells,
                lax.ppermute(head, axis, [((i + 1) % count, i) for i in range(ends)]),
            ],
            axis=dim,
        )
    return cells


def advance(padded_state, padded_x, flux_y, padded_z):
    inner = padded_state[:, 1:-1, 1:-1]
    along_x = padded_state[:, 1:-1]
    face_x = padded_x[:, 1:]
    faces_x = positive(face_x) * along_x[:, :, :-1] + negative(face_x) * along_x[:, :, 1:]
    along_z = padded_state[:, :, 1:-1]
    face_z = padded_z[1:]
    faces_z = positive(face_z) * along_z[:, :-1] + negative(face_z) * along_z[:, 1:]
    faces_y = positive(flux_y) * jnp.roll(inner, 1, 3) + negative(flux_y) * inner
    return (
        inner
        + faces_x[:, :, :-1]
        - faces_x[:, :, 1:]
        + faces_y
        - jnp.roll(faces_y, -1, 3)
        + faces_z[:, :-1]
        - faces_z[:, 1:]
    )


def by_levels(tracers, fluxes, weight_in, weight_out):
    spec_loc, depth_all, width_x, width_y = tracers.shape
    tile_at = lax.axis_index("tile")
    state = lax.all_to_all(tracers, "species", split_axis=1, concat_axis=0, tiled=True)
    spec_all, lev_loc = (state.shape[0], state.shape[1])
    grid_shape = (lev_loc, width_x, width_y)
    column = tile_at * width_x + lax.broadcasted_iota(jnp.int32, grid_shape, 1)
    level_at = lax.axis_index("species") * lev_loc + lax.broadcasted_iota(jnp.int32, grid_shape, 0)
    for interval in range(STEPS):
        own_flux = fluxes[interval]
        flux_x = jnp.where(column == 0, 0.0, own_flux[0])
        flux_y = own_flux[1]
        flux_z = jnp.where(level_at == 0, 0.0, own_flux[2])
        stacked = jnp.concatenate([state, flux_x[None], flux_z[None]], 0)
        padded = extended(stacked, (("species", 1), ("tile", 2)), 1)
        padded_state = padded[:spec_all]
        padded_x = padded[spec_all, 1:-1]
        padded_z = padded[spec_all + 1, :, 1:-1]
        state = advance(padded_state, padded_x, flux_y, padded_z)
        flattened = state.astype(jnp.bfloat16).reshape(spec_all, lev_loc, width_x * width_y)
        hidden = jax.nn.silu(
            jnp.einsum("hs,szc->hzc", weight_in, flattened, preferred_element_type=jnp.float32)
        ).astype(jnp.bfloat16)
        tendency = (
            0.5 * jnp.einsum("sh,hzc->szc", weight_out, hidden, preferred_element_type=jnp.float32)
        ).astype(jnp.bfloat16)
        state = state + tendency.reshape(state.shape).astype(jnp.float32)
    return lax.all_to_all(state, "species", split_axis=0, concat_axis=1, tiled=True)


def place_and_species(count):
    species = lax.axis_index("species")
    return jnp.where(lax.rem(lax.axis_index("tile"), 2) == 1, count - 1 - species, species), species


def columns_of(place):
    odd = lax.rem(place, 2)
    return 2 * place + odd, 2 * place + 1 - odd


def pack_kernel(count, depth, kind, *refs):
    tracers_ref, out_refs = refs[0], refs[-count:]
    width = 2 * count
    spec = tracers_ref.shape[0] // (depth * width)
    lev = depth // count
    own, _ = place_and_species(count)
    columns = [columns_of(own ^ d) for d in range(count)]

    def level(k, carry):
        for d in range(count):
            x = columns[d][0 if kind == "B" else 1]
            cells = tracers_ref[pl.ds(k * width + x, spec, stride=depth * width), :]
            out_refs[d][k] = cells.astype(jnp.bfloat16)
        return carry

    lax.fori_loop(0, depth, level, 0, unroll=2)
    if kind == "A":
        return
    flux_ref = refs[1]
    outer = lax.axis_index("tile") == 0
    for d in range(count):
        b_at, a_at = columns[d]
        low = jnp.minimum(b_at, a_at)

        def tile_of(direction, x):
            return jnp.concatenate(
                [
                    flux_ref[pl.ds((t * 3 + direction) * lev * width + x, lev, stride=width), :]
                    for t in range(STEPS)
                ],
                0,
            )

        first = jnp.where(jnp.logical_and(outer, low == 0), 0.0, tile_of(0, low))
        out_refs[d][depth] = first.astype(jnp.bfloat16)
        others = ((0, low + 1), (1, b_at), (2, b_at), (1, a_at), (2, a_at))
        for i, (direction, x) in enumerate(others):
            out_refs[d][depth + 1 + i] = tile_of(direction, x).astype(jnp.bfloat16)


def unpack_kernel(count, depth, kind, *refs):
    got, (state_ref, msg_ref) = refs[:count], refs[-2 if kind == "A" else -4 :][:2]
    lev = depth // count
    spec = got[0].shape[1]
    _, species = place_and_species(count)

    if kind == "B":
        flux_ref, near_ref = refs[-2:]
        near_ref[...] = refs[count][...]

    def level(d, k, carry):
        rows = pl.ds(pl.multiple_of((species ^ d) * spec, spec), spec)
        cells = got[d][k]
        state_ref[k, rows] = cells.astype(jnp.float32)
        msg_ref[species ^ d, k] = cells
        return carry

    for d in range(count):
        lax.fori_loop(0, depth, functools.partial(level, d), 0, unroll=4)
        source = species ^ d
        if kind == "A":
            msg_ref[source, depth] = refs[count + d][depth]
            continue
        for i in range(4):
            msg_ref[source, depth + i] = got[d][depth + i]
        for i in range(6):
            part = got[d][depth + i].astype(jnp.float32)
            for t in range(STEPS):
                flux_ref[t, i, source] = part[t * lev : (t + 1) * lev]


def column_kernel(
    t, kind, group, sends, own_ref, inner_ref, outer_ref, flux_ref, from_ref, w_in_ref, w_out_ref, *rest
):
    last = t == STEPS - 1
    coef, moved_ref, cells_ref = rest[-3:]
    count, spec, lev = from_ref.shape[0], from_ref.shape[2], flux_ref.shape[3]
    depth, spec_all, width_y = inner_ref.shape
    place, species = place_and_species(count)
    rest = list(rest)
    outs = rest[:count] if last else None
    send_ref = rest[count] if outs else rest.pop(0) if sends else None
    new_ref = None if last else rest.pop(0)

    def cells_of(ref, k):
        if ref.shape == inner_ref.shape:
            return ref[k]
        return jnp.concatenate([ref[s, k].astype(jnp.float32) for s in range(count)], 0)

    def mine(index):
        return jnp.concatenate([flux_ref[t, index, s] for s in range(count)], 0)

    def theirs(index):
        parts = [from_ref[s, depth + index].astype(jnp.float32) for s in range(count)]
        return jnp.concatenate([p[t * lev : (t + 1) * lev] for p in parts], 0)

    even = lax.rem(place, 2) == 0
    if kind == "A":
        outer_high = even
        fx = jnp.where(even, mine(1), mine(0))
        fx_hi = jnp.where(even, theirs(0), mine(1))
        fy, fz = mine(4), mine(5)
    elif kind == "B":
        outer_high = jnp.logical_not(even)
        fx = jnp.where(even, mine(0), mine(1))
        fx_hi = jnp.where(even, mine(1), theirs(0))
        fy, fz = mine(2), mine(3)
    else:
        outer_high = jnp.logical_not(even)
        fx = jnp.where(even, theirs(1), theirs(0))
        fx_hi = jnp.where(even, mine(0), theirs(1))
        fy, fz = theirs(2), theirs(3)
    fy_hi = pltpu.roll(fy, width_y - 1, 1)
    fz = jnp.where(lax.broadcasted_iota(jnp.int32, fz.shape, 0) == 0, 0.0, fz)
    fz_hi = jnp.concatenate([fz[1:], jnp.zeros_like(fz[:1])], 0)
    low, high = positive(fx), -negative(fx_hi)
    coef[0] = (
        1.0
        + (negative(fx) - positive(fx_hi))
        + (negative(fy) - positive(fy_hi))
        + (negative(fz) - positive(fz_hi))
    )
    coef[1] = jnp.where(outer_high, high, low)
    coef[2] = jnp.where(outer_high, low, high)
    coef[3] = positive(fy)
    coef[4] = -negative(fy_hi)
    coef[5] = positive(fz)
    coef[6] = -negative(fz_hi)
    w_in = w_in_ref[...]
    w_out = w_out_ref[...]

    def level(k, slot, column):
        own = cells_of(own_ref, k)
        out = coef[0, pl.ds(k, 1)] * own
        out += coef[1, pl.ds(k, 1)] * cells_of(outer_ref, k)
        out += coef[2, pl.ds(k, 1)] * inner_ref[k]
        out += coef[3, pl.ds(k, 1)] * pltpu.roll(own, 1, 1)
        out += coef[4, pl.ds(k, 1)] * pltpu.roll(own, width_y - 1, 1)
        out += coef[5, pl.ds(k, 1)] * cells_of(own_ref, jnp.maximum(k - 1, 0))
        out += coef[6, pl.ds(k, 1)] * cells_of(own_ref, jnp.minimum(k + 1, depth - 1))
        moved_ref[k] = out
        cells_ref[slot, :, column * width_y : (column + 1) * width_y] = out.astype(jnp.bfloat16)

    groups = depth // group

    def body(g, carry):
        slot = lax.rem(g, 2)
        half = jnp.dot(w_in, cells_ref[slot], preferred_element_type=jnp.float32)
        ahead = jnp.minimum(g + 1, groups - 1)
        for i in range(group):
            level(ahead * group + i, 1 - slot, i)
        hidden = (half + half * jnp.tanh(half)).astype(jnp.bfloat16)
        change = jnp.dot(w_out, hidden, preferred_element_type=jnp.float32)
        for i in range(group):
            k = g * group + i
            new = moved_ref[k] + change[:, i * width_y : (i + 1) * width_y]
            if new_ref is not None:
                new_ref[k] = new
            if send_ref is not None:
                for s in range(count):
                    send_ref[s, k] = new[s * spec : (s + 1) * spec].astype(jnp.bfloat16)
        return carry

    for i in range(group):
        level(i, 0, i)
    lax.fori_loop(0, groups, body, 0)
    if outs is not None:
        for d in range(count):
            outs[d][...] = send_ref[species ^ d]


def finish_kernel(count, *refs):
    pieces, (out_ref, held, sems) = refs[: 2 * count], refs[2 * count :]
    parts, spec, rows, width_y = held.shape
    width = 2 * count
    lev = rows // width
    own, _ = place_and_species(count)
    columns = [columns_of(own ^ d) for d in range(count)]
    copies = []
    for part in range(parts):
        flat = held.at[part].reshape(spec * rows, width_y)

        def level(k, carry):
            for d in range(count):
                for side, x in enumerate(columns[d]):
                    cells = pieces[side * count + d][part * lev + k].astype(jnp.float32)
                    flat[pl.ds(k * width + x, spec, stride=rows), :] = cells
            return carry

        lax.fori_loop(0, lev, level, 0)
        target = out_ref.at[:, pl.ds(part * rows, rows), :]
        copies.append(pltpu.make_async_copy(held.at[part], target, sems.at[part]))
        copies[-1].start()
    for copy in copies:
        copy.wait()


def call(kernel, out_shape, args, scratch=(), far_out=False):
    many = isinstance(out_shape, (list, tuple))
    anywhere = pl.BlockSpec(memory_space=pl.ANY)
    return pl.pallas_call(
        kernel,
        out_shape=out_shape,
        in_specs=[VMEM] * len(args),
        out_specs=[VMEM] * len(out_shape) if many else anywhere if far_out else VMEM,
        scratch_shapes=scratch,
        compiler_params=pltpu.CompilerParams(vmem_limit_bytes=LIMIT),
        cost_estimate=pl.CostEstimate(flops=1024, bytes_accessed=1024, transcendentals=0),
    )(*args)


def by_columns(tracers, fluxes, weight_in, weight_out):
    spec, depth, width, width_y = tracers.shape
    count, tiles = lax.axis_size("species"), lax.axis_size("tile")
    spec_all = spec * count
    f32, bf16 = jnp.float32, jnp.bfloat16
    shape = jax.ShapeDtypeStruct

    chain = []
    for t in range(tiles):
        for place in range(count):
            s = place if t % 2 == 0 else count - 1 - place
            chain.append(s * tiles + t)
    swap_a, swap_b = [], []
    for i in range(len(chain) - 1):
        (swap_a if i % 2 == 0 else swap_b).extend(
            [(chain[i], chain[i + 1]), (chain[i + 1], chain[i])]
        )

    w_in = weight_in * jnp.asarray(0.5, bf16)
    w_out = weight_out * jnp.asarray(0.5, bf16)

    def swapped(piece, d):
        return lax.ppermute(piece, "species", [(s, s ^ d) for s in range(count)])

    def exchange(pieces):
        return [piece if d == 0 else swapped(piece, d) for d, piece in enumerate(pieces)]

    row = shape((depth, spec_all, width_y), f32)
    held = pltpu.VMEM((PARTS, spec, depth * width // PARTS, width_y), f32)
    flat = tracers.reshape(-1, width_y)
    sent = shape((count, depth, spec, width_y), bf16)
    piece = shape((depth, spec, width_y), bf16)
    piece_b = shape((depth + 6, spec, width_y), bf16)
    packed_b = call(
        functools.partial(pack_kernel, count, depth, "B"),
        [piece_b] * count,
        (flat, fluxes.reshape(-1, width_y)),
    )
    got_b = exchange(packed_b)
    packed_a = call(functools.partial(pack_kernel, count, depth, "A"), [piece] * count, (flat, packed_b[0]))
    b, send_b, flux, near_a = call(
        functools.partial(unpack_kernel, count, depth, "B"),
        [
            row,
            shape((count, depth + 4, spec, width_y), bf16),
            shape((STEPS, 6, count, depth // count, width_y), f32),
            piece,
        ],
        (*got_b, packed_a[1]),
    )
    halo_b = from_b = lax.ppermute(send_b, AXES, swap_b)
    got_a = [packed_a[0], swapped(near_a, 1), *(swapped(packed_a[d], d) for d in range(2, count))]
    a, send_a = call(
        functools.partial(unpack_kernel, count, depth, "A"),
        [row, shape((count, depth + 1, spec, width_y), bf16)],
        (*got_a, *got_b, send_b),
    )
    halo_a = from_a = lax.ppermute(send_a, AXES, swap_a)
    halo_c = lax.ppermute(send_a, AXES, swap_b)
    common = [
        pltpu.VMEM((7, depth, width_y), f32),
        pltpu.VMEM(row.shape, f32),
        pltpu.VMEM((2, spec_all, GROUP * width_y), bf16),
    ]

    def column(t, kind, own, inner, outer, sends=True):
        scratch = list(common)
        if t < STEPS - 1:
            outs = [sent, row] if sends else [row]
        else:
            outs = [piece] * count
            scratch = [pltpu.VMEM(sent.shape, bf16), *common]
        return call(
            functools.partial(column_kernel, t, kind, GROUP, sends),
            outs,
            (own, inner, outer, flux, from_a if kind == "A" else from_b, w_in, w_out),
            scratch=scratch,
        )

    for t in range(0, STEPS, 2):
        send_a, new_a = column(t, "A", a, b, halo_a)
        halo_a = lax.ppermute(send_a, AXES, swap_a)
        (new_b,) = column(t, "B", b, a, halo_b, sends=False)
        (ghost,) = column(t, "G", halo_b, b, halo_c, sends=False)
        a, b = new_a, new_b
        made_b = column(t + 1, "B", b, a, ghost)
        if t + 1 == STEPS - 1:
            pieces = [*exchange(made_b), *exchange(column(t + 1, "A", a, b, halo_a))]
            break
        halo_b = lax.ppermute(made_b[0], AXES, swap_b)
        send_a, new_a = column(t + 1, "A", a, b, halo_a)
        halo_a = lax.ppermute(send_a, AXES, swap_a)
        halo_c = lax.ppermute(send_a, AXES, swap_b)
        a, b = new_a, made_b[1]
    out = call(
        functools.partial(finish_kernel, count),
        shape((spec, depth * width, width_y), f32),
        pieces,
        scratch=[held, pltpu.SemaphoreType.DMA((PARTS,))],
        far_out=True,
    )
    return out.reshape(tracers.shape)


def per_device(tracers, fluxes, weight_in, weight_out):
    spec, depth, width, width_y = tracers.shape
    count = lax.axis_size("species")
    fits = (
        width == 2 * count
        and count % 2 == 0
        and STEPS % 2 == 0
        and count & (count - 1) == 0
        and depth % count == 0
        and depth % GROUP == 0
        and depth % PARTS == 0
        and spec == PACK
        and width_y % 128 == 0
        and width % 8 == 0
        and STEPS * (depth // count) == PACK
    )
    chosen = by_columns if fits else by_levels
    return chosen(tracers, fluxes, weight_in, weight_out)


def solution(mesh):
    placed = (P("species", None, "tile", None), P(None, None, "species", "tile", None), P(), P())
    return jax.shard_map(
        per_device,
        mesh=mesh,
        in_specs=placed,
        out_specs=P("species", None, "tile", None),
        check_vma=False,
    )
```

```python
import functools

import jax
import jax.numpy as jnp
from jax import lax
from jax.experimental import pallas as pl
from jax.experimental.pallas import tpu as pltpu
from jax.sharding import PartitionSpec as P

STEPS = 4
AXES = ("species", "tile")
PACK = 16
GROUP = 4
PARTS = 4
VMEM = pl.BlockSpec(memory_space=pltpu.VMEM)
LIMIT = 24 * 1024 * 1024


def positive(value):
    return jnp.maximum(value, 0.0)


def negative(value):
    return jnp.minimum(value, 0.0)


def extended(cells, sides, width):
    for axis, dim in sides:
        count = lax.axis_size(axis)
        ends = count - 1
        head = lax.slice_in_dim(cells, 0, width, axis=dim)
        tail = lax.slice_in_dim(cells, cells.shape[dim] - width, cells.shape[dim], axis=dim)
        cells = jnp.concatenate(
            [
                lax.ppermute(tail, axis, [(i, (i + 1) % count) for i in range(ends)]),
                cells,
                lax.ppermute(head, axis, [((i + 1) % count, i) for i in range(ends)]),
            ],
            axis=dim,
        )
    return cells


def advance(padded_state, padded_x, flux_y, padded_z):
    inner = padded_state[:, 1:-1, 1:-1]
    along_x = padded_state[:, 1:-1]
    face_x = padded_x[:, 1:]
    faces_x = positive(face_x) * along_x[:, :, :-1] + negative(face_x) * along_x[:, :, 1:]
    along_z = padded_state[:, :, 1:-1]
    face_z = padded_z[1:]
    faces_z = positive(face_z) * along_z[:, :-1] + negative(face_z) * along_z[:, 1:]
    faces_y = positive(flux_y) * jnp.roll(inner, 1, 3) + negative(flux_y) * inner
    return (
        inner
        + faces_x[:, :, :-1]
        - faces_x[:, :, 1:]
        + faces_y
        - jnp.roll(faces_y, -1, 3)
        + faces_z[:, :-1]
        - faces_z[:, 1:]
    )


def by_levels(tracers, fluxes, weight_in, weight_out):
    spec_loc, depth_all, width_x, width_y = tracers.shape
    tile_at = lax.axis_index("tile")
    state = lax.all_to_all(tracers, "species", split_axis=1, concat_axis=0, tiled=True)
    spec_all, lev_loc = (state.shape[0], state.shape[1])
    grid_shape = (lev_loc, width_x, width_y)
    column = tile_at * width_x + lax.broadcasted_iota(jnp.int32, grid_shape, 1)
    level_at = lax.axis_index("species") * lev_loc + lax.broadcasted_iota(jnp.int32, grid_shape, 0)
    for interval in range(STEPS):
        own_flux = fluxes[interval]
        flux_x = jnp.where(column == 0, 0.0, own_flux[0])
        flux_y = own_flux[1]
        flux_z = jnp.where(level_at == 0, 0.0, own_flux[2])
        stacked = jnp.concatenate([state, flux_x[None], flux_z[None]], 0)
        padded = extended(stacked, (("species", 1), ("tile", 2)), 1)
        padded_state = padded[:spec_all]
        padded_x = padded[spec_all, 1:-1]
        padded_z = padded[spec_all + 1, :, 1:-1]
        state = advance(padded_state, padded_x, flux_y, padded_z)
        flattened = state.astype(jnp.bfloat16).reshape(spec_all, lev_loc, width_x * width_y)
        hidden = jax.nn.silu(
            jnp.einsum("hs,szc->hzc", weight_in, flattened, preferred_element_type=jnp.float32)
        ).astype(jnp.bfloat16)
        tendency = (
            0.5 * jnp.einsum("sh,hzc->szc", weight_out, hidden, preferred_element_type=jnp.float32)
        ).astype(jnp.bfloat16)
        state = state + tendency.reshape(state.shape).astype(jnp.float32)
    return lax.all_to_all(state, "species", split_axis=0, concat_axis=1, tiled=True)


def place_and_species(count):
    species = lax.axis_index("species")
    return jnp.where(lax.rem(lax.axis_index("tile"), 2) == 1, count - 1 - species, species), species


def columns_of(place):
    odd = lax.rem(place, 2)
    return 2 * place + odd, 2 * place + 1 - odd


def pack_kernel(count, depth, kind, *refs):
    tracers_ref, out_refs = refs[0], refs[-count:]
    width = 2 * count
    spec = tracers_ref.shape[0] // (depth * width)
    lev = depth // count
    own, _ = place_and_species(count)
    columns = [columns_of(own ^ d) for d in range(count)]

    def level(k, carry):
        for d in range(count):
            x = columns[d][0 if kind == "B" else 1]
            cells = tracers_ref[pl.ds(k * width + x, spec, stride=depth * width), :]
            out_refs[d][k] = cells.astype(jnp.bfloat16)
        return carry

    lax.fori_loop(0, depth, level, 0, unroll=2)
    if kind == "A":
        return
    flux_ref = refs[1]
    outer = lax.axis_index("tile") == 0
    for d in range(count):
        b_at, a_at = columns[d]
        low = jnp.minimum(b_at, a_at)

        def tile_of(direction, x):
            return jnp.concatenate(
                [
                    flux_ref[pl.ds((t * 3 + direction) * lev * width + x, lev, stride=width), :]
                    for t in range(STEPS)
                ],
                0,
            )

        first = jnp.where(jnp.logical_and(outer, low == 0), 0.0, tile_of(0, low))
        out_refs[d][depth] = first.astype(jnp.bfloat16)
        others = ((0, low + 1), (1, b_at), (2, b_at), (1, a_at), (2, a_at))
        for i, (direction, x) in enumerate(others):
            out_refs[d][depth + 1 + i] = tile_of(direction, x).astype(jnp.bfloat16)


def unpack_kernel(count, depth, kind, *refs):
    got, (state_ref, msg_ref) = refs[:count], refs[-2 if kind == "A" else -4 :][:2]
    lev = depth // count
    spec = got[0].shape[1]
    _, species = place_and_species(count)

    if kind == "B":
        flux_ref, near_ref = refs[-2:]
        near_ref[...] = refs[count][...]

    def level(d, k, carry):
        rows = pl.ds(pl.multiple_of((species ^ d) * spec, spec), spec)
        cells = got[d][k]
        state_ref[k, rows] = cells.astype(jnp.float32)
        msg_ref[species ^ d, k] = cells
        return carry

    for d in range(count):
        lax.fori_loop(0, depth, functools.partial(level, d), 0, unroll=4)
        source = species ^ d
        if kind == "A":
            msg_ref[source, depth] = refs[count + d][depth]
            continue
        for i in range(4):
            msg_ref[source, depth + i] = got[d][depth + i]
        for i in range(6):
            part = got[d][depth + i].astype(jnp.float32)
            for t in range(STEPS):
                flux_ref[t, i, source] = part[t * lev : (t + 1) * lev]


def column_kernel(
    t, kind, group, sends, own_ref, inner_ref, outer_ref, flux_ref, from_ref, w_in_ref, w_out_ref, *rest
):
    last = t == STEPS - 1
    coef = rest[-1]
    count, spec, lev = from_ref.shape[0], from_ref.shape[2], flux_ref.shape[3]
    depth, spec_all, width_y = inner_ref.shape
    place, species = place_and_species(count)
    rest = list(rest)
    outs = rest[:count] if last else None
    send_ref = rest[count] if outs else rest.pop(0) if sends else None
    new_ref = None if last else rest.pop(0)

    def cells_of(ref, k):
        if ref.shape == inner_ref.shape:
            return ref[k]
        return jnp.concatenate([ref[s, k].astype(jnp.float32) for s in range(count)], 0)

    def mine(index):
        return jnp.concatenate([flux_ref[t, index, s] for s in range(count)], 0)

    def theirs(index):
        parts = [from_ref[s, depth + index].astype(jnp.float32) for s in range(count)]
        return jnp.concatenate([p[t * lev : (t + 1) * lev] for p in parts], 0)

    even = lax.rem(place, 2) == 0
    if kind == "A":
        outer_high = even
        fx = jnp.where(even, mine(1), mine(0))
        fx_hi = jnp.where(even, theirs(0), mine(1))
        fy, fz = mine(4), mine(5)
    elif kind == "B":
        outer_high = jnp.logical_not(even)
        fx = jnp.where(even, mine(0), mine(1))
        fx_hi = jnp.where(even, mine(1), theirs(0))
        fy, fz = mine(2), mine(3)
    else:
        outer_high = jnp.logical_not(even)
        fx = jnp.where(even, theirs(1), theirs(0))
        fx_hi = jnp.where(even, mine(0), theirs(1))
        fy, fz = theirs(2), theirs(3)
    fy_hi = pltpu.roll(fy, width_y - 1, 1)
    fz = jnp.where(lax.broadcasted_iota(jnp.int32, fz.shape, 0) == 0, 0.0, fz)
    fz_hi = jnp.concatenate([fz[1:], jnp.zeros_like(fz[:1])], 0)
    low, high = positive(fx), -negative(fx_hi)
    coef[0] = (
        1.0
        + (negative(fx) - positive(fx_hi))
        + (negative(fy) - positive(fy_hi))
        + (negative(fz) - positive(fz_hi))
    )
    coef[1] = jnp.where(outer_high, high, low)
    coef[2] = jnp.where(outer_high, low, high)
    coef[3] = positive(fy)
    coef[4] = -negative(fy_hi)
    coef[5] = positive(fz)
    coef[6] = -negative(fz_hi)
    w_in = w_in_ref[...]
    w_out = w_out_ref[...]

    def level(k):
        own = cells_of(own_ref, k)
        out = coef[0, pl.ds(k, 1)] * own
        out += coef[1, pl.ds(k, 1)] * cells_of(outer_ref, k)
        out += coef[2, pl.ds(k, 1)] * inner_ref[k]
        out += coef[3, pl.ds(k, 1)] * pltpu.roll(own, 1, 1)
        out += coef[4, pl.ds(k, 1)] * pltpu.roll(own, width_y - 1, 1)
        out += coef[5, pl.ds(k, 1)] * cells_of(own_ref, max(k - 1, 0))
        out += coef[6, pl.ds(k, 1)] * cells_of(own_ref, min(k + 1, depth - 1))
        return out, out.astype(jnp.bfloat16)

    hid = w_in.shape[0]
    split = hid // 2
    wide = 2 * width_y
    pieces = [(i, j) for j in range(group // 2) for i in range(2)]

    def first_matmul(i, cells):
        return jnp.dot(w_in[i * split : (i + 1) * split], cells, preferred_element_type=jnp.float32)

    def columns(k0):
        levels = [level(k0 + i) for i in range(group)]
        moved = [m for m, _ in levels]
        cells = [jnp.concatenate([levels[j][1], levels[j + 1][1]], 1) for j in range(0, group, 2)]
        return moved, cells

    moved, cells = columns(0)
    halves = [first_matmul(i, cells[j]) for i, j in pieces]
    for k0 in range(0, depth, group):
        more = k0 + group < depth
        if more:
            next_moved, cells = columns(k0 + group)
        next_halves = []
        for p, (i, j) in enumerate(pieces):
            if more:
                next_halves.append(first_matmul(i, cells[j]))
            half = halves[p]
            hidden = (half + half * jnp.tanh(half)).astype(jnp.bfloat16)
            part = jnp.dot(w_out[:, i * split : (i + 1) * split], hidden, preferred_element_type=jnp.float32)
            change = part if i == 0 else change + part
            if i == 0:
                continue
            for n in range(2):
                k = k0 + 2 * j + n
                new = moved[2 * j + n] + change[:, n * width_y : (n + 1) * width_y]
                if new_ref is not None:
                    new_ref[k] = new
                if send_ref is not None:
                    for s in range(count):
                        send_ref[s, k] = new[s * spec : (s + 1) * spec].astype(jnp.bfloat16)
        halves = next_halves
        if more:
            moved = next_moved
    if outs is not None:
        for d in range(count):
            outs[d][...] = send_ref[species ^ d]


def finish_kernel(count, *refs):
    pieces, (out_ref, held, sems) = refs[: 2 * count], refs[2 * count :]
    parts, spec, rows, width_y = held.shape
    width = 2 * count
    lev = rows // width
    own, _ = place_and_species(count)
    columns = [columns_of(own ^ d) for d in range(count)]
    copies = []
    for part in range(parts):
        flat = held.at[part].reshape(spec * rows, width_y)

        def level(k, carry):
            for d in range(count):
                for side, x in enumerate(columns[d]):
                    cells = pieces[side * count + d][part * lev + k].astype(jnp.float32)
                    flat[pl.ds(k * width + x, spec, stride=rows), :] = cells
            return carry

        lax.fori_loop(0, lev, level, 0)
        target = out_ref.at[:, pl.ds(part * rows, rows), :]
        copies.append(pltpu.make_async_copy(held.at[part], target, sems.at[part]))
        copies[-1].start()
    for copy in copies:
        copy.wait()


def call(kernel, out_shape, args, scratch=(), far_out=False):
    many = isinstance(out_shape, (list, tuple))
    anywhere = pl.BlockSpec(memory_space=pl.ANY)
    return pl.pallas_call(
        kernel,
        out_shape=out_shape,
        in_specs=[VMEM] * len(args),
        out_specs=[VMEM] * len(out_shape) if many else anywhere if far_out else VMEM,
        scratch_shapes=scratch,
        compiler_params=pltpu.CompilerParams(vmem_limit_bytes=LIMIT),
        cost_estimate=pl.CostEstimate(flops=1024, bytes_accessed=1024, transcendentals=0),
    )(*args)


def by_columns(tracers, fluxes, weight_in, weight_out):
    spec, depth, width, width_y = tracers.shape
    count, tiles = lax.axis_size("species"), lax.axis_size("tile")
    spec_all = spec * count
    f32, bf16 = jnp.float32, jnp.bfloat16
    shape = jax.ShapeDtypeStruct

    chain = []
    for t in range(tiles):
        for place in range(count):
            s = place if t % 2 == 0 else count - 1 - place
            chain.append(s * tiles + t)
    swap_a, swap_b = [], []
    for i in range(len(chain) - 1):
        (swap_a if i % 2 == 0 else swap_b).extend(
            [(chain[i], chain[i + 1]), (chain[i + 1], chain[i])]
        )

    w_in = weight_in * jnp.asarray(0.5, bf16)
    w_out = weight_out * jnp.asarray(0.5, bf16)

    def swapped(piece, d):
        return lax.ppermute(piece, "species", [(s, s ^ d) for s in range(count)])

    def exchange(pieces):
        return [piece if d == 0 else swapped(piece, d) for d, piece in enumerate(pieces)]

    row = shape((depth, spec_all, width_y), f32)
    held = pltpu.VMEM((PARTS, spec, depth * width // PARTS, width_y), f32)
    flat = tracers.reshape(-1, width_y)
    sent = shape((count, depth, spec, width_y), bf16)
    piece = shape((depth, spec, width_y), bf16)
    piece_b = shape((depth + 6, spec, width_y), bf16)
    packed_b = call(
        functools.partial(pack_kernel, count, depth, "B"),
        [piece_b] * count,
        (flat, fluxes.reshape(-1, width_y)),
    )
    got_b = exchange(packed_b)
    packed_a = call(functools.partial(pack_kernel, count, depth, "A"), [piece] * count, (flat, packed_b[0]))
    b, send_b, flux, near_a = call(
        functools.partial(unpack_kernel, count, depth, "B"),
        [
            row,
            shape((count, depth + 4, spec, width_y), bf16),
            shape((STEPS, 6, count, depth // count, width_y), f32),
            piece,
        ],
        (*got_b, packed_a[1]),
    )
    halo_b = from_b = lax.ppermute(send_b, AXES, swap_b)
    got_a = [packed_a[0], swapped(near_a, 1), *(swapped(packed_a[d], d) for d in range(2, count))]
    a, send_a = call(
        functools.partial(unpack_kernel, count, depth, "A"),
        [row, shape((count, depth + 1, spec, width_y), bf16)],
        (*got_a, *got_b, send_b),
    )
    halo_a = from_a = lax.ppermute(send_a, AXES, swap_a)
    halo_c = lax.ppermute(send_a, AXES, swap_b)
    common = [
        pltpu.VMEM((7, depth, width_y), f32),
    ]

    def column(t, kind, own, inner, outer, sends=True):
        scratch = list(common)
        if t < STEPS - 1:
            outs = [sent, row] if sends else [row]
        else:
            outs = [piece] * count
            scratch = [pltpu.VMEM(sent.shape, bf16), *common]
        return call(
            functools.partial(column_kernel, t, kind, GROUP, sends),
            outs,
            (own, inner, outer, flux, from_a if kind == "A" else from_b, w_in, w_out),
            scratch=scratch,
        )

    for t in range(0, STEPS, 2):
        send_a, new_a = column(t, "A", a, b, halo_a)
        halo_a = lax.ppermute(send_a, AXES, swap_a)
        (new_b,) = column(t, "B", b, a, halo_b, sends=False)
        (ghost,) = column(t, "G", halo_b, b, halo_c, sends=False)
        a, b = new_a, new_b
        made_b = column(t + 1, "B", b, a, ghost)
        if t + 1 == STEPS - 1:
            pieces = [*exchange(made_b), *exchange(column(t + 1, "A", a, b, halo_a))]
            break
        halo_b = lax.ppermute(made_b[0], AXES, swap_b)
        send_a, new_a = column(t + 1, "A", a, b, halo_a)
        halo_a = lax.ppermute(send_a, AXES, swap_a)
        halo_c = lax.ppermute(send_a, AXES, swap_b)
        a, b = new_a, made_b[1]
    out = call(
        functools.partial(finish_kernel, count),
        shape((spec, depth * width, width_y), f32),
        pieces,
        scratch=[held, pltpu.SemaphoreType.DMA((PARTS,))],
        far_out=True,
    )
    return out.reshape(tracers.shape)


def per_device(tracers, fluxes, weight_in, weight_out):
    spec, depth, width, width_y = tracers.shape
    count = lax.axis_size("species")
    fits = (
        width == 2 * count
        and count % 2 == 0
        and STEPS % 2 == 0
        and count & (count - 1) == 0
        and depth % count == 0
        and depth % GROUP == 0
        and depth % PARTS == 0
        and spec == PACK
        and width_y % 128 == 0
        and width % 8 == 0
        and STEPS * (depth // count) == PACK
    )
    chosen = by_columns if fits else by_levels
    return chosen(tracers, fluxes, weight_in, weight_out)


def solution(mesh):
    placed = (P("species", None, "tile", None), P(None, None, "species", "tile", None), P(), P())
    return jax.shard_map(
        per_device,
        mesh=mesh,
        in_specs=placed,
        out_specs=P("species", None, "tile", None),
        check_vma=False,
    )
```

```python
import functools

import jax
import jax.numpy as jnp
from jax import lax
from jax.experimental import pallas as pl
from jax.experimental.pallas import tpu as pltpu
from jax.sharding import PartitionSpec as P

STEPS = 4
AXES = ("species", "tile")
PACK = 16
GROUP = 4
PARTS = 8
VMEM = pl.BlockSpec(memory_space=pltpu.VMEM)
LIMIT = 24 * 1024 * 1024


def positive(value):
    return jnp.maximum(value, 0.0)


def negative(value):
    return jnp.minimum(value, 0.0)


def extended(cells, sides, width):
    for axis, dim in sides:
        count = lax.axis_size(axis)
        ends = count - 1
        head = lax.slice_in_dim(cells, 0, width, axis=dim)
        tail = lax.slice_in_dim(cells, cells.shape[dim] - width, cells.shape[dim], axis=dim)
        cells = jnp.concatenate(
            [
                lax.ppermute(tail, axis, [(i, (i + 1) % count) for i in range(ends)]),
                cells,
                lax.ppermute(head, axis, [((i + 1) % count, i) for i in range(ends)]),
            ],
            axis=dim,
        )
    return cells


def advance(padded_state, padded_x, flux_y, padded_z):
    inner = padded_state[:, 1:-1, 1:-1]
    along_x = padded_state[:, 1:-1]
    face_x = padded_x[:, 1:]
    faces_x = positive(face_x) * along_x[:, :, :-1] + negative(face_x) * along_x[:, :, 1:]
    along_z = padded_state[:, :, 1:-1]
    face_z = padded_z[1:]
    faces_z = positive(face_z) * along_z[:, :-1] + negative(face_z) * along_z[:, 1:]
    faces_y = positive(flux_y) * jnp.roll(inner, 1, 3) + negative(flux_y) * inner
    return (
        inner
        + faces_x[:, :, :-1]
        - faces_x[:, :, 1:]
        + faces_y
        - jnp.roll(faces_y, -1, 3)
        + faces_z[:, :-1]
        - faces_z[:, 1:]
    )


def by_levels(tracers, fluxes, weight_in, weight_out):
    spec_loc, depth_all, width_x, width_y = tracers.shape
    tile_at = lax.axis_index("tile")
    state = lax.all_to_all(tracers, "species", split_axis=1, concat_axis=0, tiled=True)
    spec_all, lev_loc = (state.shape[0], state.shape[1])
    grid_shape = (lev_loc, width_x, width_y)
    column = tile_at * width_x + lax.broadcasted_iota(jnp.int32, grid_shape, 1)
    level_at = lax.axis_index("species") * lev_loc + lax.broadcasted_iota(jnp.int32, grid_shape, 0)
    for interval in range(STEPS):
        own_flux = fluxes[interval]
        flux_x = jnp.where(column == 0, 0.0, own_flux[0])
        flux_y = own_flux[1]
        flux_z = jnp.where(level_at == 0, 0.0, own_flux[2])
        stacked = jnp.concatenate([state, flux_x[None], flux_z[None]], 0)
        padded = extended(stacked, (("species", 1), ("tile", 2)), 1)
        padded_state = padded[:spec_all]
        padded_x = padded[spec_all, 1:-1]
        padded_z = padded[spec_all + 1, :, 1:-1]
        state = advance(padded_state, padded_x, flux_y, padded_z)
        flattened = state.astype(jnp.bfloat16).reshape(spec_all, lev_loc, width_x * width_y)
        hidden = jax.nn.silu(
            jnp.einsum("hs,szc->hzc", weight_in, flattened, preferred_element_type=jnp.float32)
        ).astype(jnp.bfloat16)
        tendency = (
            0.5 * jnp.einsum("sh,hzc->szc", weight_out, hidden, preferred_element_type=jnp.float32)
        ).astype(jnp.bfloat16)
        state = state + tendency.reshape(state.shape).astype(jnp.float32)
    return lax.all_to_all(state, "species", split_axis=0, concat_axis=1, tiled=True)


def place_and_species(count):
    species = lax.axis_index("species")
    return jnp.where(lax.rem(lax.axis_index("tile"), 2) == 1, count - 1 - species, species), species


def columns_of(place):
    odd = lax.rem(place, 2)
    return 2 * place + odd, 2 * place + 1 - odd


def pack_kernel(count, depth, kind, *refs):
    tracers_ref, out_refs = refs[0], refs[-count:]
    width = 2 * count
    spec = tracers_ref.shape[0] // (depth * width)
    lev = depth // count
    own, _ = place_and_species(count)
    columns = [columns_of(own ^ d) for d in range(count)]

    def level(k, carry):
        for d in range(count):
            x = columns[d][0 if kind == "B" else 1]
            cells = tracers_ref[pl.ds(k * width + x, spec, stride=depth * width), :]
            out_refs[d][k] = cells.astype(jnp.bfloat16)
        return carry

    lax.fori_loop(0, depth, level, 0, unroll=2)
    if kind == "A":
        return
    flux_ref = refs[1]
    for d in range(count):
        b_at, a_at = columns[d]
        low = jnp.minimum(b_at, a_at)

        def tile_of(direction, x):
            return jnp.concatenate(
                [
                    flux_ref[pl.ds((t * 3 + direction) * lev * width + x, lev, stride=width), :]
                    for t in range(STEPS)
                ],
                0,
            )

        tiles = ((0, low), (0, low + 1), (1, b_at), (2, b_at), (1, a_at), (2, a_at))
        for i, (direction, x) in enumerate(tiles):
            out_refs[d][depth + i] = tile_of(direction, x).astype(jnp.bfloat16)


def unpack_kernel(count, depth, kind, *refs):
    got, (state_ref, msg_ref) = refs[:count], refs[-2 if kind == "A" else -4 :][:2]
    lev = depth // count
    spec = got[0].shape[1]
    _, species = place_and_species(count)

    if kind == "B":
        flux_ref, near_ref = refs[-2:]
        near_ref[...] = refs[count][...]

    def level(d, k, carry):
        rows = pl.ds(pl.multiple_of((species ^ d) * spec, spec), spec)
        cells = got[d][k]
        state_ref[k, rows] = cells.astype(jnp.float32)
        msg_ref[species ^ d, k] = cells
        return carry

    for d in range(count):
        lax.fori_loop(0, depth, functools.partial(level, d), 0, unroll=4)
        source = species ^ d
        if kind == "A":
            msg_ref[source, depth] = refs[count + d][depth]
            continue
        for i in range(4):
            msg_ref[source, depth + i] = got[d][depth + i]
        for i in range(6):
            part = got[d][depth + i].astype(jnp.float32)
            for t in range(STEPS):
                flux_ref[t, i, source] = part[t * lev : (t + 1) * lev]


def column_kernel(
    t, kind, group, sends, own_ref, inner_ref, outer_ref, flux_ref, from_ref, w_in_ref, w_out_ref, *rest
):
    last = t == STEPS - 1
    coef = rest[-1]
    count, spec, lev = from_ref.shape[0], from_ref.shape[2], flux_ref.shape[3]
    depth, spec_all, width_y = inner_ref.shape
    place, species = place_and_species(count)
    rest = list(rest)
    outs = rest[:count] if last else None
    send_ref = rest[count] if outs else rest.pop(0) if sends else None
    new_ref = None if last else rest.pop(0)

    def cells_of(ref, k):
        if ref.shape == inner_ref.shape:
            return ref[k]
        return jnp.concatenate([ref[s, k].astype(jnp.float32) for s in range(count)], 0)

    def mine(index):
        return jnp.concatenate([flux_ref[t, index, s] for s in range(count)], 0)

    def theirs(index):
        parts = [from_ref[s, depth + index].astype(jnp.float32) for s in range(count)]
        return jnp.concatenate([p[t * lev : (t + 1) * lev] for p in parts], 0)

    even = lax.rem(place, 2) == 0
    if kind == "A":
        outer_high = even
        fx = jnp.where(even, mine(1), mine(0))
        fx_hi = jnp.where(even, theirs(0), mine(1))
        fy, fz = mine(4), mine(5)
    elif kind == "B":
        outer_high = jnp.logical_not(even)
        fx = jnp.where(even, mine(0), mine(1))
        fx_hi = jnp.where(even, mine(1), theirs(0))
        fy, fz = mine(2), mine(3)
    else:
        outer_high = jnp.logical_not(even)
        fx = jnp.where(even, theirs(1), theirs(0))
        fx_hi = jnp.where(even, mine(0), theirs(1))
        fy, fz = theirs(2), theirs(3)
    fy_hi = pltpu.roll(fy, width_y - 1, 1)
    fz = jnp.where(lax.broadcasted_iota(jnp.int32, fz.shape, 0) == 0, 0.0, fz)
    fz_hi = jnp.concatenate([fz[1:], jnp.zeros_like(fz[:1])], 0)
    low, high = positive(fx), -negative(fx_hi)
    coef[0] = (
        1.0
        + (negative(fx) - positive(fx_hi))
        + (negative(fy) - positive(fy_hi))
        + (negative(fz) - positive(fz_hi))
    )
    coef[1] = jnp.where(outer_high, high, low)
    coef[2] = jnp.where(outer_high, low, high)
    coef[3] = positive(fy)
    coef[4] = -negative(fy_hi)
    coef[5] = positive(fz)
    coef[6] = -negative(fz_hi)
    w_in = w_in_ref[...]
    w_out = w_out_ref[...]

    def level(k):
        own = cells_of(own_ref, k)
        out = coef[0, pl.ds(k, 1)] * own
        out += coef[1, pl.ds(k, 1)] * cells_of(outer_ref, k)
        out += coef[2, pl.ds(k, 1)] * inner_ref[k]
        out += coef[3, pl.ds(k, 1)] * pltpu.roll(own, 1, 1)
        out += coef[4, pl.ds(k, 1)] * pltpu.roll(own, width_y - 1, 1)
        out += coef[5, pl.ds(k, 1)] * cells_of(own_ref, max(k - 1, 0))
        out += coef[6, pl.ds(k, 1)] * cells_of(own_ref, min(k + 1, depth - 1))
        return out, out.astype(jnp.bfloat16)

    hid = w_in.shape[0]
    split = hid // 2
    wide = 2 * width_y
    pieces = [(i, j) for j in range(group // 2) for i in range(2)]

    def first_matmul(i, cells):
        return jnp.dot(w_in[i * split : (i + 1) * split], cells, preferred_element_type=jnp.float32)

    def columns(k0):
        levels = [level(k0 + i) for i in range(group)]
        moved = [m for m, _ in levels]
        cells = [jnp.concatenate([levels[j][1], levels[j + 1][1]], 1) for j in range(0, group, 2)]
        return moved, cells

    moved, cells = columns(0)
    halves = [first_matmul(i, cells[j]) for i, j in pieces]
    for k0 in range(0, depth, group):
        more = k0 + group < depth
        if more:
            next_moved, cells = columns(k0 + group)
        next_halves = []
        for p, (i, j) in enumerate(pieces):
            if more:
                next_halves.append(first_matmul(i, cells[j]))
            half = halves[p]
            hidden = (half + half * jnp.tanh(half)).astype(jnp.bfloat16)
            part = jnp.dot(w_out[:, i * split : (i + 1) * split], hidden, preferred_element_type=jnp.float32)
            change = part if i == 0 else change + part
            if i == 0:
                continue
            for n in range(2):
                k = k0 + 2 * j + n
                new = moved[2 * j + n] + change[:, n * width_y : (n + 1) * width_y]
                if new_ref is not None:
                    new_ref[k] = new
                if send_ref is not None:
                    for s in range(count):
                        send_ref[s, k] = new[s * spec : (s + 1) * spec].astype(jnp.bfloat16)
        halves = next_halves
        if more:
            moved = next_moved
    if outs is not None:
        for d in range(count):
            outs[d][...] = send_ref[species ^ d]


def finish_kernel(count, *refs):
    pieces, (out_ref, held, sems) = refs[: 2 * count], refs[2 * count :]
    parts, spec, rows, width_y = held.shape
    width = 2 * count
    lev = rows // width
    own, _ = place_and_species(count)
    columns = [columns_of(own ^ d) for d in range(count)]
    copies = []
    for part in range(parts):
        flat = held.at[part].reshape(spec * rows, width_y)

        def level(k, carry):
            for d in range(count):
                for side, x in enumerate(columns[d]):
                    cells = pieces[side * count + d][part * lev + k].astype(jnp.float32)
                    flat[pl.ds(k * width + x, spec, stride=rows), :] = cells
            return carry

        lax.fori_loop(0, lev, level, 0)
        target = out_ref.at[:, pl.ds(part * rows, rows), :]
        copies.append(pltpu.make_async_copy(held.at[part], target, sems.at[part]))
        copies[-1].start()
    for copy in copies:
        copy.wait()


def call(kernel, out_shape, args, scratch=(), far_out=False):
    many = isinstance(out_shape, (list, tuple))
    anywhere = pl.BlockSpec(memory_space=pl.ANY)
    return pl.pallas_call(
        kernel,
        out_shape=out_shape,
        in_specs=[VMEM] * len(args),
        out_specs=[VMEM] * len(out_shape) if many else anywhere if far_out else VMEM,
        scratch_shapes=scratch,
        compiler_params=pltpu.CompilerParams(vmem_limit_bytes=LIMIT),
        cost_estimate=pl.CostEstimate(flops=10**10, bytes_accessed=10**6, transcendentals=0),
    )(*args)


def by_columns(tracers, fluxes, weight_in, weight_out):
    spec, depth, width, width_y = tracers.shape
    count, tiles = lax.axis_size("species"), lax.axis_size("tile")
    spec_all = spec * count
    f32, bf16 = jnp.float32, jnp.bfloat16
    shape = jax.ShapeDtypeStruct

    chain = []
    for t in range(tiles):
        for place in range(count):
            s = place if t % 2 == 0 else count - 1 - place
            chain.append(s * tiles + t)
    swap_a, swap_b = [], []
    for i in range(len(chain) - 1):
        (swap_a if i % 2 == 0 else swap_b).extend(
            [(chain[i], chain[i + 1]), (chain[i + 1], chain[i])]
        )

    w_in = weight_in * jnp.asarray(0.5, bf16)
    w_out = weight_out * jnp.asarray(0.5, bf16)

    def swapped(piece, d):
        return lax.ppermute(piece, "species", [(s, s ^ d) for s in range(count)])

    def exchange(pieces):
        return [piece if d == 0 else swapped(piece, d) for d, piece in enumerate(pieces)]

    row = shape((depth, spec_all, width_y), f32)
    held = pltpu.VMEM((PARTS, spec, depth * width // PARTS, width_y), f32)
    flat = tracers.reshape(-1, width_y)
    column_at = lax.axis_index("tile") * width + lax.broadcasted_iota(jnp.int32, fluxes.shape, 3)
    closed = jnp.logical_and(column_at == 0, lax.broadcasted_iota(jnp.int32, fluxes.shape, 1) == 0)
    fluxes = jnp.where(closed, 0.0, fluxes)
    sent = shape((count, depth, spec, width_y), bf16)
    piece = shape((depth, spec, width_y), bf16)
    piece_b = shape((depth + 6, spec, width_y), bf16)
    packed_b = call(
        functools.partial(pack_kernel, count, depth, "B"),
        [piece_b] * count,
        (flat, fluxes.reshape(-1, width_y)),
    )
    got_b = exchange(packed_b)
    packed_a = call(functools.partial(pack_kernel, count, depth, "A"), [piece] * count, (flat, packed_b[0]))
    b, send_b, flux, near_a = call(
        functools.partial(unpack_kernel, count, depth, "B"),
        [
            row,
            shape((count, depth + 4, spec, width_y), bf16),
            shape((STEPS, 6, count, depth // count, width_y), f32),
            piece,
        ],
        (*got_b, packed_a[1]),
    )
    halo_b = from_b = lax.ppermute(send_b, AXES, swap_b)
    got_a = [packed_a[0], swapped(near_a, 1), *(swapped(packed_a[d], d) for d in range(2, count))]
    a, send_a = call(
        functools.partial(unpack_kernel, count, depth, "A"),
        [row, shape((count, depth + 1, spec, width_y), bf16)],
        (*got_a, *got_b, send_b),
    )
    halo_a = from_a = lax.ppermute(send_a, AXES, swap_a)
    halo_c = lax.ppermute(send_a, AXES, swap_b)
    common = [
        pltpu.VMEM((7, depth, width_y), f32),
    ]

    def column(t, kind, own, inner, outer, sends=True):
        scratch = list(common)
        if t < STEPS - 1:
            outs = [sent, row] if sends else [row]
        else:
            outs = [piece] * count
            scratch = [pltpu.VMEM(sent.shape, bf16), *common]
        return call(
            functools.partial(column_kernel, t, kind, GROUP, sends),
            outs,
            (own, inner, outer, flux, from_a if kind == "A" else from_b, w_in, w_out),
            scratch=scratch,
        )

    for t in range(0, STEPS, 2):
        send_a, new_a = column(t, "A", a, b, halo_a)
        halo_a = lax.ppermute(send_a, AXES, swap_a)
        (new_b,) = column(t, "B", b, a, halo_b, sends=False)
        (ghost,) = column(t, "G", halo_b, b, halo_c, sends=False)
        a, b = new_a, new_b
        made_b = column(t + 1, "B", b, a, ghost)
        if t + 1 == STEPS - 1:
            pieces = [*exchange(made_b), *exchange(column(t + 1, "A", a, b, halo_a))]
            break
        halo_b = lax.ppermute(made_b[0], AXES, swap_b)
        send_a, new_a = column(t + 1, "A", a, b, halo_a)
        halo_a = lax.ppermute(send_a, AXES, swap_a)
        halo_c = lax.ppermute(send_a, AXES, swap_b)
        a, b = new_a, made_b[1]
    out = call(
        functools.partial(finish_kernel, count),
        shape((spec, depth * width, width_y), f32),
        pieces,
        scratch=[held, pltpu.SemaphoreType.DMA((PARTS,))],
        far_out=True,
    )
    return out.reshape(tracers.shape)


def per_device(tracers, fluxes, weight_in, weight_out):
    spec, depth, width, width_y = tracers.shape
    count = lax.axis_size("species")
    fits = (
        width == 2 * count
        and count % 2 == 0
        and STEPS % 2 == 0
        and count & (count - 1) == 0
        and depth % count == 0
        and depth % GROUP == 0
        and depth % PARTS == 0
        and spec == PACK
        and width_y % 128 == 0
        and width % 8 == 0
        and STEPS * (depth // count) == PACK
    )
    chosen = by_columns if fits else by_levels
    return chosen(tracers, fluxes, weight_in, weight_out)


def solution(mesh):
    placed = (P("species", None, "tile", None), P(None, None, "species", "tile", None), P(), P())
    return jax.shard_map(
        per_device,
        mesh=mesh,
        in_specs=placed,
        out_specs=P("species", None, "tile", None),
        check_vma=False,
    )
```

```python
import functools

import jax
import jax.numpy as jnp
from jax import lax
from jax.experimental import pallas as pl
from jax.experimental.pallas import tpu as pltpu
from jax.sharding import PartitionSpec as P

STEPS = 4
AXES = ("species", "tile")
PACK = 16
GROUP = 4
PARTS = 8
COLUMN_COST = 10**10
A0_COST = 1024
VMEM = pl.BlockSpec(memory_space=pltpu.VMEM)
LIMIT = 24 * 1024 * 1024


def positive(value):
    return jnp.maximum(value, 0.0)


def negative(value):
    return jnp.minimum(value, 0.0)


def extended(cells, sides, width):
    for axis, dim in sides:
        count = lax.axis_size(axis)
        ends = count - 1
        head = lax.slice_in_dim(cells, 0, width, axis=dim)
        tail = lax.slice_in_dim(cells, cells.shape[dim] - width, cells.shape[dim], axis=dim)
        cells = jnp.concatenate(
            [
                lax.ppermute(tail, axis, [(i, (i + 1) % count) for i in range(ends)]),
                cells,
                lax.ppermute(head, axis, [((i + 1) % count, i) for i in range(ends)]),
            ],
            axis=dim,
        )
    return cells


def advance(padded_state, padded_x, flux_y, padded_z):
    inner = padded_state[:, 1:-1, 1:-1]
    along_x = padded_state[:, 1:-1]
    face_x = padded_x[:, 1:]
    faces_x = positive(face_x) * along_x[:, :, :-1] + negative(face_x) * along_x[:, :, 1:]
    along_z = padded_state[:, :, 1:-1]
    face_z = padded_z[1:]
    faces_z = positive(face_z) * along_z[:, :-1] + negative(face_z) * along_z[:, 1:]
    faces_y = positive(flux_y) * jnp.roll(inner, 1, 3) + negative(flux_y) * inner
    return (
        inner
        + faces_x[:, :, :-1]
        - faces_x[:, :, 1:]
        + faces_y
        - jnp.roll(faces_y, -1, 3)
        + faces_z[:, :-1]
        - faces_z[:, 1:]
    )


def by_levels(tracers, fluxes, weight_in, weight_out):
    spec_loc, depth_all, width_x, width_y = tracers.shape
    tile_at = lax.axis_index("tile")
    state = lax.all_to_all(tracers, "species", split_axis=1, concat_axis=0, tiled=True)
    spec_all, lev_loc = (state.shape[0], state.shape[1])
    grid_shape = (lev_loc, width_x, width_y)
    column = tile_at * width_x + lax.broadcasted_iota(jnp.int32, grid_shape, 1)
    level_at = lax.axis_index("species") * lev_loc + lax.broadcasted_iota(jnp.int32, grid_shape, 0)
    for interval in range(STEPS):
        own_flux = fluxes[interval]
        flux_x = jnp.where(column == 0, 0.0, own_flux[0])
        flux_y = own_flux[1]
        flux_z = jnp.where(level_at == 0, 0.0, own_flux[2])
        stacked = jnp.concatenate([state, flux_x[None], flux_z[None]], 0)
        padded = extended(stacked, (("species", 1), ("tile", 2)), 1)
        padded_state = padded[:spec_all]
        padded_x = padded[spec_all, 1:-1]
        padded_z = padded[spec_all + 1, :, 1:-1]
        state = advance(padded_state, padded_x, flux_y, padded_z)
        flattened = state.astype(jnp.bfloat16).reshape(spec_all, lev_loc, width_x * width_y)
        hidden = jax.nn.silu(
            jnp.einsum("hs,szc->hzc", weight_in, flattened, preferred_element_type=jnp.float32)
        ).astype(jnp.bfloat16)
        tendency = (
            0.5 * jnp.einsum("sh,hzc->szc", weight_out, hidden, preferred_element_type=jnp.float32)
        ).astype(jnp.bfloat16)
        state = state + tendency.reshape(state.shape).astype(jnp.float32)
    return lax.all_to_all(state, "species", split_axis=0, concat_axis=1, tiled=True)


def place_and_species(count):
    species = lax.axis_index("species")
    return jnp.where(lax.rem(lax.axis_index("tile"), 2) == 1, count - 1 - species, species), species


def columns_of(place):
    odd = lax.rem(place, 2)
    return 2 * place + odd, 2 * place + 1 - odd


def pack_kernel(count, depth, kind, *refs):
    tracers_ref, out_refs = refs[0], refs[-count:]
    width = 2 * count
    spec = tracers_ref.shape[0] // (depth * width)
    lev = depth // count
    own, _ = place_and_species(count)
    columns = [columns_of(own ^ d) for d in range(count)]

    def level(k, carry):
        for d in range(count):
            x = columns[d][0 if kind == "B" else 1]
            cells = tracers_ref[pl.ds(k * width + x, spec, stride=depth * width), :]
            out_refs[d][k] = cells.astype(jnp.bfloat16)
        return carry

    lax.fori_loop(0, depth, level, 0, unroll=2)
    if kind == "A":
        return
    flux_ref = refs[1]
    for d in range(count):
        b_at, a_at = columns[d]
        low = jnp.minimum(b_at, a_at)

        def tile_of(direction, x):
            return jnp.concatenate(
                [
                    flux_ref[pl.ds((t * 3 + direction) * lev * width + x, lev, stride=width), :]
                    for t in range(STEPS)
                ],
                0,
            )

        tiles = ((0, low), (0, low + 1), (1, b_at), (2, b_at), (1, a_at), (2, a_at))
        for i, (direction, x) in enumerate(tiles):
            out_refs[d][depth + i] = tile_of(direction, x).astype(jnp.bfloat16)


def unpack_kernel(count, depth, kind, *refs):
    got, (state_ref, msg_ref) = refs[:count], refs[-2 if kind == "A" else -4 :][:2]
    lev = depth // count
    spec = got[0].shape[1]
    _, species = place_and_species(count)

    if kind == "B":
        flux_ref, near_ref = refs[-2:]
        near_ref[...] = refs[count][...]

    def level(d, k, carry):
        rows = pl.ds(pl.multiple_of((species ^ d) * spec, spec), spec)
        cells = got[d][k]
        state_ref[k, rows] = cells.astype(jnp.float32)
        msg_ref[species ^ d, k] = cells
        return carry

    for d in range(count):
        lax.fori_loop(0, depth, functools.partial(level, d), 0, unroll=4)
        source = species ^ d
        if kind == "A":
            msg_ref[source, depth] = refs[count + d][depth]
            continue
        for i in range(4):
            msg_ref[source, depth + i] = got[d][depth + i]
        for i in range(6):
            part = got[d][depth + i].astype(jnp.float32)
            for t in range(STEPS):
                flux_ref[t, i, source] = part[t * lev : (t + 1) * lev]


def column_kernel(
    t, kind, group, sends, behind, own_ref, inner_ref, outer_ref, flux_ref, from_ref, w_in_ref, w_out_ref, *rest
):
    last = t == STEPS - 1
    coef = rest[-1]
    count, spec, lev = from_ref.shape[0], from_ref.shape[2], flux_ref.shape[3]
    depth, spec_all, width_y = inner_ref.shape
    place, species = place_and_species(count)
    rest = list(rest)[behind:]
    outs = rest[:count] if last else None
    send_ref = rest[count] if outs else rest.pop(0) if sends else None
    new_ref = None if last else rest.pop(0)

    def cells_of(ref, k):
        if ref.shape == inner_ref.shape:
            return ref[k]
        return jnp.concatenate([ref[s, k].astype(jnp.float32) for s in range(count)], 0)

    def mine(index):
        return jnp.concatenate([flux_ref[t, index, s] for s in range(count)], 0)

    def theirs(index):
        parts = [from_ref[s, depth + index].astype(jnp.float32) for s in range(count)]
        return jnp.concatenate([p[t * lev : (t + 1) * lev] for p in parts], 0)

    even = lax.rem(place, 2) == 0
    if kind == "A":
        outer_high = even
        fx = jnp.where(even, mine(1), mine(0))
        fx_hi = jnp.where(even, theirs(0), mine(1))
        fy, fz = mine(4), mine(5)
    elif kind == "B":
        outer_high = jnp.logical_not(even)
        fx = jnp.where(even, mine(0), mine(1))
        fx_hi = jnp.where(even, mine(1), theirs(0))
        fy, fz = mine(2), mine(3)
    else:
        outer_high = jnp.logical_not(even)
        fx = jnp.where(even, theirs(1), theirs(0))
        fx_hi = jnp.where(even, mine(0), theirs(1))
        fy, fz = theirs(2), theirs(3)
    fy_hi = pltpu.roll(fy, width_y - 1, 1)
    fz = jnp.where(lax.broadcasted_iota(jnp.int32, fz.shape, 0) == 0, 0.0, fz)
    fz_hi = jnp.concatenate([fz[1:], jnp.zeros_like(fz[:1])], 0)
    low, high = positive(fx), -negative(fx_hi)
    coef[0] = (
        1.0
        + (negative(fx) - positive(fx_hi))
        + (negative(fy) - positive(fy_hi))
        + (negative(fz) - positive(fz_hi))
    )
    coef[1] = jnp.where(outer_high, high, low)
    coef[2] = jnp.where(outer_high, low, high)
    coef[3] = positive(fy)
    coef[4] = -negative(fy_hi)
    coef[5] = positive(fz)
    coef[6] = -negative(fz_hi)
    w_in = w_in_ref[...]
    w_out = w_out_ref[...]

    def level(k):
        own = cells_of(own_ref, k)
        out = coef[0, pl.ds(k, 1)] * own
        out += coef[1, pl.ds(k, 1)] * cells_of(outer_ref, k)
        out += coef[2, pl.ds(k, 1)] * inner_ref[k]
        out += coef[3, pl.ds(k, 1)] * pltpu.roll(own, 1, 1)
        out += coef[4, pl.ds(k, 1)] * pltpu.roll(own, width_y - 1, 1)
        out += coef[5, pl.ds(k, 1)] * cells_of(own_ref, max(k - 1, 0))
        out += coef[6, pl.ds(k, 1)] * cells_of(own_ref, min(k + 1, depth - 1))
        return out, out.astype(jnp.bfloat16)

    hid = w_in.shape[0]
    split = hid // 2
    wide = 2 * width_y
    pieces = [(i, j) for j in range(group // 2) for i in range(2)]

    def first_matmul(i, cells):
        return jnp.dot(w_in[i * split : (i + 1) * split], cells, preferred_element_type=jnp.float32)

    def columns(k0):
        levels = [level(k0 + i) for i in range(group)]
        moved = [m for m, _ in levels]
        cells = [jnp.concatenate([levels[j][1], levels[j + 1][1]], 1) for j in range(0, group, 2)]
        return moved, cells

    moved, cells = columns(0)
    halves = [first_matmul(i, cells[j]) for i, j in pieces]
    for k0 in range(0, depth, group):
        more = k0 + group < depth
        if more:
            next_moved, cells = columns(k0 + group)
        next_halves = []
        for p, (i, j) in enumerate(pieces):
            if more:
                next_halves.append(first_matmul(i, cells[j]))
            half = halves[p]
            hidden = (half + half * jnp.tanh(half)).astype(jnp.bfloat16)
            part = jnp.dot(w_out[:, i * split : (i + 1) * split], hidden, preferred_element_type=jnp.float32)
            change = part if i == 0 else change + part
            if i == 0:
                continue
            for n in range(2):
                k = k0 + 2 * j + n
                new = moved[2 * j + n] + change[:, n * width_y : (n + 1) * width_y]
                if new_ref is not None:
                    new_ref[k] = new
                if send_ref is not None:
                    for s in range(count):
                        send_ref[s, k] = new[s * spec : (s + 1) * spec].astype(jnp.bfloat16)
        halves = next_halves
        if more:
            moved = next_moved
    if outs is not None:
        for d in range(count):
            outs[d][...] = send_ref[species ^ d]


def finish_kernel(count, *refs):
    pieces, (out_ref, held, sems) = refs[: 2 * count], refs[2 * count :]
    parts, spec, rows, width_y = held.shape
    width = 2 * count
    lev = rows // width
    own, _ = place_and_species(count)
    columns = [columns_of(own ^ d) for d in range(count)]
    copies = []
    for part in range(parts):
        flat = held.at[part].reshape(spec * rows, width_y)

        def level(k, carry):
            for d in range(count):
                for side, x in enumerate(columns[d]):
                    cells = pieces[side * count + d][part * lev + k].astype(jnp.float32)
                    flat[pl.ds(k * width + x, spec, stride=rows), :] = cells
            return carry

        lax.fori_loop(0, lev, level, 0)
        target = out_ref.at[:, pl.ds(part * rows, rows), :]
        copies.append(pltpu.make_async_copy(held.at[part], target, sems.at[part]))
        copies[-1].start()
    for copy in copies:
        copy.wait()


def call(kernel, out_shape, args, scratch=(), far_out=False, cost=COLUMN_COST):
    many = isinstance(out_shape, (list, tuple))
    anywhere = pl.BlockSpec(memory_space=pl.ANY)
    return pl.pallas_call(
        kernel,
        out_shape=out_shape,
        in_specs=[VMEM] * len(args),
        out_specs=[VMEM] * len(out_shape) if many else anywhere if far_out else VMEM,
        scratch_shapes=scratch,
        compiler_params=pltpu.CompilerParams(vmem_limit_bytes=LIMIT),
        cost_estimate=pl.CostEstimate(flops=cost, bytes_accessed=cost // 10**4, transcendentals=0),
    )(*args)


def by_columns(tracers, fluxes, weight_in, weight_out):
    spec, depth, width, width_y = tracers.shape
    count, tiles = lax.axis_size("species"), lax.axis_size("tile")
    spec_all = spec * count
    f32, bf16 = jnp.float32, jnp.bfloat16
    shape = jax.ShapeDtypeStruct

    chain = []
    for t in range(tiles):
        for place in range(count):
            s = place if t % 2 == 0 else count - 1 - place
            chain.append(s * tiles + t)
    swap_a, swap_b = [], []
    for i in range(len(chain) - 1):
        (swap_a if i % 2 == 0 else swap_b).extend(
            [(chain[i], chain[i + 1]), (chain[i + 1], chain[i])]
        )

    w_in = weight_in * jnp.asarray(0.5, bf16)
    w_out = weight_out * jnp.asarray(0.5, bf16)

    def swapped(piece, d):
        return lax.ppermute(piece, "species", [(s, s ^ d) for s in range(count)])

    def exchange(pieces):
        return [piece if d == 0 else swapped(piece, d) for d, piece in enumerate(pieces)]

    row = shape((depth, spec_all, width_y), f32)
    held = pltpu.VMEM((PARTS, spec, depth * width // PARTS, width_y), f32)
    flat = tracers.reshape(-1, width_y)
    column_at = lax.axis_index("tile") * width + lax.broadcasted_iota(jnp.int32, fluxes.shape, 3)
    closed = jnp.logical_and(column_at == 0, lax.broadcasted_iota(jnp.int32, fluxes.shape, 1) == 0)
    fluxes = jnp.where(closed, 0.0, fluxes)
    sent = shape((count, depth, spec, width_y), bf16)
    piece = shape((depth, spec, width_y), bf16)
    piece_b = shape((depth + 6, spec, width_y), bf16)
    packed_b = call(
        functools.partial(pack_kernel, count, depth, "B"),
        [piece_b] * count,
        (flat, fluxes.reshape(-1, width_y)),
    )
    got_b = exchange(packed_b)
    packed_a = call(functools.partial(pack_kernel, count, depth, "A"), [piece] * count, (flat, packed_b[0]))
    b, send_b, flux, near_a = call(
        functools.partial(unpack_kernel, count, depth, "B"),
        [
            row,
            shape((count, depth + 4, spec, width_y), bf16),
            shape((STEPS, 6, count, depth // count, width_y), f32),
            piece,
        ],
        (*got_b, packed_a[1]),
    )
    halo_b = from_b = lax.ppermute(send_b, AXES, swap_b)
    got_a = [packed_a[0], swapped(near_a, 1), *(swapped(packed_a[d], d) for d in range(2, count))]
    a, send_a = call(
        functools.partial(unpack_kernel, count, depth, "A"),
        [row, shape((count, depth + 1, spec, width_y), bf16)],
        (*got_a, *got_b, send_b),
    )
    halo_a = from_a = lax.ppermute(send_a, AXES, swap_a)
    halo_c = lax.ppermute(send_a, AXES, swap_b)
    common = [
        pltpu.VMEM((7, depth, width_y), f32),
    ]

    def column(t, kind, own, inner, outer, sends=True, after=()):
        scratch = list(common)
        if t < STEPS - 1:
            outs = [sent, row] if sends else [row]
        else:
            outs = [piece] * count
            scratch = [pltpu.VMEM(sent.shape, bf16), *common]
        return call(
            functools.partial(column_kernel, t, kind, GROUP, sends, len(after)),
            outs,
            (own, inner, outer, flux, from_a if kind == "A" else from_b, w_in, w_out, *after),
            cost=A0_COST if kind == "A" and t == 0 else COLUMN_COST,
            scratch=scratch,
        )

    for t in range(0, STEPS, 2):
        send_a, new_a = column(t, "A", a, b, halo_a)
        halo_a = lax.ppermute(send_a, AXES, swap_a)
        (new_b,) = column(t, "B", b, a, halo_b, sends=False, after=(send_a,) if t == 0 else ())
        made_a = column(t + 1, "A", new_a, new_b, halo_a)
        (ghost,) = column(t, "G", halo_b, b, halo_c, sends=False, after=made_a[:1])
        made_b = column(t + 1, "B", new_b, new_a, ghost)
        if t + 1 == STEPS - 1:
            pieces = [*exchange(made_b), *exchange(made_a)]
            break
        (send_b, b), (send_a, a) = made_b, made_a
        halo_b = lax.ppermute(send_b, AXES, swap_b)
        halo_a = lax.ppermute(send_a, AXES, swap_a)
        halo_c = lax.ppermute(send_a, AXES, swap_b)
    out = call(
        functools.partial(finish_kernel, count),
        shape((spec, depth * width, width_y), f32),
        pieces,
        scratch=[held, pltpu.SemaphoreType.DMA((PARTS,))],
        far_out=True,
    )
    return out.reshape(tracers.shape)


def per_device(tracers, fluxes, weight_in, weight_out):
    spec, depth, width, width_y = tracers.shape
    count = lax.axis_size("species")
    fits = (
        width == 2 * count
        and count % 2 == 0
        and STEPS % 2 == 0
        and count & (count - 1) == 0
        and depth % count == 0
        and depth % GROUP == 0
        and depth % PARTS == 0
        and spec == PACK
        and width_y % 128 == 0
        and width % 8 == 0
        and STEPS * (depth // count) == PACK
    )
    chosen = by_columns if fits else by_levels
    return chosen(tracers, fluxes, weight_in, weight_out)


def solution(mesh):
    placed = (P("species", None, "tile", None), P(None, None, "species", "tile", None), P(), P())
    return jax.shard_map(
        per_device,
        mesh=mesh,
        in_specs=placed,
        out_specs=P("species", None, "tile", None),
        check_vma=False,
    )
```

```python
import functools

import jax
import jax.numpy as jnp
from jax import lax
from jax.experimental import pallas as pl
from jax.experimental.pallas import tpu as pltpu
from jax.sharding import PartitionSpec as P

STEPS = 4
AXES = ("species", "tile")
PACK = 16
GROUP = 4
PARTS = 8
COLUMN_COST = 10**10
A0_COST = 1024
VMEM = pl.BlockSpec(memory_space=pltpu.VMEM)
LIMIT = 24 * 1024 * 1024


def positive(value):
    return jnp.maximum(value, 0.0)


def negative(value):
    return jnp.minimum(value, 0.0)


def extended(cells, sides, width):
    for axis, dim in sides:
        count = lax.axis_size(axis)
        ends = count - 1
        head = lax.slice_in_dim(cells, 0, width, axis=dim)
        tail = lax.slice_in_dim(cells, cells.shape[dim] - width, cells.shape[dim], axis=dim)
        cells = jnp.concatenate(
            [
                lax.ppermute(tail, axis, [(i, (i + 1) % count) for i in range(ends)]),
                cells,
                lax.ppermute(head, axis, [((i + 1) % count, i) for i in range(ends)]),
            ],
            axis=dim,
        )
    return cells


def advance(padded_state, padded_x, flux_y, padded_z):
    inner = padded_state[:, 1:-1, 1:-1]
    along_x = padded_state[:, 1:-1]
    face_x = padded_x[:, 1:]
    faces_x = positive(face_x) * along_x[:, :, :-1] + negative(face_x) * along_x[:, :, 1:]
    along_z = padded_state[:, :, 1:-1]
    face_z = padded_z[1:]
    faces_z = positive(face_z) * along_z[:, :-1] + negative(face_z) * along_z[:, 1:]
    faces_y = positive(flux_y) * jnp.roll(inner, 1, 3) + negative(flux_y) * inner
    return (
        inner
        + faces_x[:, :, :-1]
        - faces_x[:, :, 1:]
        + faces_y
        - jnp.roll(faces_y, -1, 3)
        + faces_z[:, :-1]
        - faces_z[:, 1:]
    )


def by_levels(tracers, fluxes, weight_in, weight_out):
    spec_loc, depth_all, width_x, width_y = tracers.shape
    tile_at = lax.axis_index("tile")
    state = lax.all_to_all(tracers, "species", split_axis=1, concat_axis=0, tiled=True)
    spec_all, lev_loc = (state.shape[0], state.shape[1])
    grid_shape = (lev_loc, width_x, width_y)
    column = tile_at * width_x + lax.broadcasted_iota(jnp.int32, grid_shape, 1)
    level_at = lax.axis_index("species") * lev_loc + lax.broadcasted_iota(jnp.int32, grid_shape, 0)
    for interval in range(STEPS):
        own_flux = fluxes[interval]
        flux_x = jnp.where(column == 0, 0.0, own_flux[0])
        flux_y = own_flux[1]
        flux_z = jnp.where(level_at == 0, 0.0, own_flux[2])
        stacked = jnp.concatenate([state, flux_x[None], flux_z[None]], 0)
        padded = extended(stacked, (("species", 1), ("tile", 2)), 1)
        padded_state = padded[:spec_all]
        padded_x = padded[spec_all, 1:-1]
        padded_z = padded[spec_all + 1, :, 1:-1]
        state = advance(padded_state, padded_x, flux_y, padded_z)
        flattened = state.astype(jnp.bfloat16).reshape(spec_all, lev_loc, width_x * width_y)
        hidden = jax.nn.silu(
            jnp.einsum("hs,szc->hzc", weight_in, flattened, preferred_element_type=jnp.float32)
        ).astype(jnp.bfloat16)
        tendency = (
            0.5 * jnp.einsum("sh,hzc->szc", weight_out, hidden, preferred_element_type=jnp.float32)
        ).astype(jnp.bfloat16)
        state = state + tendency.reshape(state.shape).astype(jnp.float32)
    return lax.all_to_all(state, "species", split_axis=0, concat_axis=1, tiled=True)


def place_and_species(count):
    species = lax.axis_index("species")
    return jnp.where(lax.rem(lax.axis_index("tile"), 2) == 1, count - 1 - species, species), species


def columns_of(place):
    odd = lax.rem(place, 2)
    return 2 * place + odd, 2 * place + 1 - odd


def pack_kernel(count, depth, kind, *refs):
    tracers_ref, out_refs = refs[0], refs[-count:]
    width = 2 * count
    spec = tracers_ref.shape[0] // (depth * width)
    lev = depth // count
    own, _ = place_and_species(count)
    columns = [columns_of(own ^ d) for d in range(count)]

    def level(k, carry):
        for d in range(count):
            x = columns[d][0 if kind == "B" else 1]
            cells = tracers_ref[pl.ds(k * width + x, spec, stride=depth * width), :]
            out_refs[d][k] = cells.astype(jnp.bfloat16)
        return carry

    lax.fori_loop(0, depth, level, 0, unroll=2)
    if kind == "A":
        return
    flux_ref = refs[1]
    for d in range(count):
        b_at, a_at = columns[d]
        low = jnp.minimum(b_at, a_at)

        def tile_of(direction, x):
            return jnp.concatenate(
                [
                    flux_ref[pl.ds((t * 3 + direction) * lev * width + x, lev, stride=width), :]
                    for t in range(STEPS)
                ],
                0,
            )

        tiles = ((0, low), (0, low + 1), (1, b_at), (2, b_at), (1, a_at), (2, a_at))
        for i, (direction, x) in enumerate(tiles):
            out_refs[d][depth + i] = tile_of(direction, x).astype(jnp.bfloat16)


def unpack_kernel(count, depth, kind, *refs):
    got, (state_ref, msg_ref) = refs[:count], refs[-2 if kind == "A" else -4 :][:2]
    lev = depth // count
    spec = got[0].shape[1]
    _, species = place_and_species(count)

    if kind == "B":
        flux_ref, near_ref = refs[-2:]
        near_ref[...] = refs[count][...]

    def level(d, k, carry):
        rows = pl.ds(pl.multiple_of((species ^ d) * spec, spec), spec)
        cells = got[d][k]
        state_ref[k, rows] = cells.astype(jnp.float32)
        msg_ref[species ^ d, k] = cells
        return carry

    for d in range(count):
        lax.fori_loop(0, depth, functools.partial(level, d), 0, unroll=4)
        source = species ^ d
        if kind == "A":
            msg_ref[source, depth] = refs[count + d][depth]
            continue
        for i in range(4):
            msg_ref[source, depth + i] = got[d][depth + i]
        for i in range(6):
            part = got[d][depth + i].astype(jnp.float32)
            for t in range(STEPS):
                flux_ref[t, i, source] = part[t * lev : (t + 1) * lev]


def column_kernel(
    t, kind, group, sends, behind, own_ref, inner_ref, outer_ref, flux_ref, from_ref, w_in_ref, w_out_ref, *rest
):
    last = t == STEPS - 1
    coef = rest[-1]
    count, spec, lev = from_ref.shape[0], from_ref.shape[2], flux_ref.shape[3]
    depth, spec_all, width_y = inner_ref.shape
    place, species = place_and_species(count)
    rest = list(rest)[behind:]
    outs = rest[:count] if last else None
    send_ref = rest[count] if outs else rest.pop(0) if sends else None
    new_ref = None if last else rest.pop(0)
    old_ref = rest.pop(0) if kind == "A" and t == 0 else None

    def cells_of(ref, k):
        if ref.shape == inner_ref.shape:
            return ref[k]
        return jnp.concatenate([ref[s, k].astype(jnp.float32) for s in range(count)], 0)

    def mine(index):
        return jnp.concatenate([flux_ref[t, index, s] for s in range(count)], 0)

    def theirs(index):
        parts = [from_ref[s, depth + index].astype(jnp.float32) for s in range(count)]
        return jnp.concatenate([p[t * lev : (t + 1) * lev] for p in parts], 0)

    even = lax.rem(place, 2) == 0
    if kind == "A":
        outer_high = even
        fx = jnp.where(even, mine(1), mine(0))
        fx_hi = jnp.where(even, theirs(0), mine(1))
        fy, fz = mine(4), mine(5)
    elif kind == "B":
        outer_high = jnp.logical_not(even)
        fx = jnp.where(even, mine(0), mine(1))
        fx_hi = jnp.where(even, mine(1), theirs(0))
        fy, fz = mine(2), mine(3)
    else:
        outer_high = jnp.logical_not(even)
        fx = jnp.where(even, theirs(1), theirs(0))
        fx_hi = jnp.where(even, mine(0), theirs(1))
        fy, fz = theirs(2), theirs(3)
    fy_hi = pltpu.roll(fy, width_y - 1, 1)
    fz = jnp.where(lax.broadcasted_iota(jnp.int32, fz.shape, 0) == 0, 0.0, fz)
    fz_hi = jnp.concatenate([fz[1:], jnp.zeros_like(fz[:1])], 0)
    low, high = positive(fx), -negative(fx_hi)
    coef[0] = (
        1.0
        + (negative(fx) - positive(fx_hi))
        + (negative(fy) - positive(fy_hi))
        + (negative(fz) - positive(fz_hi))
    )
    coef[1] = jnp.where(outer_high, high, low)
    coef[2] = jnp.where(outer_high, low, high)
    coef[3] = positive(fy)
    coef[4] = -negative(fy_hi)
    coef[5] = positive(fz)
    coef[6] = -negative(fz_hi)
    w_in = w_in_ref[...]
    w_out = w_out_ref[...]

    def level(k):
        own = cells_of(own_ref, k)
        if old_ref is not None:
            for s in range(count):
                old_ref[s, k] = own[s * spec : (s + 1) * spec].astype(jnp.bfloat16)
        out = coef[0, pl.ds(k, 1)] * own
        out += coef[1, pl.ds(k, 1)] * cells_of(outer_ref, k)
        out += coef[2, pl.ds(k, 1)] * inner_ref[k]
        out += coef[3, pl.ds(k, 1)] * pltpu.roll(own, 1, 1)
        out += coef[4, pl.ds(k, 1)] * pltpu.roll(own, width_y - 1, 1)
        out += coef[5, pl.ds(k, 1)] * cells_of(own_ref, max(k - 1, 0))
        out += coef[6, pl.ds(k, 1)] * cells_of(own_ref, min(k + 1, depth - 1))
        return out, out.astype(jnp.bfloat16)

    hid = w_in.shape[0]
    split = hid // 2
    wide = 2 * width_y
    pieces = [(i, j) for j in range(group // 2) for i in range(2)]

    def first_matmul(i, cells):
        return jnp.dot(w_in[i * split : (i + 1) * split], cells, preferred_element_type=jnp.float32)

    def columns(k0):
        levels = [level(k0 + i) for i in range(group)]
        moved = [m for m, _ in levels]
        cells = [jnp.concatenate([levels[j][1], levels[j + 1][1]], 1) for j in range(0, group, 2)]
        return moved, cells

    moved, cells = columns(0)
    halves = [first_matmul(i, cells[j]) for i, j in pieces]
    for k0 in range(0, depth, group):
        more = k0 + group < depth
        if more:
            next_moved, cells = columns(k0 + group)
        next_halves = []
        for p, (i, j) in enumerate(pieces):
            if more:
                next_halves.append(first_matmul(i, cells[j]))
            half = halves[p]
            half = half.astype(jnp.bfloat16)
            hidden = half + half * jnp.tanh(half)
            part = jnp.dot(w_out[:, i * split : (i + 1) * split], hidden, preferred_element_type=jnp.float32)
            change = part if i == 0 else change + part
            if i == 0:
                continue
            for n in range(2):
                k = k0 + 2 * j + n
                new = moved[2 * j + n] + change[:, n * width_y : (n + 1) * width_y]
                if new_ref is not None:
                    new_ref[k] = new
                if send_ref is not None:
                    for s in range(count):
                        send_ref[s, k] = new[s * spec : (s + 1) * spec].astype(jnp.bfloat16)
        halves = next_halves
        if more:
            moved = next_moved
    if outs is not None:
        for d in range(count):
            outs[d][...] = send_ref[species ^ d]


def finish_kernel(count, *refs):
    pieces, (out_ref, held, sems) = refs[: 2 * count], refs[2 * count :]
    parts, spec, rows, width_y = held.shape
    width = 2 * count
    lev = rows // width
    own, _ = place_and_species(count)
    columns = [columns_of(own ^ d) for d in range(count)]
    copies = []
    for part in range(parts):
        flat = held.at[part].reshape(spec * rows, width_y)

        def level(k, carry):
            for d in range(count):
                for side, x in enumerate(columns[d]):
                    cells = pieces[side * count + d][part * lev + k].astype(jnp.float32)
                    flat[pl.ds(k * width + x, spec, stride=rows), :] = cells
            return carry

        lax.fori_loop(0, lev, level, 0)
        target = out_ref.at[:, pl.ds(part * rows, rows), :]
        copies.append(pltpu.make_async_copy(held.at[part], target, sems.at[part]))
        copies[-1].start()
    for copy in copies:
        copy.wait()


def call(kernel, out_shape, args, scratch=(), far_out=False, cost=COLUMN_COST):
    many = isinstance(out_shape, (list, tuple))
    anywhere = pl.BlockSpec(memory_space=pl.ANY)
    return pl.pallas_call(
        kernel,
        out_shape=out_shape,
        in_specs=[VMEM] * len(args),
        out_specs=[VMEM] * len(out_shape) if many else anywhere if far_out else VMEM,
        scratch_shapes=scratch,
        compiler_params=pltpu.CompilerParams(vmem_limit_bytes=LIMIT),
        cost_estimate=pl.CostEstimate(flops=cost, bytes_accessed=cost // 10**4, transcendentals=0),
    )(*args)


def by_columns(tracers, fluxes, weight_in, weight_out):
    spec, depth, width, width_y = tracers.shape
    count, tiles = lax.axis_size("species"), lax.axis_size("tile")
    spec_all = spec * count
    f32, bf16 = jnp.float32, jnp.bfloat16
    shape = jax.ShapeDtypeStruct

    chain = []
    for t in range(tiles):
        for place in range(count):
            s = place if t % 2 == 0 else count - 1 - place
            chain.append(s * tiles + t)
    swap_a, swap_b = [], []
    for i in range(len(chain) - 1):
        (swap_a if i % 2 == 0 else swap_b).extend(
            [(chain[i], chain[i + 1]), (chain[i + 1], chain[i])]
        )

    w_in = weight_in * jnp.asarray(0.5, bf16)
    w_out = weight_out * jnp.asarray(0.5, bf16)

    def swapped(piece, d):
        return lax.ppermute(piece, "species", [(s, s ^ d) for s in range(count)])

    def exchange(pieces):
        return [piece if d == 0 else swapped(piece, d) for d, piece in enumerate(pieces)]

    row = shape((depth, spec_all, width_y), f32)
    held = pltpu.VMEM((PARTS, spec, depth * width // PARTS, width_y), f32)
    flat = tracers.reshape(-1, width_y)
    column_at = lax.axis_index("tile") * width + lax.broadcasted_iota(jnp.int32, fluxes.shape, 3)
    closed = jnp.logical_and(column_at == 0, lax.broadcasted_iota(jnp.int32, fluxes.shape, 1) == 0)
    fluxes = jnp.where(closed, 0.0, fluxes)
    sent = shape((count, depth, spec, width_y), bf16)
    piece = shape((depth, spec, width_y), bf16)
    piece_b = shape((depth + 6, spec, width_y), bf16)
    packed_b = call(
        functools.partial(pack_kernel, count, depth, "B"),
        [piece_b] * count,
        (flat, fluxes.reshape(-1, width_y)),
    )
    got_b = exchange(packed_b)
    packed_a = call(functools.partial(pack_kernel, count, depth, "A"), [piece] * count, (flat, packed_b[0]))
    b, send_b, flux, near_a = call(
        functools.partial(unpack_kernel, count, depth, "B"),
        [
            row,
            shape((count, depth + 4, spec, width_y), bf16),
            shape((STEPS, 6, count, depth // count, width_y), f32),
            piece,
        ],
        (*got_b, packed_a[1]),
    )
    halo_b = from_b = lax.ppermute(send_b, AXES, swap_b)
    got_a = [packed_a[0], swapped(near_a, 1), *(swapped(packed_a[d], d) for d in range(2, count))]
    a, send_a = call(
        functools.partial(unpack_kernel, count, depth, "A"),
        [row, shape((count, depth + 1, spec, width_y), bf16)],
        (*got_a, *got_b, send_b),
    )
    halo_a = from_a = lax.ppermute(send_a, AXES, swap_a)
    common = [
        pltpu.VMEM((7, depth, width_y), f32),
    ]

    def column(t, kind, own, inner, outer, sends=True, after=()):
        scratch = list(common)
        if t < STEPS - 1:
            outs = ([sent, row] if sends else [row]) + ([sent] if kind == "A" and t == 0 else [])
        else:
            outs = [piece] * count
            scratch = [pltpu.VMEM(sent.shape, bf16), *common]
        return call(
            functools.partial(column_kernel, t, kind, GROUP, sends, len(after)),
            outs,
            (own, inner, outer, flux, from_a if kind == "A" else from_b, w_in, w_out, *after),
            cost=A0_COST if kind == "A" and t == 0 else COLUMN_COST,
            scratch=scratch,
        )

    for t in range(0, STEPS, 2):
        send_a, new_a, *old_a = column(t, "A", a, b, halo_a)
        halo_a = lax.ppermute(send_a, AXES, swap_a)
        if t == 0:
            halo_c = lax.ppermute(old_a[0], AXES, swap_b)
        (new_b,) = column(t, "B", b, a, halo_b, sends=False, after=(send_a,) if t == 0 else ())
        made_a = column(t + 1, "A", new_a, new_b, halo_a)
        (ghost,) = column(t, "G", halo_b, b, halo_c, sends=False, after=made_a[:1])
        made_b = column(t + 1, "B", new_b, new_a, ghost)
        if t + 1 == STEPS - 1:
            pieces = [*exchange(made_b), *exchange(made_a)]
            break
        (send_b, b), (send_a, a) = made_b, made_a
        halo_b = lax.ppermute(send_b, AXES, swap_b)
        halo_a = lax.ppermute(send_a, AXES, swap_a)
        halo_c = lax.ppermute(send_a, AXES, swap_b)
    out = call(
        functools.partial(finish_kernel, count),
        shape((spec, depth * width, width_y), f32),
        pieces,
        scratch=[held, pltpu.SemaphoreType.DMA((PARTS,))],
        far_out=True,
    )
    return out.reshape(tracers.shape)


def per_device(tracers, fluxes, weight_in, weight_out):
    spec, depth, width, width_y = tracers.shape
    count = lax.axis_size("species")
    fits = (
        width == 2 * count
        and count % 2 == 0
        and STEPS % 2 == 0
        and count & (count - 1) == 0
        and depth % count == 0
        and depth % GROUP == 0
        and depth % PARTS == 0
        and spec == PACK
        and width_y % 128 == 0
        and width % 8 == 0
        and STEPS * (depth // count) == PACK
    )
    chosen = by_columns if fits else by_levels
    return chosen(tracers, fluxes, weight_in, weight_out)


def solution(mesh):
    placed = (P("species", None, "tile", None), P(None, None, "species", "tile", None), P(), P())
    return jax.shard_map(
        per_device,
        mesh=mesh,
        in_specs=placed,
        out_specs=P("species", None, "tile", None),
        check_vma=False,
    )
```

```python
import functools

import jax
import jax.numpy as jnp
from jax import lax
from jax.experimental import pallas as pl
from jax.experimental.pallas import tpu as pltpu
from jax.sharding import PartitionSpec as P

STEPS = 4
AXES = ("species", "tile")
PACK = 16
GROUP = 4
PARTS = 8
COLUMN_COST = 10**10
A0_COST = 1024
VMEM = pl.BlockSpec(memory_space=pltpu.VMEM)
LIMIT = 24 * 1024 * 1024


def positive(value):
    return jnp.maximum(value, 0.0)


def negative(value):
    return jnp.minimum(value, 0.0)


def extended(cells, sides, width):
    for axis, dim in sides:
        count = lax.axis_size(axis)
        ends = count - 1
        head = lax.slice_in_dim(cells, 0, width, axis=dim)
        tail = lax.slice_in_dim(cells, cells.shape[dim] - width, cells.shape[dim], axis=dim)
        cells = jnp.concatenate(
            [
                lax.ppermute(tail, axis, [(i, (i + 1) % count) for i in range(ends)]),
                cells,
                lax.ppermute(head, axis, [((i + 1) % count, i) for i in range(ends)]),
            ],
            axis=dim,
        )
    return cells


def advance(padded_state, padded_x, flux_y, padded_z):
    inner = padded_state[:, 1:-1, 1:-1]
    along_x = padded_state[:, 1:-1]
    face_x = padded_x[:, 1:]
    faces_x = positive(face_x) * along_x[:, :, :-1] + negative(face_x) * along_x[:, :, 1:]
    along_z = padded_state[:, :, 1:-1]
    face_z = padded_z[1:]
    faces_z = positive(face_z) * along_z[:, :-1] + negative(face_z) * along_z[:, 1:]
    faces_y = positive(flux_y) * jnp.roll(inner, 1, 3) + negative(flux_y) * inner
    return (
        inner
        + faces_x[:, :, :-1]
        - faces_x[:, :, 1:]
        + faces_y
        - jnp.roll(faces_y, -1, 3)
        + faces_z[:, :-1]
        - faces_z[:, 1:]
    )


def by_levels(tracers, fluxes, weight_in, weight_out):
    spec_loc, depth_all, width_x, width_y = tracers.shape
    tile_at = lax.axis_index("tile")
    state = lax.all_to_all(tracers, "species", split_axis=1, concat_axis=0, tiled=True)
    spec_all, lev_loc = (state.shape[0], state.shape[1])
    grid_shape = (lev_loc, width_x, width_y)
    column = tile_at * width_x + lax.broadcasted_iota(jnp.int32, grid_shape, 1)
    level_at = lax.axis_index("species") * lev_loc + lax.broadcasted_iota(jnp.int32, grid_shape, 0)
    for interval in range(STEPS):
        own_flux = fluxes[interval]
        flux_x = jnp.where(column == 0, 0.0, own_flux[0])
        flux_y = own_flux[1]
        flux_z = jnp.where(level_at == 0, 0.0, own_flux[2])
        stacked = jnp.concatenate([state, flux_x[None], flux_z[None]], 0)
        padded = extended(stacked, (("species", 1), ("tile", 2)), 1)
        padded_state = padded[:spec_all]
        padded_x = padded[spec_all, 1:-1]
        padded_z = padded[spec_all + 1, :, 1:-1]
        state = advance(padded_state, padded_x, flux_y, padded_z)
        flattened = state.astype(jnp.bfloat16).reshape(spec_all, lev_loc, width_x * width_y)
        hidden = jax.nn.silu(
            jnp.einsum("hs,szc->hzc", weight_in, flattened, preferred_element_type=jnp.float32)
        ).astype(jnp.bfloat16)
        tendency = (
            0.5 * jnp.einsum("sh,hzc->szc", weight_out, hidden, preferred_element_type=jnp.float32)
        ).astype(jnp.bfloat16)
        state = state + tendency.reshape(state.shape).astype(jnp.float32)
    return lax.all_to_all(state, "species", split_axis=0, concat_axis=1, tiled=True)


def place_and_species(count):
    species = lax.axis_index("species")
    return jnp.where(lax.rem(lax.axis_index("tile"), 2) == 1, count - 1 - species, species), species


def columns_of(place):
    odd = lax.rem(place, 2)
    return 2 * place + odd, 2 * place + 1 - odd


def pack_kernel(count, depth, kind, *refs):
    tracers_ref, out_refs = refs[0], refs[-count:]
    width = 2 * count
    spec = tracers_ref.shape[0] // (depth * width)
    lev = depth // count
    own, _ = place_and_species(count)
    columns = [columns_of(own ^ d) for d in range(count)]

    def level(k, carry):
        for d in range(count):
            x = columns[d][0 if kind == "B" else 1]
            cells = tracers_ref[pl.ds(k * width + x, spec, stride=depth * width), :]
            out_refs[d][k] = cells.astype(jnp.bfloat16)
        return carry

    lax.fori_loop(0, depth, level, 0, unroll=2)
    if kind == "A":
        return
    flux_ref = refs[1]
    for d in range(count):
        b_at, a_at = columns[d]
        low = jnp.minimum(b_at, a_at)

        def tile_of(direction, x):
            return jnp.concatenate(
                [
                    flux_ref[pl.ds((t * 3 + direction) * lev * width + x, lev, stride=width), :]
                    for t in range(STEPS)
                ],
                0,
            )

        tiles = ((0, low), (0, low + 1), (1, b_at), (2, b_at), (1, a_at), (2, a_at))
        for i, (direction, x) in enumerate(tiles):
            out_refs[d][depth + i] = tile_of(direction, x).astype(jnp.bfloat16)


def unpack_kernel(count, depth, kind, *refs):
    got, (state_ref, msg_ref) = refs[:count], refs[-2 if kind == "A" else -4 :][:2]
    lev = depth // count
    spec = got[0].shape[1]
    _, species = place_and_species(count)

    if kind == "B":
        flux_ref, near_ref = refs[-2:]
        near_ref[...] = refs[count][...]

    def level(d, k, carry):
        rows = pl.ds(pl.multiple_of((species ^ d) * spec, spec), spec)
        cells = got[d][k]
        state_ref[k, rows] = cells.astype(jnp.float32)
        msg_ref[species ^ d, k] = cells
        return carry

    for d in range(count):
        lax.fori_loop(0, depth, functools.partial(level, d), 0, unroll=4)
        source = species ^ d
        if kind == "A":
            msg_ref[source, depth] = refs[count + d][depth]
            continue
        for i in range(4):
            msg_ref[source, depth + i] = got[d][depth + i]
        for i in range(6):
            part = got[d][depth + i].astype(jnp.float32)
            for t in range(STEPS):
                flux_ref[t, i, source] = part[t * lev : (t + 1) * lev]


def column_kernel(
    t, kind, group, sends, behind, own_ref, inner_ref, outer_ref, flux_ref, from_ref, w_in_ref, w_out_ref, *rest
):
    last = t == STEPS - 1
    coef = rest[-1]
    count, spec, lev = from_ref.shape[0], from_ref.shape[2], flux_ref.shape[3]
    depth, spec_all, width_y = inner_ref.shape
    place, species = place_and_species(count)
    rest = list(rest)[behind:]
    outs = rest[:count] if last else None
    send_ref = rest[count] if outs else rest.pop(0) if sends else None
    new_ref = None if last else rest.pop(0)

    def cells_of(ref, k):
        if ref.shape == inner_ref.shape:
            return ref[k]
        return jnp.concatenate([ref[s, k].astype(jnp.float32) for s in range(count)], 0)

    def mine(index):
        return jnp.concatenate([flux_ref[t, index, s] for s in range(count)], 0)

    def theirs(index):
        parts = [from_ref[s, depth + index].astype(jnp.float32) for s in range(count)]
        return jnp.concatenate([p[t * lev : (t + 1) * lev] for p in parts], 0)

    even = lax.rem(place, 2) == 0
    if kind == "A":
        outer_high = even
        fx = jnp.where(even, mine(1), mine(0))
        fx_hi = jnp.where(even, theirs(0), mine(1))
        fy, fz = mine(4), mine(5)
    elif kind == "B":
        outer_high = jnp.logical_not(even)
        fx = jnp.where(even, mine(0), mine(1))
        fx_hi = jnp.where(even, mine(1), theirs(0))
        fy, fz = mine(2), mine(3)
    else:
        outer_high = jnp.logical_not(even)
        fx = jnp.where(even, theirs(1), theirs(0))
        fx_hi = jnp.where(even, mine(0), theirs(1))
        fy, fz = theirs(2), theirs(3)
    fy_hi = pltpu.roll(fy, width_y - 1, 1)
    fz = jnp.where(lax.broadcasted_iota(jnp.int32, fz.shape, 0) == 0, 0.0, fz)
    fz_hi = jnp.concatenate([fz[1:], jnp.zeros_like(fz[:1])], 0)
    low, high = positive(fx), -negative(fx_hi)
    coef[0] = (
        1.0
        + (negative(fx) - positive(fx_hi))
        + (negative(fy) - positive(fy_hi))
        + (negative(fz) - positive(fz_hi))
    )
    coef[1] = jnp.where(outer_high, high, low)
    coef[2] = jnp.where(outer_high, low, high)
    coef[3] = positive(fy)
    coef[4] = -negative(fy_hi)
    coef[5] = positive(fz)
    coef[6] = -negative(fz_hi)
    w_in = w_in_ref[...]
    w_out = w_out_ref[...]

    def level(k):
        own = cells_of(own_ref, k)
        out = coef[0, pl.ds(k, 1)] * own
        out += coef[1, pl.ds(k, 1)] * cells_of(outer_ref, k)
        out += coef[2, pl.ds(k, 1)] * inner_ref[k]
        out += coef[3, pl.ds(k, 1)] * pltpu.roll(own, 1, 1)
        out += coef[4, pl.ds(k, 1)] * pltpu.roll(own, width_y - 1, 1)
        out += coef[5, pl.ds(k, 1)] * cells_of(own_ref, max(k - 1, 0))
        out += coef[6, pl.ds(k, 1)] * cells_of(own_ref, min(k + 1, depth - 1))
        return out, out.astype(jnp.bfloat16)

    hid = w_in.shape[0]
    split = hid // 2
    wide = 2 * width_y
    pieces = [(i, j) for j in range(group // 2) for i in range(2)]

    def first_matmul(i, cells):
        return jnp.dot(w_in[i * split : (i + 1) * split], cells, preferred_element_type=jnp.float32)

    def columns(k0):
        levels = [level(k0 + i) for i in range(group)]
        moved = [m for m, _ in levels]
        cells = [jnp.concatenate([levels[j][1], levels[j + 1][1]], 1) for j in range(0, group, 2)]
        return moved, cells

    moved, cells = columns(0)
    halves = [first_matmul(i, cells[j]) for i, j in pieces]
    for k0 in range(0, depth, group):
        more = k0 + group < depth
        if more:
            next_moved, cells = columns(k0 + group)
        next_halves = []
        for p, (i, j) in enumerate(pieces):
            if more:
                next_halves.append(first_matmul(i, cells[j]))
            half = halves[p]
            hidden = (half + half * jnp.tanh(half)).astype(jnp.bfloat16)
            part = jnp.dot(w_out[:, i * split : (i + 1) * split], hidden, preferred_element_type=jnp.float32)
            change = part if i == 0 else change + part
            if i == 0:
                continue
            for n in range(2):
                k = k0 + 2 * j + n
                new = moved[2 * j + n] + change[:, n * width_y : (n + 1) * width_y]
                if new_ref is not None:
                    new_ref[k] = new
                if send_ref is not None:
                    for s in range(count):
                        send_ref[s, k] = new[s * spec : (s + 1) * spec].astype(jnp.bfloat16)
        halves = next_halves
        if more:
            moved = next_moved
    if outs is not None:
        for d in range(count):
            outs[d][...] = send_ref[species ^ d]


def finish_kernel(count, *refs):
    pieces, (out_ref, held, sems) = refs[: 2 * count], refs[2 * count :]
    parts, spec, rows, width_y = held.shape
    width = 2 * count
    lev = rows // width
    own, _ = place_and_species(count)
    columns = [columns_of(own ^ d) for d in range(count)]
    copies = []
    for part in range(parts):
        flat = held.at[part].reshape(spec * rows, width_y)

        def level(k, carry):
            for d in range(count):
                for side, x in enumerate(columns[d]):
                    cells = pieces[side * count + d][part * lev + k].astype(jnp.float32)
                    flat[pl.ds(k * width + x, spec, stride=rows), :] = cells
            return carry

        lax.fori_loop(0, lev, level, 0)
        target = out_ref.at[:, pl.ds(part * rows, rows), :]
        copies.append(pltpu.make_async_copy(held.at[part], target, sems.at[part]))
        copies[-1].start()
    for copy in copies:
        copy.wait()


def call(kernel, out_shape, args, scratch=(), far_out=False, cost=COLUMN_COST):
    many = isinstance(out_shape, (list, tuple))
    anywhere = pl.BlockSpec(memory_space=pl.ANY)
    return pl.pallas_call(
        kernel,
        out_shape=out_shape,
        in_specs=[VMEM] * len(args),
        out_specs=[VMEM] * len(out_shape) if many else anywhere if far_out else VMEM,
        scratch_shapes=scratch,
        compiler_params=pltpu.CompilerParams(vmem_limit_bytes=LIMIT),
        cost_estimate=pl.CostEstimate(flops=cost, bytes_accessed=cost // 10**4, transcendentals=0),
    )(*args)


def by_columns(tracers, fluxes, weight_in, weight_out):
    spec, depth, width, width_y = tracers.shape
    count, tiles = lax.axis_size("species"), lax.axis_size("tile")
    spec_all = spec * count
    f32, bf16 = jnp.float32, jnp.bfloat16
    shape = jax.ShapeDtypeStruct

    chain = []
    for t in range(tiles):
        for place in range(count):
            s = place if t % 2 == 0 else count - 1 - place
            chain.append(s * tiles + t)
    swap_a, swap_b = [], []
    for i in range(len(chain) - 1):
        (swap_a if i % 2 == 0 else swap_b).extend(
            [(chain[i], chain[i + 1]), (chain[i + 1], chain[i])]
        )

    w_in = weight_in * jnp.asarray(0.5, bf16)
    w_out = weight_out * jnp.asarray(0.5, bf16)

    def swapped(piece, d):
        return lax.ppermute(piece, "species", [(s, s ^ d) for s in range(count)])

    def exchange(pieces):
        return [piece if d == 0 else swapped(piece, d) for d, piece in enumerate(pieces)]

    row = shape((depth, spec_all, width_y), f32)
    held = pltpu.VMEM((PARTS, spec, depth * width // PARTS, width_y), f32)
    flat = tracers.reshape(-1, width_y)
    column_at = lax.axis_index("tile") * width + lax.broadcasted_iota(jnp.int32, fluxes.shape, 3)
    closed = jnp.logical_and(column_at == 0, lax.broadcasted_iota(jnp.int32, fluxes.shape, 1) == 0)
    fluxes = jnp.where(closed, 0.0, fluxes)
    sent = shape((count, depth, spec, width_y), bf16)
    piece = shape((depth, spec, width_y), bf16)
    piece_b = shape((depth + 6, spec, width_y), bf16)
    packed_b = call(
        functools.partial(pack_kernel, count, depth, "B"),
        [piece_b] * count,
        (flat, fluxes.reshape(-1, width_y)),
    )
    got_b = exchange(packed_b)
    packed_a = call(functools.partial(pack_kernel, count, depth, "A"), [piece] * count, (flat, packed_b[0]))
    b, send_b, flux, near_a = call(
        functools.partial(unpack_kernel, count, depth, "B"),
        [
            row,
            shape((count, depth + 4, spec, width_y), bf16),
            shape((STEPS, 6, count, depth // count, width_y), f32),
            piece,
        ],
        (*got_b, packed_a[1], w_in, w_out),
    )
    halo_b = from_b = lax.ppermute(send_b, AXES, swap_b)
    got_a = [packed_a[0], swapped(near_a, 1), *(swapped(packed_a[d], d) for d in range(2, count))]
    a, send_a = call(
        functools.partial(unpack_kernel, count, depth, "A"),
        [row, shape((count, depth + 1, spec, width_y), bf16)],
        (*got_a, *got_b, send_b),
    )
    halo_a = from_a = lax.ppermute(send_a, AXES, swap_a)
    halo_c = lax.ppermute(send_a, AXES, swap_b)
    common = [
        pltpu.VMEM((7, depth, width_y), f32),
    ]

    def column(t, kind, own, inner, outer, sends=True, after=()):
        scratch = list(common)
        if t < STEPS - 1:
            outs = [sent, row] if sends else [row]
        else:
            outs = [piece] * count
            scratch = [pltpu.VMEM(sent.shape, bf16), *common]
        return call(
            functools.partial(column_kernel, t, kind, GROUP, sends, len(after)),
            outs,
            (own, inner, outer, flux, from_a if kind == "A" else from_b, w_in, w_out, *after),
            cost=A0_COST if kind == "A" and t == 0 else COLUMN_COST,
            scratch=scratch,
        )

    for t in range(0, STEPS, 2):
        send_a, new_a = column(t, "A", a, b, halo_a)
        halo_a = lax.ppermute(send_a, AXES, swap_a)
        (new_b,) = column(t, "B", b, a, halo_b, sends=False, after=(send_a,) if t == 0 else ())
        made_a = column(t + 1, "A", new_a, new_b, halo_a)
        (ghost,) = column(t, "G", halo_b, b, halo_c, sends=False, after=made_a[:1])
        made_b = column(t + 1, "B", new_b, new_a, ghost)
        if t + 1 == STEPS - 1:
            pieces = [*exchange(made_b), *exchange(made_a)]
            break
        (send_b, b), (send_a, a) = made_b, made_a
        halo_b = lax.ppermute(send_b, AXES, swap_b)
        halo_a = lax.ppermute(send_a, AXES, swap_a)
        halo_c = lax.ppermute(send_a, AXES, swap_b)
    out = call(
        functools.partial(finish_kernel, count),
        shape((spec, depth * width, width_y), f32),
        pieces,
        scratch=[held, pltpu.SemaphoreType.DMA((PARTS,))],
        far_out=True,
    )
    return out.reshape(tracers.shape)


def per_device(tracers, fluxes, weight_in, weight_out):
    spec, depth, width, width_y = tracers.shape
    count = lax.axis_size("species")
    fits = (
        width == 2 * count
        and count % 2 == 0
        and STEPS % 2 == 0
        and count & (count - 1) == 0
        and depth % count == 0
        and depth % GROUP == 0
        and depth % PARTS == 0
        and spec == PACK
        and width_y % 128 == 0
        and width % 8 == 0
        and STEPS * (depth // count) == PACK
    )
    chosen = by_columns if fits else by_levels
    return chosen(tracers, fluxes, weight_in, weight_out)


def solution(mesh):
    placed = (P("species", None, "tile", None), P(None, None, "species", "tile", None), P(), P())
    return jax.shard_map(
        per_device,
        mesh=mesh,
        in_specs=placed,
        out_specs=P("species", None, "tile", None),
        check_vma=False,
    )
```
